256 devices in a mesh: view: 8 (over z), patch: 32 (over x, y, core).
Axes of the slice: x: 4, y: 4, z: 8, core: 2. Of those that a mesh axis runs over, the one named last changes fastest.
Arguments:
- coefficients: bfloat16 [8, 2304, 128, 512], P('view', 'patch'), may hold values from -0.25 to 0.25
- sky_year: bfloat16 [2304, 8760], P('patch'), may hold values from 0.19921875 to 5
- hour_list: int32 [96], replicated, may hold values from 0 to 8759
- retention: float32 [128, 512], P('patch'), may hold values from 0 to 1
Outputs:
- acuity: float32 [128, 8, 96, 512], P('patch', 'view')
- veil: float32 [128, 8, 96, 512], P('patch', 'view')
The draws below stay inside these ranges and needn't reach their ends.
All inputs are finite; a program needn't handle non-finite values.
Results may differ from the reference program's by a relative error of at most 0.0003.
Values may be sent and summed in bfloat16 or wider, within the bound.
No kernel may reach another device: no remote copies, remote signals or barrier semaphores. Data moves between devices by JAX's collectives and lax.ppermute only.
A program may use at most 128 MiB of HBM per device.

```python
import math
import jax
import jax.numpy as jnp
from jax import lax

VIEWS = 8
PATCHES = 2304
COLS = 512
HOURS = 96
YEAR = 8760
STRIP_LINE_COUNT = 128


def draw_retention(key, part):
    key_rate, key_rough, marker_image_lines, key_depth = jax.random.split(key, 4)
    spread = jax.random.uniform(key_rate, (COLS,), jnp.float32, math.log(0.3), math.log(40.0))
    strength = jnp.exp(spread)
    roughness = jax.random.uniform(key_rough, (STRIP_LINE_COUNT, COLS), jnp.float32, 0.5, 1.5)
    dazzle_spike_lines = jax.random.randint(marker_image_lines, (3,), 0, STRIP_LINE_COUNT)
    sample_locations = jnp.arange(STRIP_LINE_COUNT, dtype=jnp.int32)
    lit_sample_spots = jnp.any(sample_locations[:, None] == dazzle_spike_lines[None, :], axis=1)
    depths = jax.random.uniform(key_depth, (STRIP_LINE_COUNT, COLS), jnp.float32, 0.5, 0.8)
    factor = jnp.where(lit_sample_spots[:, None], depths, jnp.float32(1.0))
    return jnp.exp(-strength[None, :] * roughness / STRIP_LINE_COUNT) * factor


def place_ends(array, stream_key, low, top_value):
    shape = array.shape
    index_at = [jax.random.randint(jax.random.fold_in(stream_key, axis), (), 0, shape[axis]) for axis in range(len(shape))]
    array = array.at[tuple(index_at)].set(low)
    longest = shape.index(max(shape))
    index_at[longest] = (index_at[longest] + 1) % shape[longest]
    return array.at[tuple(index_at)].set(top_value)


def with_spikes(drawn, own_key, source, target, shards_of, factor):
    owner, partner = [(jnp.arange(drawn.shape[axis_at]) // (drawn.shape[axis_at] // shards_of)).reshape([-1 if axis == axis_at else 1 for axis in range(drawn.ndim)]) for axis_at in (source, target)]
    chosen = jax.random.permutation(own_key, shards_of)[partner]
    strong = (owner == chosen) | (owner == (partner + shards_of // 2) % shards_of)
    return jnp.where(strong, factor * drawn, drawn)


def levels(own_key, shape, cuts, smallest, high):
    level, own = 1.0, jax.random.fold_in(own_key, 6)
    for dim, parts in cuts:
        draws = jnp.exp(jax.random.uniform(jax.random.fold_in(own, dim), (parts,), jnp.float32, smallest / len(cuts), high / len(cuts)))
        level = level * jnp.repeat(draws, shape[dim] // parts).reshape([-1 if axis == dim else 1 for axis in range(len(shape))])
    return level


def heavy_noise(key, extent, scale, limit, cuts, heavy, held_as=jnp.bfloat16):
    values = scale * jax.random.normal(key, extent, jnp.float32)
    if cuts:
        values = values * levels(key, extent, cuts, -0.22, 0.18)
    return jnp.clip(with_spikes(values, jax.random.fold_in(key, 3), *heavy), -limit, limit).astype(held_as)


def setup_inputs(seed: int = 0) -> dict:
    arg_keys = jax.random.split(jax.random.key(seed), 5)
    coefficients = heavy_noise(arg_keys[0], (VIEWS, PATCHES, STRIP_LINE_COUNT, COLS), PATCHES ** -0.5, 0.25, ((0, 8), (1, 32)), (1, 2, 32, 2.75))
    sky_year = jnp.clip(jnp.exp(math.log(5.0) - 3.2227897 * jax.random.uniform(arg_keys[1], (PATCHES, YEAR), jnp.float32) ** levels(arg_keys[1], (PATCHES, YEAR), ((0, 32),), -0.2, 0.2)), 0.19921875, 5.0).astype(jnp.bfloat16)
    hour_list = place_ends(jax.random.randint(arg_keys[2], (HOURS,), 0, YEAR), jax.random.fold_in(arg_keys[2], 1), 0, YEAR - 1).astype(jnp.int32)
    retention = draw_retention(jax.random.fold_in(arg_keys[4], 71), 0)
    return {"coefficients": coefficients, "sky_year": sky_year, "hour_list": hour_list, "retention": retention}


binomial_taps = (0.0625, 0.25, 0.375, 0.25, 0.0625)


def pascal_kernel(field, device_axis_name):
    size = field.shape[device_axis_name]
    widths = [(0, 0)] * field.ndim
    widths[device_axis_name] = (2, 2)
    padded = jnp.pad(field, widths)
    total = jnp.zeros_like(field)
    for offset in range(5):
        total = total + binomial_taps[offset] * lax.slice_in_dim(padded, offset, offset + size, axis=device_axis_name)
    return total


def reference(coefficients, sky_year, hour_list, retention):
    sky = jnp.take(sky_year, hour_list, axis=1)
    sky_rows = sky.T

    def render(single_view):
        flat = single_view.reshape(single_view.shape[0], -1)
        return jnp.dot(sky_rows, flat, preferred_element_type=jnp.float32).reshape(sky_rows.shape[0], single_view.shape[1], single_view.shape[2])

    images = lax.map(render, coefficients)
    luminance = jnp.transpose(images, (2, 0, 1, 3))
    across = pascal_kernel(luminance, 3)
    acuity = pascal_kernel(across, 0)

    def advance(state, inputs):
        carried = inputs[0][None, None, :] * state + inputs[1]
        return carried, carried

    initial_state = jnp.zeros(luminance.shape[1:], jnp.float32)
    _, forward = lax.scan(advance, initial_state, (retention, luminance))
    _, reverse_pass = lax.scan(advance, initial_state, (retention, luminance), reverse=True)
    veil = 0.125 * (forward + reverse_pass)
    return acuity, veil
```

```python
import jax
import jax.numpy as jnp
from jax import lax
from jax.experimental import pallas as pl
from jax.experimental.pallas import tpu as pltpu
from jax.sharding import PartitionSpec as P

taps = (0.0625, 0.25, 0.375, 0.25, 0.0625)

SIDE = 4
ROWS = 128
HALF = 256
LANES = 128
HOURS = 96
GROUP = HOURS // SIDE
FINAL = GROUP // SIDE
BLOCK = 16
STEPS = 64.0
TOP = 32752.0
FLOOR = 2.0**-100


def place(x, y, core):
    return ((x % SIDE) * SIDE + y % SIDE) * 2 + core


def ring(hop, second):
    pairs = []
    for x in range(SIDE):
        for y in range(SIDE):
            for core in range(2):
                along_x = (core == 0) != second
                target = place(x + hop, y, core) if along_x else place(x, y + hop, core)
                pairs.append((place(x, y, core), target))
    return pairs


siblings = [(i, i ^ 1) for i in range(2 * SIDE * SIDE)]


def level_of(biggest):
    return jnp.ceil(STEPS * jnp.log2(jnp.maximum(biggest, FLOOR)))


def coded(values, level):
    return jnp.round(values * (TOP * jnp.exp2(level * (-1.0 / STEPS)))).astype(jnp.int32)


def unit_of(level):
    return jnp.exp2(level * (1.0 / STEPS)) * (1.0 / TOP)


def wide(block):
    return block.astype(jnp.int32).astype(jnp.float32)


def narrow(block):
    return block.astype(jnp.int32).astype(jnp.int16)


def tail(hours):
    return -(-hours // 16) * 16


def encode_tile(tile, hour, out, levels):
    level = level_of(jnp.max(jnp.abs(tile), axis=0, keepdims=True))
    out[pl.ds(hour * ROWS, ROWS), :] = coded(tile, level).astype(jnp.int16)
    levels[pl.ds(hour, 1), :] = level


def render_kernel(core, sky, own, other, near, far, back, mine, lines, images, levels):
    step = pl.program_id(0)
    half = 72 * BLOCK
    for side in range(2):
        columns = slice(side * LANES, (side + 1) * LANES)
        for index, block in enumerate((own, other)):
            values = block[:, :, columns].astype(jnp.float32)
            lines[side, index * half : (index + 1) * half, :] = values.reshape(half, LANES)
    for row in range(BLOCK):
        patches = jnp.concatenate(
            [lines[side, pl.ds(row, 144, stride=BLOCK), :] for side in range(2)], axis=1
        )
        image = jnp.dot(
            sky[...], patches.astype(jnp.bfloat16), preferred_element_type=jnp.float32
        )
        for side in range(2):
            images[side, pl.ds(step * BLOCK + row, HOURS, stride=ROWS), :] = image[
                :, side * LANES : (side + 1) * LANES
            ]

    @pl.when(step == pl.num_programs(0) - 1)
    def _():
        size = GROUP * ROWS
        for side in range(2):
            mine[:, side * LANES : (side + 1) * LANES] = images[side, 0:size, :]
        for part, out in enumerate((near, far, back)):
            levels[...] = jnp.zeros_like(levels)

            def hour_step(hour, carry):
                start = pl.multiple_of((part + 1) * size + hour * ROWS, ROWS)
                tile = [images[side, pl.ds(start, ROWS), :] for side in range(2)]
                encode_tile(jnp.concatenate(tile, axis=1), hour, out, levels)
                return carry

            lax.fori_loop(0, GROUP, hour_step, 0)
            out[size:, :] = narrow(levels[...])


def render(core, sky, own, other):
    size, extra = GROUP * ROWS, tail(GROUP)
    whole = lambda i, core: (0, 0)
    sent = jax.ShapeDtypeStruct((size + extra, HALF), jnp.int16)
    return pl.pallas_call(
        render_kernel,
        grid_spec=pltpu.PrefetchScalarGridSpec(
            num_scalar_prefetch=1,
            grid=(ROWS // BLOCK,),
            in_specs=[
                pl.BlockSpec((HOURS, 144), whole),
                pl.BlockSpec((None, 72, BLOCK, HALF), lambda i, core: (0, 0, i, core[0])),
                pl.BlockSpec((72, BLOCK, HALF), lambda i, core: (0, i, 0)),
            ],
            out_specs=[pl.BlockSpec((size + extra, HALF), whole)] * 3
            + [pl.BlockSpec((size, HALF), whole)],
            scratch_shapes=[
                pltpu.VMEM((2, 144 * BLOCK, LANES), jnp.float32),
                pltpu.VMEM((2, HOURS * ROWS, LANES), jnp.float32),
                pltpu.VMEM((extra, HALF), jnp.float32),
            ],
        ),
        out_shape=[sent] * 3 + [jax.ShapeDtypeStruct((size, HALF), jnp.float32)],
        compiler_params=pltpu.CompilerParams(vmem_limit_bytes=44 * 2**20),
        name="render",
    )(core, sky, own, other)


def join_kernel(mine, near, far, back, near_out, far_out, back_out, mine_out, units, levels):
    size = GROUP * ROWS
    for index, got in enumerate((near, far, back)):
        units[index] = unit_of(wide(got[size:, :]))
    for part, out in enumerate((mine_out, near_out, far_out, back_out)):
        if part:
            levels[...] = jnp.zeros_like(levels)

        def hour_step(hour, carry):
            at = part * FINAL + hour
            rows = pl.ds(pl.multiple_of(at * ROWS, ROWS), ROWS)
            tile = mine[rows, :]
            for index, got in enumerate((near, far, back)):
                tile = tile + wide(got[rows, :]) * units[index, pl.ds(at, 1), :]
            if part:
                encode_tile(tile, hour, out, levels)
            else:
                out[pl.ds(pl.multiple_of(hour * ROWS, ROWS), ROWS), :] = tile
            return carry

        lax.fori_loop(0, FINAL, hour_step, 0)
        if part:
            out[FINAL * ROWS :, :] = narrow(levels[...])


def join(mine, near, far, back):
    size, extra = FINAL * ROWS, tail(FINAL)
    sent = jax.ShapeDtypeStruct((size + extra, HALF), jnp.int16)
    return pl.pallas_call(
        join_kernel,
        out_shape=[sent] * 3 + [jax.ShapeDtypeStruct((size, HALF), jnp.float32)],
        in_specs=[pl.BlockSpec(memory_space=pltpu.VMEM)] * 4,
        out_specs=[pl.BlockSpec(memory_space=pltpu.VMEM)] * 4,
        scratch_shapes=[
            pltpu.VMEM((3, tail(GROUP), HALF), jnp.float32),
            pltpu.VMEM((extra, HALF), jnp.float32),
        ],
        compiler_params=pltpu.CompilerParams(vmem_limit_bytes=44 * 2**20),
        name="join",
    )(mine, near, far, back)


def glare_kernel(chips, mine, near, far, back, rates, out, image, lines, front):
    size = FINAL * ROWS
    units = [unit_of(wide(got[size:, :])) for got in (near, far, back)]
    for hour in range(FINAL):
        rows = pl.ds(hour * ROWS, ROWS)
        tile = mine[rows, :]
        for got, unit in zip((near, far, back), units):
            tile = tile + wide(got[rows, :]) * unit[hour : hour + 1, :]
        for side in range(2):
            image[side, rows, :] = tile[:, side * LANES : (side + 1) * LANES]
    image[:, size:, :] = jnp.zeros((2, 8 * ROWS - size, LANES), jnp.float32)
    lines[0:16, :] = jnp.zeros((16, HALF), jnp.float32)
    lines[8 * (ROWS + 2) :, :] = jnp.zeros((16, HALF), jnp.float32)

    def rate(row):
        return rates[pl.ds(chips[row // 8] * 8 + row % 8, 1), :]

    def down(row, state):
        light = jnp.concatenate(
            [image[side, pl.ds(row, 8, stride=ROWS), :] for side in range(2)], axis=1
        )
        state = rate(row) * state + light
        lines[pl.ds(pl.multiple_of(8 * row + 16, 8), 8), :] = light
        front[pl.ds(pl.multiple_of(8 * row, 8), 8), :] = state
        return state

    nothing = jnp.zeros((8, HALF), jnp.float32)
    lax.fori_loop(0, ROWS, down, nothing, unroll=4)
    slot = lax.broadcasted_iota(jnp.int32, (8, HALF), 0)

    def up(step, state):
        owner = 31 - step
        veils, blurs = [], []
        for k in (3, 2, 1, 0):
            row = owner * 4 + k
            light = [
                lines[pl.ds(pl.multiple_of(8 * (row + offset), 8), 8), :] for offset in range(5)
            ]
            state = rate(row) * state + light[2]
            veils.insert(0, 0.125 * (front[pl.ds(pl.multiple_of(8 * row, 8), 8), :] + state))
            blurs.insert(0, sum(tap * line for tap, line in zip(taps, light)))
        for index, values in enumerate((blurs, veils)):
            biggest = jnp.abs(values[0])
            for value in values[1:]:
                biggest = jnp.maximum(biggest, jnp.abs(value))
            level = level_of(jnp.max(biggest, axis=0, keepdims=True))
            mark = level.astype(jnp.int32)
            block = jnp.concatenate(
                [jnp.where(slot < FINAL, coded(value, level), mark) for value in values], axis=0
            )
            start = pl.multiple_of(owner * 64 + index * 32, 32)
            out[pl.ds(start, 32), :] = block.astype(jnp.int16)
        return state

    lax.fori_loop(0, 32, up, nothing)


def glare(chips, mine, near, far, back, rates):
    return pl.pallas_call(
        glare_kernel,
        out_shape=jax.ShapeDtypeStruct((32 * 64, HALF), jnp.int16),
        in_specs=[pl.BlockSpec(memory_space=pltpu.SMEM)]
        + [pl.BlockSpec(memory_space=pltpu.VMEM)] * 5,
        out_specs=pl.BlockSpec(memory_space=pltpu.VMEM),
        scratch_shapes=[
            pltpu.VMEM((2, 8 * ROWS, LANES), jnp.float32),
            pltpu.VMEM((8 * (ROWS + 4), HALF), jnp.float32),
            pltpu.VMEM((8 * ROWS, HALF), jnp.float32),
        ],
        compiler_params=pltpu.CompilerParams(vmem_limit_bytes=32 * 2**20),
        name="glare",
    )(chips, mine, near, far, back, rates)


def finish_kernel(parts, acuity, veil, blurred):
    for source in range(32):
        x, y, core = source // 8, source // 2 % 4, source % 2
        first, second = (x, y) if core == 0 else (y, x)
        hour = first * GROUP + second * FINAL
        columns = slice(core * HALF, (core + 1) * HALF)
        for index, out in enumerate((blurred, veil)):
            start = source * 64 + index * 32
            block = wide(parts[start : start + 32, :])
            block = block * unit_of(block[FINAL : FINAL + 1, :])
            for row in range(4):
                piece = block[row * 8 : row * 8 + FINAL, :]
                if index:
                    out[row, 0, hour : hour + FINAL, columns] = piece
                else:
                    out[row, hour : hour + FINAL, columns] = piece
    column = lax.broadcasted_iota(jnp.int32, (HOURS, 2 * HALF), 1)
    for row in range(4):
        image = blurred[row]
        total = taps[2] * image
        for offset in (-2, -1, 1, 2):
            moved = pltpu.roll(image, (-offset) % (2 * HALF), 1)
            inside = (column + offset >= 0) & (column + offset < 2 * HALF)
            total = total + taps[2 + offset] * jnp.where(inside, moved, 0.0)
        acuity[row, 0] = total


def finish(parts):
    shape = jax.ShapeDtypeStruct((4, 1, HOURS, 2 * HALF), jnp.float32)
    return pl.pallas_call(
        finish_kernel,
        out_shape=[shape, shape],
        in_specs=[pl.BlockSpec(memory_space=pltpu.VMEM)],
        out_specs=[pl.BlockSpec(memory_space=pltpu.VMEM)] * 2,
        scratch_shapes=[pltpu.VMEM((4, HOURS, 2 * HALF), jnp.float32)],
        compiler_params=pltpu.CompilerParams(vmem_limit_bytes=32 * 2**20),
        name="finish",
    )(parts)


def hour_order(first, second):
    steps = jnp.arange(HOURS, dtype=jnp.int32)
    group, part, inner = steps // GROUP, steps // FINAL % SIDE, steps % FINAL
    return (first + group) % SIDE * GROUP + (second + part) % SIDE * FINAL + inner


def shards(coefficients, sky_year, hour_list, retention):
    me = lax.axis_index("patch")
    x, y, core = me // (2 * SIDE), me // 2 % SIDE, me % 2
    first, second = jnp.where(core == 0, x, y), jnp.where(core == 0, y, x)
    move = lambda value, pairs: lax.ppermute(value, "patch", pairs)

    own_rates = lax.dynamic_slice(retention, (0, core * HALF), (4, HALF))
    sibling_rates = move(
        lax.dynamic_slice(retention, (0, (1 - core) * HALF), (4, HALF)), siblings
    )
    rates = jnp.where(
        core == 0,
        jnp.concatenate([own_rates, sibling_rates]),
        jnp.concatenate([sibling_rates, own_rates]),
    )
    chip = jnp.arange(SIDE * SIDE, dtype=jnp.int32)
    one, two = chip // SIDE, chip % SIDE
    chips = jnp.where(
        core == 0,
        (x - one) % SIDE + SIDE * ((y - two) % SIDE),
        (y - two) % SIDE + SIDE * ((x - one) % SIDE),
    )

    theirs = lax.dynamic_slice(
        coefficients[0], (0, 0, (1 - core) * HALF), coefficients.shape[1:3] + (HALF,)
    )
    other = move(theirs, siblings)
    order = jnp.concatenate([hour_order(first, second), hour_order(second, first)])
    both = jnp.take(sky_year, hour_list[order], axis=1, mode="clip")
    sky = jnp.concatenate([both[:, :HOURS], move(both[:, HOURS:], siblings)], axis=0).T

    near, far, back, mine = render(core.reshape(1), sky, coefficients, other)
    rates, near = lax.optimization_barrier((rates, near))
    near, far, back = [
        move(part, ring(hop, False)) for hop, part in ((1, near), (2, far), (3, back))
    ]
    rates = jnp.concatenate([rates] + [move(rates, ring(hop, False)) for hop in (1, 2, 3)])
    rates = jnp.concatenate([rates] + [move(rates, ring(hop, True)) for hop in (1, 2, 3)])
    near, far, back, mine = join(mine, near, far, back)
    near, far, back = [
        move(part, ring(hop, True)) for hop, part in ((1, near), (2, far), (3, back))
    ]
    parts = glare(chips, mine, near, far, back, rates)
    parts = lax.all_to_all(parts, "patch", 0, 0, tiled=True)
    return tuple(finish(parts))


def solution(mesh):
    placed = (P("view", "patch", None, None), P("patch", None), P(), P("patch", None))
    return jax.shard_map(
        shards,
        mesh=mesh,
        in_specs=placed,
        out_specs=(P("patch", "view", None, None), P("patch", "view", None, None)),
        check_vma=False,
    )
```

```python
import functools

import jax
import jax.numpy as jnp
from jax import lax
from jax.experimental import pallas as pl
from jax.experimental.pallas import tpu as pltpu
from jax.sharding import PartitionSpec as P

taps = (0.0625, 0.25, 0.375, 0.25, 0.0625)

SIDE = 4
ROWS = 128
HALF = 256
HOURS = 96
GROUP = HOURS // SIDE
FINAL = GROUP // SIDE
PATCHES = 144
BLOCK = 16
PIECES = 2
PIECE = ROWS // PIECES
PART = PIECE // 2 * GROUP
PAIR = 2 * GROUP
STEPS = 64.0
TOP = 32752.0
FLOOR = 2.0**-100
CHUNK = 56
CHIP_ROWS = 8
RATES = 3 * CHIP_ROWS
SENT = 2 * PART + PAIR + RATES + 8
MESSAGE = 104


def place(x, y, core):
    return ((x % SIDE) * SIDE + y % SIDE) * 2 + core


def ring(hop, second):
    pairs = []
    for x in range(SIDE):
        for y in range(SIDE):
            for core in range(2):
                along_x = (core == 0) != second
                target = place(x + hop, y, core) if along_x else place(x, y + hop, core)
                pairs.append((place(x, y, core), target))
    return pairs


siblings = [(i, i ^ 1) for i in range(2 * SIDE * SIDE)]


def level_of(biggest):
    return jnp.ceil(STEPS * jnp.log2(jnp.maximum(biggest, FLOOR)))


def factor_of(level):
    return TOP * jnp.exp2(level * (-1.0 / STEPS))


def unit_of(level):
    return jnp.exp2(level * (1.0 / STEPS)) * (1.0 / TOP)


def coded(values, factor):
    return jnp.round(values * factor).astype(jnp.int32).astype(jnp.int16)


def wide(block):
    return block.astype(jnp.int32).astype(jnp.float32)


def narrow(block):
    return block.astype(jnp.int32).astype(jnp.int16)


def digits(rates):
    rest, parts = rates, []
    for _ in range(3):
        rest = rest * 32768.0
        part = jnp.minimum(jnp.floor(rest), 32767.0)
        rest = rest - part
        parts.append(part)
    return jnp.concatenate(parts, axis=0)


def undigits(lines):
    first, second, third = [lines[k * CHIP_ROWS : (k + 1) * CHIP_ROWS] for k in range(3)]
    return (first + (second + third * 2.0**-15) * 2.0**-15) * 2.0**-15


def twice(block):
    return jnp.concatenate([block, block], axis=0)


def lines_at(index, count):
    return pl.ds(pl.multiple_of(index * count, count), count)


def split_kernel(piece, core, source, out, sems):
    columns = pl.ds(pl.multiple_of((1 - core[0]) * HALF, HALF), HALF)
    copies = []
    for index in range(8):
        patches = pl.ds(index * (PATCHES // 16), PATCHES // 16)
        part = source.at[0, patches, pl.ds(piece * PIECE, PIECE), columns]
        copies.append(pltpu.make_async_copy(part, out.at[patches], sems.at[index]))
    for copy in copies:
        copy.start()
    for copy in copies:
        copy.wait()


def split(piece, core, coefficients):
    return pl.pallas_call(
        functools.partial(split_kernel, piece),
        out_shape=jax.ShapeDtypeStruct((PATCHES // 2, PIECE, HALF), jnp.bfloat16),
        in_specs=[pl.BlockSpec(memory_space=pltpu.SMEM), pl.BlockSpec(memory_space=pl.ANY)],
        out_specs=pl.BlockSpec(memory_space=pl.ANY),
        scratch_shapes=[pltpu.SemaphoreType.DMA((8,))],
        compiler_params=pltpu.CompilerParams(vmem_limit_bytes=2**20),
        cost_estimate=pl.CostEstimate(flops=0, bytes_accessed=5 * 2**20, transcendentals=0),
        name="split",
    )(core, coefficients)


def select_kernel(hours, sky, rates, out):
    hour = lax.broadcasted_iota(jnp.int32, (HOURS, sky.shape[1]), 1)
    chosen = jnp.where(hours[...] == hour, 1.0, 0.0).astype(jnp.bfloat16)
    out[0:HOURS, 0 : PATCHES // 2] = lax.dot_general(
        chosen, sky[...], (((1,), (1,)), ((), ())), preferred_element_type=jnp.float32
    )
    out[0:HOURS, PATCHES // 2 :] = jnp.zeros((HOURS, HALF - PATCHES // 2), jnp.float32)
    out[HOURS:, :] = jnp.concatenate([rates[...], jnp.zeros_like(rates)], axis=0)


def select(hours, sky, rates):
    out = jax.ShapeDtypeStruct((MESSAGE, HALF), jnp.float32)
    return in_vmem(select_kernel, out, [], "select", 4, (hours, sky, rates))


def render_kernel(
    core, order, sky, rates, own, other, up, down, keep_up, keep_down, mine, images, peaks, ordered
):
    step = pl.program_id(0)

    @pl.when(step == 0)
    def _():
        hour = lax.broadcasted_iota(jnp.int32, (HOURS, HOURS), 1)
        chosen = jnp.where(order[...] == hour, 1.0, 0.0).astype(jnp.bfloat16)
        sorted_sky = jnp.dot(chosen, sky[...], preferred_element_type=jnp.float32)
        ordered[...] = sorted_sky.astype(jnp.bfloat16)
        peaks[...] = jnp.zeros_like(peaks)

    patches = jnp.concatenate([own[...], other[...]], axis=0)
    by_row = jnp.swapaxes(patches, 0, 1)
    rows_seen = ordered[...]
    peak = jnp.zeros((HOURS, HALF), jnp.float32)
    for row in range(BLOCK):
        image = jnp.dot(rows_seen, by_row[row], preferred_element_type=jnp.float32)
        peak = jnp.maximum(peak, jnp.abs(image))
        images[lines_at(step * BLOCK + row, HOURS), :] = image
        mine[lines_at(step * BLOCK + row, GROUP), :] = image[:GROUP]
    half = step // (PIECE // BLOCK // 2)
    peaks[half] = jnp.maximum(peaks[half], peak)

    @pl.when(step == pl.num_programs(0) - 1)
    def _():
        for out, parts in ((up, ((2, 0), (1, 1))), (down, ((2, 1), (3, 0)))):
            levels = []
            for index, (group, half) in enumerate(parts):
                hours = slice(group * GROUP, (group + 1) * GROUP)
                level = level_of(peaks[half, hours, :])
                factor = factor_of(level)
                levels.append(level)
                first = half * (PIECE // 2)

                def pair_step(pair, carry):
                    for k in range(2):
                        start = (first + 2 * pair + k) * HOURS + group * GROUP
                        start = pl.multiple_of(start, GROUP)
                        tile = images[pl.ds(start, GROUP), :] * factor
                        carry = carry + (jnp.round(tile).astype(jnp.int32),)
                    at = pl.multiple_of(index * PART + pair * PAIR, PAIR)
                    out[pl.ds(at, PAIR), :] = jnp.concatenate(carry, axis=0).astype(jnp.int16)
                    return ()

                lax.fori_loop(0, PIECE // 4, pair_step, (), unroll=2)
            pad = jnp.zeros((8, HALF), jnp.float32)
            last = jnp.concatenate(levels + [digits(rates[...]), pad], axis=0)
            out[2 * PART :, :] = narrow(last)
        for out, group, half in ((keep_up, 1, 0), (keep_down, 3, 1)):

            def keep_step(row, carry):
                start = (half * (PIECE // 2) + row) * HOURS + group * GROUP
                out[lines_at(row, GROUP), :] = images[pl.ds(pl.multiple_of(start, GROUP), GROUP), :]
                return carry

            lax.fori_loop(0, PIECE // 2, keep_step, 0, unroll=4)


def render(piece, core, order, sky, rates, own, other):
    whole = lambda i, core: (0, 0)
    steps = PIECE // BLOCK
    sent = jax.ShapeDtypeStruct((SENT, HALF), jnp.int16)
    kept = jax.ShapeDtypeStruct((PART, HALF), jnp.float32)
    outs = [sent, sent, kept, kept, jax.ShapeDtypeStruct((2 * PART, HALF), jnp.float32)]
    return pl.pallas_call(
        render_kernel,
        grid_spec=pltpu.PrefetchScalarGridSpec(
            num_scalar_prefetch=1,
            grid=(steps,),
            in_specs=[
                pl.BlockSpec((HOURS, 1), whole),
                pl.BlockSpec((HOURS, PATCHES), whole),
                pl.BlockSpec((CHIP_ROWS, HALF), whole),
                pl.BlockSpec(
                    (None, PATCHES // 2, BLOCK, HALF),
                    lambda i, core: (0, 0, piece * steps + i, core[0]),
                ),
                pl.BlockSpec((PATCHES // 2, BLOCK, HALF), lambda i, core: (0, i, 0)),
            ],
            out_specs=[pl.BlockSpec(out.shape, whole) for out in outs],
            scratch_shapes=[
                pltpu.VMEM((HOURS * PIECE, HALF), jnp.float32),
                pltpu.VMEM((2, HOURS, HALF), jnp.float32),
                pltpu.VMEM((HOURS, PATCHES), jnp.bfloat16),
            ],
        ),
        out_shape=outs,
        compiler_params=pltpu.CompilerParams(vmem_limit_bytes=24 * 2**20),
        cost_estimate=pl.CostEstimate(
            flops=2 * PATCHES * HOURS * PIECE * HALF, bytes_accessed=18 * 2**20, transcendentals=0
        ),
        name="render",
    )(core, order, sky, rates, own, other)


def in_vmem(kernel, outs, scratch, name, cost, operands, scalars=0):
    spaces = [pltpu.SMEM] * scalars + [pltpu.VMEM] * (len(operands) - scalars)
    return pl.pallas_call(
        kernel,
        out_shape=outs,
        in_specs=[pl.BlockSpec(memory_space=space) for space in spaces],
        out_specs=jax.tree.map(lambda out: pl.BlockSpec(memory_space=pltpu.VMEM), outs),
        scratch_shapes=scratch,
        compiler_params=pltpu.CompilerParams(vmem_limit_bytes=12 * 2**20),
        cost_estimate=pl.CostEstimate(flops=0, bytes_accessed=cost * 2**20, transcendentals=0),
        name=name,
    )(*operands)


def merge_kernel(keep_up, keep_down, got_up, got_down, up, down, total):
    nothing = jnp.zeros((PAIR, HALF), jnp.float32)
    for keep, got, out in ((keep_up, got_up, up), (keep_down, got_down, down)):
        last = wide(got[2 * PART :, :])
        unit = twice(unit_of(last[:GROUP]))

        def add_step(pair, peak):
            at = lines_at(pair, PAIR)
            tile = keep[at, :] + wide(got[at, :]) * unit
            total[at, :] = tile
            return jnp.maximum(peak, jnp.abs(tile))

        peak = lax.fori_loop(0, PART // PAIR, add_step, nothing, unroll=2)
        level = level_of(jnp.maximum(peak[:GROUP], peak[GROUP:]))
        factor = twice(factor_of(level))

        def code_step(pair, carry):
            at = lines_at(pair, PAIR)
            out[at, :] = coded(total[at, :], factor)
            return carry

        lax.fori_loop(0, PART // PAIR, code_step, 0, unroll=2)
        out[PART:, :] = narrow(jnp.concatenate([level, last[PAIR : PAIR + RATES]], axis=0))


def merge(keep_up, keep_down, got_up, got_down):
    sent = jax.ShapeDtypeStruct((PART + GROUP + RATES, HALF), jnp.int16)
    scratch = [pltpu.VMEM((PART, HALF), jnp.float32)]
    return in_vmem(
        merge_kernel, [sent, sent], scratch, "merge", 5, (keep_up, keep_down, got_up, got_down)
    )


def join_kernel(rates, mine, got_up, got_down, up, down, near, far, back, own, own_rates, total):
    peak = jnp.zeros((PAIR, HALF), jnp.float32)
    for half, (direct, relayed) in enumerate(((got_down, up), (got_up, down))):
        direct_unit = twice(unit_of(wide(direct[2 * PART :, :])[GROUP:PAIR]))
        relayed_unit = twice(unit_of(wide(relayed[PART:, :])[:GROUP]))

        def add_step(pair, peak):
            at = lines_at(pair, PAIR)
            direct_at = pl.ds(pl.multiple_of(PART + pair * PAIR, PAIR), PAIR)
            out_at = pl.ds(pl.multiple_of(half * PART + pair * PAIR, PAIR), PAIR)
            tile = mine[out_at, :] + wide(direct[direct_at, :]) * direct_unit
            tile = tile + wide(relayed[at, :]) * relayed_unit
            total[out_at, :] = tile
            return jnp.maximum(peak, jnp.abs(tile))

        peak = lax.fori_loop(0, PART // PAIR, add_step, peak, unroll=2)
    level = level_of(jnp.maximum(peak[:GROUP], peak[GROUP:]))
    factor = factor_of(level)
    outs = (own, near, far, back)
    factors = [
        jnp.concatenate([factor[part * FINAL : (part + 1) * FINAL]] * 8, axis=0)
        for part in range(SIDE)
    ]

    def split_step(eight, carry):
        tile = total[lines_at(eight, 8 * GROUP), :]
        for part, out in enumerate(outs):
            starts = [k * GROUP + part * FINAL for k in range(8)]
            block = jnp.concatenate([tile[at : at + FINAL] for at in starts], axis=0)
            at = lines_at(eight, 8 * FINAL)
            out[at, :] = coded(block, factors[part]) if part else block
        return carry

    lax.fori_loop(0, PIECE // 8, split_step, 0)
    places = ((got_up, 2 * PART, PAIR), (up, PART, GROUP), (got_down, 2 * PART, PAIR))
    ahead = [wide(got[start:, :])[at : at + RATES] for got, start, at in places]
    all_rates = narrow(jnp.concatenate([digits(rates[...])] + ahead, axis=0))
    own_rates[...] = all_rates
    for part, out in enumerate(outs):
        if part:
            mark = level[part * FINAL : (part + 1) * FINAL]
            rest = jnp.zeros((16 - FINAL, HALF), jnp.float32)
            out[PIECE * FINAL : PIECE * FINAL + 16, :] = narrow(
                jnp.concatenate([mark, rest], axis=0)
            )
            if out.shape[0] > PIECE * FINAL + 16:
                out[PIECE * FINAL + 16 :, :] = all_rates


def join(piece, rates, mine, got_up, got_down, up, down):
    size = PIECE * FINAL + 16 + (0 if piece else SIDE * RATES)
    sent = jax.ShapeDtypeStruct((size, HALF), jnp.int16)
    own_rates = jax.ShapeDtypeStruct((SIDE * RATES, HALF), jnp.int16)
    own = jax.ShapeDtypeStruct((PIECE * FINAL, HALF), jnp.float32)
    scratch = [pltpu.VMEM((2 * PART, HALF), jnp.float32)]
    return in_vmem(
        join_kernel,
        [sent] * 3 + [own, own_rates],
        scratch,
        "join",
        6,
        (rates, mine, got_up, got_down, up, down),
    )


def glare_kernel(chips, own_rates, *refs):
    pieces = [refs[4 * piece : 4 * piece + 4] for piece in range(PIECES)]
    out, lines, front, rates = refs[4 * PIECES :]
    size = PIECE * FINAL + 16
    for back, block in enumerate((own_rates, *[got.at[size:] for got in pieces[0][:3]])):
        coded_rates = wide(block[...])
        for chip in range(SIDE):
            start = (back * SIDE + chip) * CHIP_ROWS
            rates[start : start + CHIP_ROWS, :] = undigits(
                coded_rates[chip * RATES : (chip + 1) * RATES]
            )
    eights = PIECE // 8
    lines[0:16, :] = jnp.zeros((16, HALF), jnp.float32)
    lines[8 * (ROWS + 2) :, :] = jnp.zeros((16, HALF), jnp.float32)
    state = jnp.zeros((FINAL, HALF), jnp.float32)
    nothing = state

    def spots(eight, k):
        return pl.ds(pl.multiple_of(64 * eight, 64) + 8 * k, FINAL)

    for piece, (near, far, back, mine) in enumerate(pieces):
        gots = (near, far, back)
        units = [unit_of(wide(got[PIECE * FINAL : size, :])[:FINAL]) for got in gots]
        units = [jnp.concatenate([unit] * 8, axis=0) for unit in units]

        def down(index, state):
            eight = piece * eights + index
            at = lines_at(index, 8 * FINAL)
            tile = mine[at, :]
            for got, unit in zip(gots, units):
                tile = tile + wide(got[at, :]) * unit
            share = rates[lines_at(chips[eight], 8), :]
            for k in range(8):
                light = tile[k * FINAL : (k + 1) * FINAL]
                state = share[k : k + 1] * state + light
                lines[spots(eight, k + 2), :] = light
                front[spots(eight, k), :] = state
            return state

        state = lax.fori_loop(0, eights, down, state)

    def up(step, state):
        eight = ROWS // 8 - 1 - step
        share = rates[lines_at(chips[eight], 8), :]
        light = [lines[spots(eight, k), :] for k in range(12)]
        for owner in (1, 0):
            veils, blurs = [None] * 4, [None] * 4
            for k in (3, 2, 1, 0):
                row = owner * 4 + k
                state = share[row : row + 1] * state + light[row + 2]
                veils[k] = 0.125 * (front[spots(eight, row), :] + state)
                near, wider = light[row + 1] + light[row + 3], light[row] + light[row + 4]
                blurs[k] = taps[2] * light[row + 2] + taps[1] * near + taps[0] * wider
            blocks, levels = [], []
            for values in (blurs, veils):
                block = jnp.concatenate(values, axis=0)
                level = level_of(jnp.max(jnp.abs(block), axis=0, keepdims=True))
                blocks.append(jnp.round(block * factor_of(level)))
                levels.append(level)
            rest = jnp.zeros((CHUNK - 8 * FINAL - 2, HALF), jnp.float32)
            out[2 * eight + owner] = narrow(jnp.concatenate(blocks + levels + [rest], axis=0))
        return state

    lax.fori_loop(0, ROWS // 8, up, nothing)


def glare(chips, own_rates, pieces):
    out = jax.ShapeDtypeStruct((32, CHUNK, HALF), jnp.int16)
    scratch = [
        pltpu.VMEM((8 * (ROWS + 4), HALF), jnp.float32),
        pltpu.VMEM((8 * ROWS, HALF), jnp.float32),
        pltpu.VMEM((ROWS, HALF), jnp.float32),
    ]
    operands = (chips, own_rates) + tuple(part for piece in pieces for part in piece)
    return in_vmem(glare_kernel, out, scratch, "glare", 8, operands, scalars=1)


def finish_kernel(parts, acuity, veil, blurred):
    for source in range(32):
        x, y, core = source // 8, source // 2 % 4, source % 2
        first, second = (x, y) if core == 0 else (y, x)
        hour = first * GROUP + second * FINAL
        columns = slice(core * HALF, (core + 1) * HALF)
        block = wide(parts[source])
        units = unit_of(block[8 * FINAL : 8 * FINAL + 2])
        for row in range(4):
            at = row * FINAL
            blurred[row, hour : hour + FINAL, columns] = block[at : at + FINAL] * units[0:1]
            at = (row + 4) * FINAL
            veil[row, 0, hour : hour + FINAL, columns] = block[at : at + FINAL] * units[1:2]
    column = lax.broadcasted_iota(jnp.int32, (HOURS, 2 * HALF), 1)
    for row in range(4):
        image = blurred[row]
        total = taps[2] * image
        for offset in (-2, -1, 1, 2):
            moved = pltpu.roll(image, (-offset) % (2 * HALF), 1)
            inside = (column + offset >= 0) & (column + offset < 2 * HALF)
            total = total + taps[2 + offset] * jnp.where(inside, moved, 0.0)
        acuity[row, 0] = total


def finish(parts):
    shape = jax.ShapeDtypeStruct((4, 1, HOURS, 2 * HALF), jnp.float32)
    scratch = [pltpu.VMEM((4, HOURS, 2 * HALF), jnp.float32)]
    return in_vmem(finish_kernel, [shape, shape], scratch, "finish", 4, (parts,))


def hour_order(first, second):
    steps = jnp.arange(HOURS, dtype=jnp.int32)
    group, part, inner = steps // GROUP, steps // FINAL % SIDE, steps % FINAL
    return (first + group) % SIDE * GROUP + (second + part) % SIDE * FINAL + inner


def shards(coefficients, sky_year, hour_list, retention):
    me = lax.axis_index("patch")
    x, y, core = me // (2 * SIDE), me // 2 % SIDE, me % 2
    first, second = jnp.where(core == 0, x, y), jnp.where(core == 0, y, x)
    move = lambda value, pairs: lax.ppermute(value, "patch", pairs)
    first_up, first_down = ring(1, False), ring(-1, False)

    chip = jnp.arange(SIDE * SIDE, dtype=jnp.int32)
    one, two = chip // SIDE, chip % SIDE
    chips = jnp.where(
        core == 0,
        (x - one) % SIDE + SIDE * ((y - two) % SIDE),
        (y - two) % SIDE + SIDE * ((x - one) % SIDE),
    )

    spot = core.reshape(1)
    coefficients = pltpu.with_memory_space_constraint(coefficients, pltpu.HBM)
    others = [move(split(piece, spot, coefficients), siblings) for piece in range(PIECES)]
    own_rates = lax.dynamic_slice(retention, (0, core * HALF), (4, HALF))
    their_rates = lax.dynamic_slice(retention, (0, (1 - core) * HALF), (4, HALF))
    chosen = select(hour_list[:, None], sky_year, their_rates)
    got = move(chosen, siblings)
    sky = [message[:HOURS, : PATCHES // 2] for message in (chosen, got)]
    sky = jnp.concatenate(sky, axis=1).astype(jnp.bfloat16)
    sibling_rates = got[HOURS : HOURS + 4]
    rates = jnp.where(
        core == 0,
        jnp.concatenate([own_rates, sibling_rates]),
        jnp.concatenate([sibling_rates, own_rates]),
    )
    order = hour_order(first, second)[:, None]

    rendered = []
    for piece in range(PIECES):
        up, down, *kept = render(piece, spot, order, sky, rates, coefficients, others[piece])
        rendered.append((move(up, first_up), move(down, first_down), *kept))
    merged = []
    for up, down, keep_up, keep_down, mine in rendered:
        relay_up, relay_down = merge(keep_up, keep_down, up, down)
        merged.append((mine, up, down, move(relay_up, first_up), move(relay_down, first_down)))
    pieces, coded_rates = [], []
    for piece, parts in enumerate(merged):
        *sent, own, own_coded = join(piece, rates, *parts)
        coded_rates.append(own_coded)
        got = [move(part, ring(hop, True)) for hop, part in zip((1, 2, 3), sent)]
        pieces.append((*got, own))
    parts = glare(chips, coded_rates[0], pieces)
    parts = lax.all_to_all(parts, "patch", 0, 0, tiled=True)
    return tuple(finish(parts))


def solution(mesh):
    placed = (P("view", "patch", None, None), P("patch", None), P(), P("patch", None))
    return jax.shard_map(
        shards,
        mesh=mesh,
        in_specs=placed,
        out_specs=(P("patch", "view", None, None), P("patch", "view", None, None)),
        check_vma=False,
    )
```

```python
import functools

import jax
import jax.numpy as jnp
from jax import lax
from jax.experimental import pallas as pl
from jax.experimental.pallas import tpu as pltpu
from jax.sharding import PartitionSpec as P

taps = (0.0625, 0.25, 0.375, 0.25, 0.0625)

SIDE = 4
ROWS = 128
HALF = 256
HOURS = 96
GROUP = HOURS // SIDE
FINAL = GROUP // SIDE
PATCHES = 144
BLOCK = 16
PIECES = 2
PIECE = ROWS // PIECES
PART = PIECE // 2 * GROUP
PAIR = 2 * GROUP
STEPS = 64.0
TOP = 32752.0
FLOOR = 2.0**-100
CHUNK = 56
CHIP_ROWS = 8
RATES = 3 * CHIP_ROWS
SENT = 2 * PART + PAIR + RATES + 8
FIRST = PIECE * FINAL + 16 + 4 * RATES
MESSAGE = 104


def place(x, y, core):
    return ((x % SIDE) * SIDE + y % SIDE) * 2 + core


def ring(hop, second):
    pairs = []
    for x in range(SIDE):
        for y in range(SIDE):
            for core in range(2):
                along_x = (core == 0) != second
                target = place(x + hop, y, core) if along_x else place(x, y + hop, core)
                pairs.append((place(x, y, core), target))
    return pairs


siblings = [(i, i ^ 1) for i in range(2 * SIDE * SIDE)]


def level_of(biggest):
    return jnp.ceil(STEPS * jnp.log2(jnp.maximum(biggest, FLOOR)))


def factor_of(level):
    return TOP * jnp.exp2(level * (-1.0 / STEPS))


def unit_of(level):
    return jnp.exp2(level * (1.0 / STEPS)) * (1.0 / TOP)


def coded(values, factor):
    return jnp.round(values * factor).astype(jnp.int32).astype(jnp.int16)


def wide(block):
    return block.astype(jnp.int32).astype(jnp.float32)


def narrow(block):
    return block.astype(jnp.int32).astype(jnp.int16)


def digits(rates):
    rest, parts = rates, []
    for _ in range(3):
        rest = rest * 32768.0
        part = jnp.minimum(jnp.floor(rest), 32767.0)
        rest = rest - part
        parts.append(part)
    return jnp.concatenate(parts, axis=0)


def undigits(lines):
    first, second, third = [lines[k * CHIP_ROWS : (k + 1) * CHIP_ROWS] for k in range(3)]
    return (first + (second + third * 2.0**-15) * 2.0**-15) * 2.0**-15


def twice(block):
    return jnp.concatenate([block, block], axis=0)


def lines_at(index, count):
    return pl.ds(pl.multiple_of(index * count, count), count)


def split_kernel(core, source, out):
    out[...] = source[...]


def split(piece, core, coefficients):
    count = PATCHES // 16
    return pl.pallas_call(
        split_kernel,
        grid_spec=pltpu.PrefetchScalarGridSpec(
            num_scalar_prefetch=1,
            grid=(8,),
            in_specs=[
                pl.BlockSpec((None, count, PIECE, HALF), lambda i, core: (0, i, piece, 1 - core[0]))
            ],
            out_specs=pl.BlockSpec((count, PIECE, HALF), lambda i, core: (i, 0, 0)),
        ),
        out_shape=jax.ShapeDtypeStruct((PATCHES // 2, PIECE, HALF), jnp.bfloat16),
        compiler_params=pltpu.CompilerParams(vmem_limit_bytes=4 * 2**20),
        cost_estimate=pl.CostEstimate(flops=0, bytes_accessed=5 * 2**20, transcendentals=0),
        name="split",
    )(core, coefficients)


def select_kernel(hours, sky, rates, out):
    hour = lax.broadcasted_iota(jnp.int32, (HOURS, sky.shape[1]), 1)
    chosen = jnp.where(hours[...] == hour, 1.0, 0.0).astype(jnp.bfloat16)
    out[0:HOURS, 0 : PATCHES // 2] = lax.dot_general(
        chosen, sky[...], (((1,), (1,)), ((), ())), preferred_element_type=jnp.float32
    )
    out[0:HOURS, PATCHES // 2 :] = jnp.zeros((HOURS, HALF - PATCHES // 2), jnp.float32)
    out[HOURS:, :] = jnp.concatenate([rates[...], jnp.zeros_like(rates)], axis=0)


def select(hours, sky, rates):
    out = jax.ShapeDtypeStruct((MESSAGE, HALF), jnp.float32)
    return in_vmem(select_kernel, out, [], "select", 4, (hours, sky, rates))


def render_kernel(
    core, order, sky, rates, own, other, up, down, keep_up, keep_down, mine, images, peaks, ordered
):
    step = pl.program_id(0)

    @pl.when(step == 0)
    def _():
        hour = lax.broadcasted_iota(jnp.int32, (HOURS, HOURS), 1)
        chosen = jnp.where(order[...] == hour, 1.0, 0.0).astype(jnp.bfloat16)
        sorted_sky = jnp.dot(chosen, sky[...], preferred_element_type=jnp.float32)
        ordered[...] = sorted_sky.astype(jnp.bfloat16)
        peaks[...] = jnp.zeros_like(peaks)

    patches = jnp.concatenate([own[...], other[...]], axis=0)
    by_row = jnp.swapaxes(patches, 0, 1)
    rows_seen = ordered[...]
    peak = jnp.zeros((HOURS, HALF), jnp.float32)
    for row in range(BLOCK):
        image = jnp.dot(rows_seen, by_row[row], preferred_element_type=jnp.float32)
        peak = jnp.maximum(peak, jnp.abs(image))
        images[lines_at(step * BLOCK + row, HOURS), :] = image
        mine[lines_at(step * BLOCK + row, GROUP), :] = image[:GROUP]
    half = step // (PIECE // BLOCK // 2)
    peaks[half] = jnp.maximum(peaks[half], peak)

    @pl.when(step == pl.num_programs(0) - 1)
    def _():
        for out, parts in ((up, ((2, 0), (1, 1))), (down, ((2, 1), (3, 0)))):
            levels = []
            for index, (group, half) in enumerate(parts):
                hours = slice(group * GROUP, (group + 1) * GROUP)
                level = level_of(peaks[half, hours, :])
                factor = factor_of(level)
                levels.append(level)
                first = half * (PIECE // 2)

                def pair_step(pair, carry):
                    for k in range(2):
                        start = (first + 2 * pair + k) * HOURS + group * GROUP
                        start = pl.multiple_of(start, GROUP)
                        tile = images[pl.ds(start, GROUP), :] * factor
                        carry = carry + (jnp.round(tile).astype(jnp.int32),)
                    at = pl.multiple_of(index * PART + pair * PAIR, PAIR)
                    out[pl.ds(at, PAIR), :] = jnp.concatenate(carry, axis=0).astype(jnp.int16)
                    return ()

                lax.fori_loop(0, PIECE // 4, pair_step, (), unroll=2)
            pad = jnp.zeros((8, HALF), jnp.float32)
            last = jnp.concatenate(levels + [digits(rates[...]), pad], axis=0)
            out[2 * PART :, :] = narrow(last)
        for out, group, half in ((keep_up, 1, 0), (keep_down, 3, 1)):

            def keep_step(row, carry):
                start = (half * (PIECE // 2) + row) * HOURS + group * GROUP
                out[lines_at(row, GROUP), :] = images[pl.ds(pl.multiple_of(start, GROUP), GROUP), :]
                return carry

            lax.fori_loop(0, PIECE // 2, keep_step, 0, unroll=4)


def render(piece, core, order, sky, rates, own, other):
    whole = lambda i, core: (0, 0)
    steps = PIECE // BLOCK
    sent = jax.ShapeDtypeStruct((SENT, HALF), jnp.int16)
    kept = jax.ShapeDtypeStruct((PART, HALF), jnp.float32)
    outs = [sent, sent, kept, kept, jax.ShapeDtypeStruct((2 * PART, HALF), jnp.float32)]
    return pl.pallas_call(
        render_kernel,
        grid_spec=pltpu.PrefetchScalarGridSpec(
            num_scalar_prefetch=1,
            grid=(steps,),
            in_specs=[
                pl.BlockSpec((HOURS, 1), whole),
                pl.BlockSpec((HOURS, PATCHES), whole),
                pl.BlockSpec((CHIP_ROWS, HALF), whole),
                pl.BlockSpec(
                    (None, PATCHES // 2, BLOCK, HALF),
                    lambda i, core: (0, 0, piece * steps + i, core[0]),
                ),
                pl.BlockSpec((PATCHES // 2, BLOCK, HALF), lambda i, core: (0, i, 0)),
            ],
            out_specs=[pl.BlockSpec(out.shape, whole) for out in outs],
            scratch_shapes=[
                pltpu.VMEM((HOURS * PIECE, HALF), jnp.float32),
                pltpu.VMEM((2, HOURS, HALF), jnp.float32),
                pltpu.VMEM((HOURS, PATCHES), jnp.bfloat16),
            ],
        ),
        out_shape=outs,
        compiler_params=pltpu.CompilerParams(vmem_limit_bytes=24 * 2**20),
        cost_estimate=pl.CostEstimate(
            flops=2 * PATCHES * HOURS * PIECE * HALF, bytes_accessed=18 * 2**20, transcendentals=0
        ),
        name="render",
    )(core, order, sky, rates, own, other)


def in_vmem(kernel, outs, scratch, name, cost, operands, scalars=0):
    spaces = [pltpu.SMEM] * scalars + [pltpu.VMEM] * (len(operands) - scalars)
    return pl.pallas_call(
        kernel,
        out_shape=outs,
        in_specs=[pl.BlockSpec(memory_space=space) for space in spaces],
        out_specs=jax.tree.map(lambda out: pl.BlockSpec(memory_space=pltpu.VMEM), outs),
        scratch_shapes=scratch,
        compiler_params=pltpu.CompilerParams(vmem_limit_bytes=12 * 2**20),
        cost_estimate=pl.CostEstimate(flops=0, bytes_accessed=cost * 2**20, transcendentals=0),
        name=name,
    )(*operands)


def merge_kernel(keep_up, keep_down, got_up, got_down, up, down, total):
    nothing = jnp.zeros((PAIR, HALF), jnp.float32)
    for keep, got, out in ((keep_up, got_up, up), (keep_down, got_down, down)):
        last = wide(got[2 * PART :, :])
        unit = twice(unit_of(last[:GROUP]))

        def add_step(pair, peak):
            at = lines_at(pair, PAIR)
            tile = keep[at, :] + wide(got[at, :]) * unit
            total[at, :] = tile
            return jnp.maximum(peak, jnp.abs(tile))

        peak = lax.fori_loop(0, PART // PAIR, add_step, nothing, unroll=2)
        level = level_of(jnp.maximum(peak[:GROUP], peak[GROUP:]))
        factor = twice(factor_of(level))

        def code_step(pair, carry):
            at = lines_at(pair, PAIR)
            out[at, :] = coded(total[at, :], factor)
            return carry

        lax.fori_loop(0, PART // PAIR, code_step, 0, unroll=2)
        out[PART:, :] = narrow(jnp.concatenate([level, last[PAIR : PAIR + RATES]], axis=0))


def merge(keep_up, keep_down, got_up, got_down):
    sent = jax.ShapeDtypeStruct((PART + GROUP + RATES, HALF), jnp.int16)
    scratch = [pltpu.VMEM((PART, HALF), jnp.float32)]
    return in_vmem(
        merge_kernel, [sent, sent], scratch, "merge", 5, (keep_up, keep_down, got_up, got_down)
    )


def join_kernel(piece, *refs):
    if piece:
        (mine, got_up, got_down, up, down), refs = refs[:5], refs[5:]
        earlier, (near, far, back, own, total) = refs[:3], refs[3:]
        for out, before in zip((near, far, back), earlier):
            out[: before.shape[0], :] = before[...]
    else:
        rates, mine, got_up, got_down, up, down, near, far, back, own, own_rates, total = refs
    peak = jnp.zeros((PAIR, HALF), jnp.float32)
    for half, (direct, relayed) in enumerate(((got_down, up), (got_up, down))):
        direct_unit = twice(unit_of(wide(direct[2 * PART :, :])[GROUP:PAIR]))
        relayed_unit = twice(unit_of(wide(relayed[PART:, :])[:GROUP]))

        def add_step(pair, peak):
            at = lines_at(pair, PAIR)
            direct_at = pl.ds(pl.multiple_of(PART + pair * PAIR, PAIR), PAIR)
            out_at = pl.ds(pl.multiple_of(half * PART + pair * PAIR, PAIR), PAIR)
            tile = mine[out_at, :] + wide(direct[direct_at, :]) * direct_unit
            tile = tile + wide(relayed[at, :]) * relayed_unit
            total[out_at, :] = tile
            return jnp.maximum(peak, jnp.abs(tile))

        peak = lax.fori_loop(0, PART // PAIR, add_step, peak, unroll=2)
    level = level_of(jnp.maximum(peak[:GROUP], peak[GROUP:]))
    factor = factor_of(level)
    outs = (own, near, far, back)
    factors = [
        jnp.concatenate([factor[part * FINAL : (part + 1) * FINAL]] * 8, axis=0)
        for part in range(SIDE)
    ]

    first = earlier[0].shape[0] if piece else 0

    def split_step(eight, carry):
        tile = total[lines_at(eight, 8 * GROUP), :]
        for part, out in enumerate(outs):
            starts = [k * GROUP + part * FINAL for k in range(8)]
            block = jnp.concatenate([tile[at : at + FINAL] for at in starts], axis=0)
            if part:
                at = pl.ds(pl.multiple_of(first + eight * 8 * FINAL, 16), 8 * FINAL)
                out[at, :] = coded(block, factors[part])
            else:
                out[lines_at(eight, 8 * FINAL), :] = block
        return carry

    lax.fori_loop(0, PIECE // 8, split_step, 0)
    first = first + PIECE * FINAL
    for part, out in enumerate(outs):
        if part:
            mark = level[part * FINAL : (part + 1) * FINAL]
            rest = jnp.zeros((16 - FINAL, HALF), jnp.float32)
            out[first : first + 16, :] = narrow(jnp.concatenate([mark, rest], axis=0))
    if not piece:
        places = ((got_up, 2 * PART, PAIR), (up, PART, GROUP), (got_down, 2 * PART, PAIR))
        ahead = [wide(got[start:, :])[at : at + RATES] for got, start, at in places]
        all_rates = narrow(jnp.concatenate([digits(rates[...])] + ahead, axis=0))
        for out in (near, far, back):
            out[first + 16 :, :] = all_rates
        own_rates[...] = all_rates


def join(piece, rates, mine, got_up, got_down, up, down, earlier):
    size = PIECE * FINAL + 16
    sent = jax.ShapeDtypeStruct((PIECES * size + SIDE * RATES if piece else FIRST, HALF), jnp.int16)
    outs = [sent] * 3 + [jax.ShapeDtypeStruct((PIECE * FINAL, HALF), jnp.float32)]
    operands = (mine, got_up, got_down, up, down)
    if piece:
        operands = operands + tuple(earlier)
    else:
        operands = (rates,) + operands
        outs = outs + [jax.ShapeDtypeStruct((SIDE * RATES, HALF), jnp.int16)]
    scratch = [pltpu.VMEM((2 * PART, HALF), jnp.float32)]
    return in_vmem(functools.partial(join_kernel, piece), outs, scratch, "join", 6, operands)


def glare_kernel(chips, own_rates, near, far, back, mine, later, out, lines, front, rates):
    gots = (near, far, back)
    size = PIECE * FINAL
    for behind, block in enumerate((own_rates, *[got.at[size + 16 : FIRST] for got in gots])):
        coded_rates = wide(block[...])
        for chip in range(SIDE):
            start = (behind * SIDE + chip) * CHIP_ROWS
            rates[start : start + CHIP_ROWS, :] = undigits(
                coded_rates[chip * RATES : (chip + 1) * RATES]
            )
    eights = PIECE // 8
    lines[0:16, :] = jnp.zeros((16, HALF), jnp.float32)
    lines[8 * (ROWS + 2) :, :] = jnp.zeros((16, HALF), jnp.float32)
    state = jnp.zeros((FINAL, HALF), jnp.float32)
    nothing = state

    def spots(eight, k):
        return pl.ds(pl.multiple_of(64 * eight, 64) + 8 * k, FINAL)

    for piece, (first, own) in enumerate(((0, mine), (FIRST, later))):
        marks = slice(first + size, first + size + 16)
        units = [unit_of(wide(got[marks, :])[:FINAL]) for got in gots]
        units = [jnp.concatenate([unit] * 8, axis=0) for unit in units]

        def down(index, state):
            eight = piece * eights + index
            at = pl.ds(pl.multiple_of(first + index * 8 * FINAL, 16), 8 * FINAL)
            tile = own[lines_at(index, 8 * FINAL), :]
            for got, unit in zip(gots, units):
                tile = tile + wide(got[at, :]) * unit
            share = rates[lines_at(chips[eight], 8), :]
            for k in range(8):
                light = tile[k * FINAL : (k + 1) * FINAL]
                state = share[k : k + 1] * state + light
                lines[spots(eight, k + 2), :] = light
                front[spots(eight, k), :] = state
            return state

        state = lax.fori_loop(0, eights, down, state)

    def up(step, state):
        eight = ROWS // 8 - 1 - step
        share = rates[lines_at(chips[eight], 8), :]
        light = [lines[spots(eight, k), :] for k in range(12)]
        for owner in (1, 0):
            veils, blurs = [None] * 4, [None] * 4
            for k in (3, 2, 1, 0):
                row = owner * 4 + k
                state = share[row : row + 1] * state + light[row + 2]
                veils[k] = 0.125 * (front[spots(eight, row), :] + state)
                near, wider = light[row + 1] + light[row + 3], light[row] + light[row + 4]
                blurs[k] = taps[2] * light[row + 2] + taps[1] * near + taps[0] * wider
            blocks, levels = [], []
            for values in (blurs, veils):
                block = jnp.concatenate(values, axis=0)
                level = level_of(jnp.max(jnp.abs(block), axis=0, keepdims=True))
                blocks.append(jnp.round(block * factor_of(level)))
                levels.append(level)
            rest = jnp.zeros((CHUNK - 8 * FINAL - 2, HALF), jnp.float32)
            out[2 * eight + owner] = narrow(jnp.concatenate(blocks + levels + [rest], axis=0))
        return state

    lax.fori_loop(0, ROWS // 8, up, nothing)


def glare(chips, *operands):
    out = jax.ShapeDtypeStruct((32, CHUNK, HALF), jnp.int16)
    scratch = [
        pltpu.VMEM((8 * (ROWS + 4), HALF), jnp.float32),
        pltpu.VMEM((8 * ROWS, HALF), jnp.float32),
        pltpu.VMEM((ROWS, HALF), jnp.float32),
    ]
    return in_vmem(glare_kernel, out, scratch, "glare", 8, (chips, *operands), scalars=1)


def finish_kernel(parts, acuity, veil, blurred):
    for source in range(32):
        x, y, core = source // 8, source // 2 % 4, source % 2
        first, second = (x, y) if core == 0 else (y, x)
        hour = first * GROUP + second * FINAL
        columns = slice(core * HALF, (core + 1) * HALF)
        block = wide(parts[source])
        units = unit_of(block[8 * FINAL : 8 * FINAL + 2])
        for row in range(4):
            at = row * FINAL
            blurred[row, hour : hour + FINAL, columns] = block[at : at + FINAL] * units[0:1]
            at = (row + 4) * FINAL
            veil[row, 0, hour : hour + FINAL, columns] = block[at : at + FINAL] * units[1:2]
    column = lax.broadcasted_iota(jnp.int32, (HOURS, 2 * HALF), 1)
    for row in range(4):
        image = blurred[row]
        total = taps[2] * image
        for offset in (-2, -1, 1, 2):
            moved = pltpu.roll(image, (-offset) % (2 * HALF), 1)
            inside = (column + offset >= 0) & (column + offset < 2 * HALF)
            total = total + taps[2 + offset] * jnp.where(inside, moved, 0.0)
        acuity[row, 0] = total


def finish(parts):
    shape = jax.ShapeDtypeStruct((4, 1, HOURS, 2 * HALF), jnp.float32)
    scratch = [pltpu.VMEM((4, HOURS, 2 * HALF), jnp.float32)]
    return in_vmem(finish_kernel, [shape, shape], scratch, "finish", 4, (parts,))


def hour_order(first, second):
    steps = jnp.arange(HOURS, dtype=jnp.int32)
    group, part, inner = steps // GROUP, steps // FINAL % SIDE, steps % FINAL
    return (first + group) % SIDE * GROUP + (second + part) % SIDE * FINAL + inner


def shards(coefficients, sky_year, hour_list, retention):
    me = lax.axis_index("patch")
    x, y, core = me // (2 * SIDE), me // 2 % SIDE, me % 2
    first, second = jnp.where(core == 0, x, y), jnp.where(core == 0, y, x)
    move = lambda value, pairs: lax.ppermute(value, "patch", pairs)
    first_up, first_down = ring(1, False), ring(-1, False)

    chip = jnp.arange(SIDE * SIDE, dtype=jnp.int32)
    one, two = chip // SIDE, chip % SIDE
    chips = jnp.where(
        core == 0,
        (x - one) % SIDE + SIDE * ((y - two) % SIDE),
        (y - two) % SIDE + SIDE * ((x - one) % SIDE),
    )

    spot = core.reshape(1)
    coefficients = pltpu.with_memory_space_constraint(coefficients, pltpu.HBM)
    others = [move(split(piece, spot, coefficients), siblings) for piece in range(PIECES)]
    own_rates = lax.dynamic_slice(retention, (0, core * HALF), (4, HALF))
    their_rates = lax.dynamic_slice(retention, (0, (1 - core) * HALF), (4, HALF))
    chosen = select(hour_list[:, None], sky_year, their_rates)
    got = move(chosen, siblings)
    sky = [message[:HOURS, : PATCHES // 2] for message in (chosen, got)]
    sky = jnp.concatenate(sky, axis=1).astype(jnp.bfloat16)
    sibling_rates = got[HOURS : HOURS + 4]
    rates = jnp.where(
        core == 0,
        jnp.concatenate([own_rates, sibling_rates]),
        jnp.concatenate([sibling_rates, own_rates]),
    )
    order = hour_order(first, second)[:, None]

    rendered = []
    for piece in range(PIECES):
        up, down, *kept = render(piece, spot, order, sky, rates, coefficients, others[piece])
        rendered.append((move(up, first_up), move(down, first_down), *kept))
    merged = []
    for up, down, keep_up, keep_down, mine in rendered:
        relay_up, relay_down = merge(keep_up, keep_down, up, down)
        merged.append((mine, up, down, move(relay_up, first_up), move(relay_down, first_down)))
    *sent, mine, coded_rates = join(0, rates, *merged[0], None)
    *sent, later = join(1, rates, *merged[1], sent)
    got = [move(part, ring(hop, True)) for hop, part in zip((1, 2, 3), sent)]
    parts = glare(chips, coded_rates, *got, mine, later)
    parts = lax.all_to_all(parts, "patch", 0, 0, tiled=True)
    return tuple(finish(parts))


def solution(mesh):
    placed = (P("view", "patch", None, None), P("patch", None), P(), P("patch", None))
    return jax.shard_map(
        shards,
        mesh=mesh,
        in_specs=placed,
        out_specs=(P("patch", "view", None, None), P("patch", "view", None, None)),
        check_vma=False,
    )
```

```python
import functools

import jax
import jax.numpy as jnp
from jax import lax
from jax.experimental import pallas as pl
from jax.experimental.pallas import tpu as pltpu
from jax.sharding import PartitionSpec as P

taps = (0.0625, 0.25, 0.375, 0.25, 0.0625)

SIDE = 4
ROWS = 128
HALF = 256
HOURS = 96
GROUP = HOURS // SIDE
FINAL = GROUP // SIDE
PATCHES = 144
BLOCK = 16
PIECES = 2
PIECE = ROWS // PIECES
PART = PIECE // 2 * GROUP
PAIR = 2 * GROUP
STEPS = 64.0
TOP = 32752.0
FLOOR = 2.0**-100
CHUNK = 56
CHIP_ROWS = 8
RATES = 3 * CHIP_ROWS
SENT = 2 * PART + PAIR + RATES + 8
FIRST = PIECE * FINAL + 16 + 4 * RATES
MESSAGE = 104


def place(x, y, core):
    return ((x % SIDE) * SIDE + y % SIDE) * 2 + core


def ring(hop, second):
    pairs = []
    for x in range(SIDE):
        for y in range(SIDE):
            for core in range(2):
                along_x = (core == 0) != second
                target = place(x + hop, y, core) if along_x else place(x, y + hop, core)
                pairs.append((place(x, y, core), target))
    return pairs


siblings = [(i, i ^ 1) for i in range(2 * SIDE * SIDE)]


def level_of(biggest):
    return jnp.ceil(STEPS * jnp.log2(jnp.maximum(biggest, FLOOR)))


def factor_of(level):
    return TOP * jnp.exp2(level * (-1.0 / STEPS))


def unit_of(level):
    return jnp.exp2(level * (1.0 / STEPS)) * (1.0 / TOP)


def coded(values, factor):
    return jnp.round(values * factor).astype(jnp.int32).astype(jnp.int16)


def wide(block):
    return block.astype(jnp.int32).astype(jnp.float32)


def narrow(block):
    return block.astype(jnp.int32).astype(jnp.int16)


def digits(rates):
    rest, parts = rates, []
    for _ in range(3):
        rest = rest * 32768.0
        part = jnp.minimum(jnp.floor(rest), 32767.0)
        rest = rest - part
        parts.append(part)
    return jnp.concatenate(parts, axis=0)


def undigits(lines):
    first, second, third = [lines[k * CHIP_ROWS : (k + 1) * CHIP_ROWS] for k in range(3)]
    return (first + (second + third * 2.0**-15) * 2.0**-15) * 2.0**-15


def twice(block):
    return jnp.concatenate([block, block], axis=0)


def lines_at(index, count):
    return pl.ds(pl.multiple_of(index * count, count), count)


def split_kernel(piece, core, source, out, sems):
    columns = pl.ds(pl.multiple_of((1 - core[0]) * HALF, HALF), HALF)
    copies = []
    for index in range(8):
        patches = pl.ds(index * (PATCHES // 16), PATCHES // 16)
        part = source.at[0, patches, pl.ds(piece * PIECE, PIECE), columns]
        copies.append(pltpu.make_async_copy(part, out.at[patches], sems.at[index]))
    for copy in copies:
        copy.start()
    for copy in copies:
        copy.wait()


def split(piece, core, coefficients):
    return pl.pallas_call(
        functools.partial(split_kernel, piece),
        out_shape=pltpu.VMEM((PATCHES // 2, PIECE, HALF), jnp.bfloat16),
        in_specs=[pl.BlockSpec(memory_space=pltpu.SMEM), pl.BlockSpec(memory_space=pl.ANY)],
        out_specs=pl.BlockSpec(memory_space=pltpu.VMEM),
        scratch_shapes=[pltpu.SemaphoreType.DMA((8,))],
        compiler_params=pltpu.CompilerParams(vmem_limit_bytes=8 * 2**20),
        cost_estimate=pl.CostEstimate(flops=0, bytes_accessed=5 * 2**20, transcendentals=0),
        name="split",
    )(core, coefficients)


def select_kernel(hours, sky, rates, out):
    hour = lax.broadcasted_iota(jnp.int32, (HOURS, sky.shape[1]), 1)
    chosen = jnp.where(hours[...] == hour, 1.0, 0.0).astype(jnp.bfloat16)
    out[0:HOURS, 0 : PATCHES // 2] = lax.dot_general(
        chosen, sky[...], (((1,), (1,)), ((), ())), preferred_element_type=jnp.float32
    )
    out[0:HOURS, PATCHES // 2 :] = jnp.zeros((HOURS, HALF - PATCHES // 2), jnp.float32)
    out[HOURS:, :] = jnp.concatenate([rates[...], jnp.zeros_like(rates)], axis=0)


def select(hours, sky, rates):
    out = jax.ShapeDtypeStruct((MESSAGE, HALF), jnp.float32)
    return in_vmem(select_kernel, out, [], "select", 4, (hours, sky, rates))


def render_kernel(
    core, order, sky, rates, own, other, up, down, keep_up, keep_down, mine, images, peaks, ordered
):
    step = pl.program_id(0)

    @pl.when(step == 0)
    def _():
        hour = lax.broadcasted_iota(jnp.int32, (HOURS, HOURS), 1)
        chosen = jnp.where(order[...] == hour, 1.0, 0.0).astype(jnp.bfloat16)
        sorted_sky = jnp.dot(chosen, sky[...], preferred_element_type=jnp.float32)
        ordered[...] = sorted_sky.astype(jnp.bfloat16)
        peaks[...] = jnp.zeros_like(peaks)

    patches = jnp.concatenate([own[...], other[...]], axis=0)
    by_row = jnp.swapaxes(patches, 0, 1)
    rows_seen = ordered[...]
    peak = jnp.zeros((HOURS, HALF), jnp.float32)
    for row in range(BLOCK):
        image = jnp.dot(rows_seen, by_row[row], preferred_element_type=jnp.float32)
        peak = jnp.maximum(peak, jnp.abs(image))
        images[lines_at(step * BLOCK + row, HOURS), :] = image
        mine[lines_at(step * BLOCK + row, GROUP), :] = image[:GROUP]
    half = step // (PIECE // BLOCK // 2)
    peaks[half] = jnp.maximum(peaks[half], peak)

    @pl.when(step == pl.num_programs(0) - 1)
    def _():
        for out, parts in ((up, ((2, 0), (1, 1))), (down, ((2, 1), (3, 0)))):
            levels = []
            for index, (group, half) in enumerate(parts):
                hours = slice(group * GROUP, (group + 1) * GROUP)
                level = level_of(peaks[half, hours, :])
                factor = factor_of(level)
                levels.append(level)
                first = half * (PIECE // 2)

                def pair_step(pair, carry):
                    for k in range(2):
                        start = (first + 2 * pair + k) * HOURS + group * GROUP
                        start = pl.multiple_of(start, GROUP)
                        tile = images[pl.ds(start, GROUP), :] * factor
                        carry = carry + (jnp.round(tile).astype(jnp.int32),)
                    at = pl.multiple_of(index * PART + pair * PAIR, PAIR)
                    out[pl.ds(at, PAIR), :] = jnp.concatenate(carry, axis=0).astype(jnp.int16)
                    return ()

                lax.fori_loop(0, PIECE // 4, pair_step, (), unroll=2)
            pad = jnp.zeros((8, HALF), jnp.float32)
            last = jnp.concatenate(levels + [digits(rates[...]), pad], axis=0)
            out[2 * PART :, :] = narrow(last)
        for out, group, half in ((keep_up, 1, 0), (keep_down, 3, 1)):

            def keep_step(row, carry):
                start = (half * (PIECE // 2) + row) * HOURS + group * GROUP
                out[lines_at(row, GROUP), :] = images[pl.ds(pl.multiple_of(start, GROUP), GROUP), :]
                return carry

            lax.fori_loop(0, PIECE // 2, keep_step, 0, unroll=4)


def render(piece, core, order, sky, rates, own, other):
    whole = lambda i, core: (0, 0)
    steps = PIECE // BLOCK
    sent = jax.ShapeDtypeStruct((SENT, HALF), jnp.int16)
    kept = jax.ShapeDtypeStruct((PART, HALF), jnp.float32)
    outs = [sent, sent, kept, kept, jax.ShapeDtypeStruct((2 * PART, HALF), jnp.float32)]
    return pl.pallas_call(
        render_kernel,
        grid_spec=pltpu.PrefetchScalarGridSpec(
            num_scalar_prefetch=1,
            grid=(steps,),
            in_specs=[
                pl.BlockSpec((HOURS, 1), whole),
                pl.BlockSpec((HOURS, PATCHES), whole),
                pl.BlockSpec((CHIP_ROWS, HALF), whole),
                pl.BlockSpec(
                    (None, PATCHES // 2, BLOCK, HALF),
                    lambda i, core: (0, 0, piece * steps + i, core[0]),
                ),
                pl.BlockSpec((PATCHES // 2, BLOCK, HALF), lambda i, core: (0, i, 0)),
            ],
            out_specs=[pl.BlockSpec(out.shape, whole) for out in outs],
            scratch_shapes=[
                pltpu.VMEM((HOURS * PIECE, HALF), jnp.float32),
                pltpu.VMEM((2, HOURS, HALF), jnp.float32),
                pltpu.VMEM((HOURS, PATCHES), jnp.bfloat16),
            ],
        ),
        out_shape=outs,
        compiler_params=pltpu.CompilerParams(vmem_limit_bytes=24 * 2**20),
        cost_estimate=pl.CostEstimate(
            flops=2 * PATCHES * HOURS * PIECE * HALF, bytes_accessed=18 * 2**20, transcendentals=0
        ),
        name="render",
    )(core, order, sky, rates, own, other)


def in_vmem(kernel, outs, scratch, name, cost, operands, scalars=0):
    spaces = [pltpu.SMEM] * scalars + [pltpu.VMEM] * (len(operands) - scalars)
    return pl.pallas_call(
        kernel,
        out_shape=outs,
        in_specs=[pl.BlockSpec(memory_space=space) for space in spaces],
        out_specs=jax.tree.map(lambda out: pl.BlockSpec(memory_space=pltpu.VMEM), outs),
        scratch_shapes=scratch,
        compiler_params=pltpu.CompilerParams(vmem_limit_bytes=12 * 2**20),
        cost_estimate=pl.CostEstimate(flops=0, bytes_accessed=cost * 2**20, transcendentals=0),
        name=name,
    )(*operands)


def merge_kernel(keep_up, keep_down, got_up, got_down, up, down, total):
    nothing = jnp.zeros((PAIR, HALF), jnp.float32)
    for keep, got, out in ((keep_up, got_up, up), (keep_down, got_down, down)):
        last = wide(got[2 * PART :, :])
        unit = twice(unit_of(last[:GROUP]))

        def add_step(pair, peak):
            at = lines_at(pair, PAIR)
            tile = keep[at, :] + wide(got[at, :]) * unit
            total[at, :] = tile
            return jnp.maximum(peak, jnp.abs(tile))

        peak = lax.fori_loop(0, PART // PAIR, add_step, nothing, unroll=2)
        level = level_of(jnp.maximum(peak[:GROUP], peak[GROUP:]))
        factor = twice(factor_of(level))

        def code_step(pair, carry):
            at = lines_at(pair, PAIR)
            out[at, :] = coded(total[at, :], factor)
            return carry

        lax.fori_loop(0, PART // PAIR, code_step, 0, unroll=2)
        out[PART:, :] = narrow(jnp.concatenate([level, last[PAIR : PAIR + RATES]], axis=0))


def merge(keep_up, keep_down, got_up, got_down):
    sent = jax.ShapeDtypeStruct((PART + GROUP + RATES, HALF), jnp.int16)
    scratch = [pltpu.VMEM((PART, HALF), jnp.float32)]
    return in_vmem(
        merge_kernel, [sent, sent], scratch, "merge", 5, (keep_up, keep_down, got_up, got_down)
    )


def join_kernel(piece, *refs):
    if piece:
        (mine, got_up, got_down, up, down), refs = refs[:5], refs[5:]
        earlier, (near, far, back, own, total) = refs[:3], refs[3:]
        for out, before in zip((near, far, back), earlier):
            out[: before.shape[0], :] = before[...]
    else:
        rates, mine, got_up, got_down, up, down, near, far, back, own, own_rates, total = refs
    peak = jnp.zeros((PAIR, HALF), jnp.float32)
    for half, (direct, relayed) in enumerate(((got_down, up), (got_up, down))):
        direct_unit = twice(unit_of(wide(direct[2 * PART :, :])[GROUP:PAIR]))
        relayed_unit = twice(unit_of(wide(relayed[PART:, :])[:GROUP]))

        def add_step(pair, peak):
            at = lines_at(pair, PAIR)
            direct_at = pl.ds(pl.multiple_of(PART + pair * PAIR, PAIR), PAIR)
            out_at = pl.ds(pl.multiple_of(half * PART + pair * PAIR, PAIR), PAIR)
            tile = mine[out_at, :] + wide(direct[direct_at, :]) * direct_unit
            tile = tile + wide(relayed[at, :]) * relayed_unit
            total[out_at, :] = tile
            return jnp.maximum(peak, jnp.abs(tile))

        peak = lax.fori_loop(0, PART // PAIR, add_step, peak, unroll=2)
    level = level_of(jnp.maximum(peak[:GROUP], peak[GROUP:]))
    factor = factor_of(level)
    outs = (own, near, far, back)
    factors = [
        jnp.concatenate([factor[part * FINAL : (part + 1) * FINAL]] * 8, axis=0)
        for part in range(SIDE)
    ]

    first = earlier[0].shape[0] if piece else 0

    def split_step(eight, carry):
        tile = total[lines_at(eight, 8 * GROUP), :]
        for part, out in enumerate(outs):
            starts = [k * GROUP + part * FINAL for k in range(8)]
            block = jnp.concatenate([tile[at : at + FINAL] for at in starts], axis=0)
            if part:
                at = pl.ds(pl.multiple_of(first + eight * 8 * FINAL, 16), 8 * FINAL)
                out[at, :] = coded(block, factors[part])
            else:
                out[lines_at(eight, 8 * FINAL), :] = block
        return carry

    lax.fori_loop(0, PIECE // 8, split_step, 0)
    first = first + PIECE * FINAL
    for part, out in enumerate(outs):
        if part:
            mark = level[part * FINAL : (part + 1) * FINAL]
            rest = jnp.zeros((16 - FINAL, HALF), jnp.float32)
            out[first : first + 16, :] = narrow(jnp.concatenate([mark, rest], axis=0))
    if not piece:
        places = ((got_up, 2 * PART, PAIR), (up, PART, GROUP), (got_down, 2 * PART, PAIR))
        ahead = [wide(got[start:, :])[at : at + RATES] for got, start, at in places]
        all_rates = narrow(jnp.concatenate([digits(rates[...])] + ahead, axis=0))
        for out in (near, far, back):
            out[first + 16 :, :] = all_rates
        own_rates[...] = all_rates


def join(piece, rates, mine, got_up, got_down, up, down, earlier):
    size = PIECE * FINAL + 16
    sent = jax.ShapeDtypeStruct((PIECES * size + SIDE * RATES if piece else FIRST, HALF), jnp.int16)
    outs = [sent] * 3 + [jax.ShapeDtypeStruct((PIECE * FINAL, HALF), jnp.float32)]
    operands = (mine, got_up, got_down, up, down)
    if piece:
        operands = operands + tuple(earlier)
    else:
        operands = (rates,) + operands
        outs = outs + [jax.ShapeDtypeStruct((SIDE * RATES, HALF), jnp.int16)]
    scratch = [pltpu.VMEM((2 * PART, HALF), jnp.float32)]
    return in_vmem(functools.partial(join_kernel, piece), outs, scratch, "join", 6, operands)


def glare_kernel(chips, own_rates, near, far, back, mine, later, out, lines, front, rates):
    gots = (near, far, back)
    size = PIECE * FINAL
    for behind, block in enumerate((own_rates, *[got.at[size + 16 : FIRST] for got in gots])):
        coded_rates = wide(block[...])
        for chip in range(SIDE):
            start = (behind * SIDE + chip) * CHIP_ROWS
            rates[start : start + CHIP_ROWS, :] = undigits(
                coded_rates[chip * RATES : (chip + 1) * RATES]
            )
    eights = PIECE // 8
    lines[0:16, :] = jnp.zeros((16, HALF), jnp.float32)
    lines[8 * (ROWS + 2) :, :] = jnp.zeros((16, HALF), jnp.float32)
    state = jnp.zeros((FINAL, HALF), jnp.float32)
    nothing = state

    def spots(eight, k):
        return pl.ds(pl.multiple_of(64 * eight, 64) + 8 * k, FINAL)

    for piece, (first, own) in enumerate(((0, mine), (FIRST, later))):
        marks = slice(first + size, first + size + 16)
        units = [unit_of(wide(got[marks, :])[:FINAL]) for got in gots]
        units = [jnp.concatenate([unit] * 8, axis=0) for unit in units]

        def down(index, state):
            eight = piece * eights + index
            at = pl.ds(pl.multiple_of(first + index * 8 * FINAL, 16), 8 * FINAL)
            tile = own[lines_at(index, 8 * FINAL), :]
            for got, unit in zip(gots, units):
                tile = tile + wide(got[at, :]) * unit
            share = rates[lines_at(chips[eight], 8), :]
            for k in range(8):
                light = tile[k * FINAL : (k + 1) * FINAL]
                state = share[k : k + 1] * state + light
                lines[spots(eight, k + 2), :] = light
                front[spots(eight, k), :] = state
            return state

        state = lax.fori_loop(0, eights, down, state)

    def up(step, state):
        eight = ROWS // 8 - 1 - step
        share = rates[lines_at(chips[eight], 8), :]
        light = [lines[spots(eight, k), :] for k in range(12)]
        for owner in (1, 0):
            veils, blurs = [None] * 4, [None] * 4
            for k in (3, 2, 1, 0):
                row = owner * 4 + k
                state = share[row : row + 1] * state + light[row + 2]
                veils[k] = 0.125 * (front[spots(eight, row), :] + state)
                near, wider = light[row + 1] + light[row + 3], light[row] + light[row + 4]
                blurs[k] = taps[2] * light[row + 2] + taps[1] * near + taps[0] * wider
            blocks, levels = [], []
            for values in (blurs, veils):
                block = jnp.concatenate(values, axis=0)
                level = level_of(jnp.max(jnp.abs(block), axis=0, keepdims=True))
                blocks.append(jnp.round(block * factor_of(level)))
                levels.append(level)
            rest = jnp.zeros((CHUNK - 8 * FINAL - 2, HALF), jnp.float32)
            out[2 * eight + owner] = narrow(jnp.concatenate(blocks + levels + [rest], axis=0))
        return state

    lax.fori_loop(0, ROWS // 8, up, nothing)


def glare(chips, *operands):
    out = jax.ShapeDtypeStruct((32, CHUNK, HALF), jnp.int16)
    scratch = [
        pltpu.VMEM((8 * (ROWS + 4), HALF), jnp.float32),
        pltpu.VMEM((8 * ROWS, HALF), jnp.float32),
        pltpu.VMEM((ROWS, HALF), jnp.float32),
    ]
    return in_vmem(glare_kernel, out, scratch, "glare", 8, (chips, *operands), scalars=1)


def finish_kernel(parts, acuity, veil, blurred):
    for source in range(32):
        x, y, core = source // 8, source // 2 % 4, source % 2
        first, second = (x, y) if core == 0 else (y, x)
        hour = first * GROUP + second * FINAL
        columns = slice(core * HALF, (core + 1) * HALF)
        block = wide(parts[source])
        units = unit_of(block[8 * FINAL : 8 * FINAL + 2])
        for row in range(4):
            at = row * FINAL
            blurred[row, hour : hour + FINAL, columns] = block[at : at + FINAL] * units[0:1]
            at = (row + 4) * FINAL
            veil[row, 0, hour : hour + FINAL, columns] = block[at : at + FINAL] * units[1:2]
    column = lax.broadcasted_iota(jnp.int32, (HOURS, 2 * HALF), 1)
    for row in range(4):
        image = blurred[row]
        total = taps[2] * image
        for offset in (-2, -1, 1, 2):
            moved = pltpu.roll(image, (-offset) % (2 * HALF), 1)
            inside = (column + offset >= 0) & (column + offset < 2 * HALF)
            total = total + taps[2 + offset] * jnp.where(inside, moved, 0.0)
        acuity[row, 0] = total


def finish(parts):
    shape = jax.ShapeDtypeStruct((4, 1, HOURS, 2 * HALF), jnp.float32)
    scratch = [pltpu.VMEM((4, HOURS, 2 * HALF), jnp.float32)]
    return in_vmem(finish_kernel, [shape, shape], scratch, "finish", 4, (parts,))


def hour_order(first, second):
    steps = jnp.arange(HOURS, dtype=jnp.int32)
    group, part, inner = steps // GROUP, steps // FINAL % SIDE, steps % FINAL
    return (first + group) % SIDE * GROUP + (second + part) % SIDE * FINAL + inner


def shards(coefficients, sky_year, hour_list, retention):
    me = lax.axis_index("patch")
    x, y, core = me // (2 * SIDE), me // 2 % SIDE, me % 2
    first, second = jnp.where(core == 0, x, y), jnp.where(core == 0, y, x)
    move = lambda value, pairs: lax.ppermute(value, "patch", pairs)
    first_up, first_down = ring(1, False), ring(-1, False)

    chip = jnp.arange(SIDE * SIDE, dtype=jnp.int32)
    one, two = chip // SIDE, chip % SIDE
    chips = jnp.where(
        core == 0,
        (x - one) % SIDE + SIDE * ((y - two) % SIDE),
        (y - two) % SIDE + SIDE * ((x - one) % SIDE),
    )

    spot = core.reshape(1)
    coefficients = pltpu.with_memory_space_constraint(coefficients, pltpu.HBM)
    others = [move(split(piece, spot, coefficients), siblings) for piece in range(PIECES)]
    own_rates = lax.dynamic_slice(retention, (0, core * HALF), (4, HALF))
    their_rates = lax.dynamic_slice(retention, (0, (1 - core) * HALF), (4, HALF))
    chosen = select(hour_list[:, None], sky_year, their_rates)
    got = move(chosen, siblings)
    sky = [message[:HOURS, : PATCHES // 2] for message in (chosen, got)]
    sky = jnp.concatenate(sky, axis=1).astype(jnp.bfloat16)
    sibling_rates = got[HOURS : HOURS + 4]
    rates = jnp.where(
        core == 0,
        jnp.concatenate([own_rates, sibling_rates]),
        jnp.concatenate([sibling_rates, own_rates]),
    )
    order = hour_order(first, second)[:, None]

    rendered = []
    for piece in range(PIECES):
        up, down, *kept = render(piece, spot, order, sky, rates, coefficients, others[piece])
        rendered.append((move(up, first_up), move(down, first_down), *kept))
    merged = []
    for up, down, keep_up, keep_down, mine in rendered:
        relay_up, relay_down = merge(keep_up, keep_down, up, down)
        merged.append((mine, up, down, move(relay_up, first_up), move(relay_down, first_down)))
    *sent, mine, coded_rates = join(0, rates, *merged[0], None)
    *sent, later = join(1, rates, *merged[1], sent)
    got = [move(part, ring(hop, True)) for hop, part in zip((1, 2, 3), sent)]
    parts = glare(chips, coded_rates, *got, mine, later)
    parts = lax.all_to_all(parts, "patch", 0, 0, tiled=True)
    return tuple(finish(parts))


def solution(mesh):
    placed = (P("view", "patch", None, None), P("patch", None), P(), P("patch", None))
    return jax.shard_map(
        shards,
        mesh=mesh,
        in_specs=placed,
        out_specs=(P("patch", "view", None, None), P("patch", "view", None, None)),
        check_vma=False,
    )
```

```python
import functools

import jax
import jax.numpy as jnp
from jax import lax
from jax.experimental import pallas as pl
from jax.experimental.pallas import tpu as pltpu
from jax.sharding import PartitionSpec as P

taps = (0.0625, 0.25, 0.375, 0.25, 0.0625)

SIDE = 4
ROWS = 128
HALF = 256
HOURS = 96
GROUP = HOURS // SIDE
FINAL = GROUP // SIDE
PATCHES = 144
BLOCK = 16
PIECES = 2
PIECE = ROWS // PIECES
PART = PIECE // 2 * GROUP
PAIR = 2 * GROUP
STEPS = 64.0
TOP = 32752.0
FLOOR = 2.0**-100
CHUNK = 56
CHIP_ROWS = 8
RATES = 3 * CHIP_ROWS
SENT = 2 * PART + PAIR + RATES + 8
SECOND = PIECE * FINAL + 16
FIRST = SECOND + SIDE * RATES
MESSAGE = 104


def place(x, y, core):
    return ((x % SIDE) * SIDE + y % SIDE) * 2 + core


def ring(hop, second):
    pairs = []
    for x in range(SIDE):
        for y in range(SIDE):
            for core in range(2):
                along_x = (core == 0) != second
                target = place(x + hop, y, core) if along_x else place(x, y + hop, core)
                pairs.append((place(x, y, core), target))
    return pairs


siblings = [(i, i ^ 1) for i in range(2 * SIDE * SIDE)]


def level_of(biggest):
    return jnp.ceil(STEPS * jnp.log2(jnp.maximum(biggest, FLOOR)))


def factor_of(level):
    return TOP * jnp.exp2(level * (-1.0 / STEPS))


def unit_of(level):
    return jnp.exp2(level * (1.0 / STEPS)) * (1.0 / TOP)


def coded(values, factor):
    return jnp.round(values * factor).astype(jnp.int32).astype(jnp.int16)


def wide(block):
    return block.astype(jnp.int32).astype(jnp.float32)


def narrow(block):
    return block.astype(jnp.int32).astype(jnp.int16)


def digits(rates):
    rest, parts = rates, []
    for _ in range(3):
        rest = rest * 32768.0
        part = jnp.minimum(jnp.floor(rest), 32767.0)
        rest = rest - part
        parts.append(part)
    return jnp.concatenate(parts, axis=0)


def undigits(lines):
    first, second, third = [lines[k * CHIP_ROWS : (k + 1) * CHIP_ROWS] for k in range(3)]
    return (first + (second + third * 2.0**-15) * 2.0**-15) * 2.0**-15


def twice(block):
    return jnp.concatenate([block, block], axis=0)


def lines_at(index, count):
    return pl.ds(pl.multiple_of(index * count, count), count)


def split_kernel(piece, core, source, out, sems):
    columns = pl.ds(pl.multiple_of((1 - core[0]) * HALF, HALF), HALF)
    copies = []
    for index in range(8):
        patches = pl.ds(index * (PATCHES // 16), PATCHES // 16)
        part = source.at[0, patches, pl.ds(piece * PIECE, PIECE), columns]
        copies.append(pltpu.make_async_copy(part, out.at[patches], sems.at[index]))
    for copy in copies:
        copy.start()
    for copy in copies:
        copy.wait()


def split(piece, core, coefficients):
    return pl.pallas_call(
        functools.partial(split_kernel, piece),
        out_shape=pltpu.VMEM((PATCHES // 2, PIECE, HALF), jnp.bfloat16),
        in_specs=[pl.BlockSpec(memory_space=pltpu.SMEM), pl.BlockSpec(memory_space=pl.ANY)],
        out_specs=pl.BlockSpec(memory_space=pltpu.VMEM),
        scratch_shapes=[pltpu.SemaphoreType.DMA((8,))],
        compiler_params=pltpu.CompilerParams(vmem_limit_bytes=4 * 2**20),
        cost_estimate=pl.CostEstimate(flops=0, bytes_accessed=5 * 2**20, transcendentals=0),
        name="split",
    )(core, coefficients)


def select_kernel(hours, sky, rates, out):
    hour = lax.broadcasted_iota(jnp.int32, (HOURS, sky.shape[1]), 1)
    chosen = jnp.where(hours[...] == hour, 1.0, 0.0).astype(jnp.bfloat16)
    out[0:HOURS, 0 : PATCHES // 2] = lax.dot_general(
        chosen, sky[...], (((1,), (1,)), ((), ())), preferred_element_type=jnp.float32
    )
    out[0:HOURS, PATCHES // 2 :] = jnp.zeros((HOURS, HALF - PATCHES // 2), jnp.float32)
    out[HOURS:, :] = jnp.concatenate([rates[...], jnp.zeros_like(rates)], axis=0)


def select(hours, sky, rates):
    out = jax.ShapeDtypeStruct((MESSAGE, HALF), jnp.float32)
    return in_vmem(select_kernel, out, [], "select", 4, (hours, sky, rates))


def render_kernel(
    core, order, sky, rates, own, other, up, down, keep_up, keep_down, mine, images, peaks, ordered
):
    step = pl.program_id(0)

    @pl.when(step == 0)
    def _():
        hour = lax.broadcasted_iota(jnp.int32, (HOURS, HOURS), 1)
        chosen = jnp.where(order[...] == hour, 1.0, 0.0).astype(jnp.bfloat16)
        sorted_sky = jnp.dot(chosen, sky[...], preferred_element_type=jnp.float32)
        ordered[...] = sorted_sky.astype(jnp.bfloat16)
        peaks[...] = jnp.zeros_like(peaks)

    patches = jnp.concatenate([own[...], other[...]], axis=0)
    by_row = jnp.swapaxes(patches, 0, 1)
    rows_seen = ordered[...]
    peak = jnp.zeros((HOURS, HALF), jnp.float32)
    for row in range(BLOCK):
        image = jnp.dot(rows_seen, by_row[row], preferred_element_type=jnp.float32)
        peak = jnp.maximum(peak, jnp.abs(image))
        images[lines_at(step * BLOCK + row, HOURS), :] = image
        mine[lines_at(step * BLOCK + row, GROUP), :] = image[:GROUP]
    half = step // (PIECE // BLOCK // 2)
    peaks[half] = jnp.maximum(peaks[half], peak)

    @pl.when(step == pl.num_programs(0) - 1)
    def _():
        for out, parts in ((up, ((2, 0), (1, 1))), (down, ((2, 1), (3, 0)))):
            levels = []
            for index, (group, half) in enumerate(parts):
                hours = slice(group * GROUP, (group + 1) * GROUP)
                level = level_of(peaks[half, hours, :])
                factor = factor_of(level)
                levels.append(level)
                first = half * (PIECE // 2)

                def pair_step(pair, carry):
                    for k in range(2):
                        start = (first + 2 * pair + k) * HOURS + group * GROUP
                        start = pl.multiple_of(start, GROUP)
                        tile = images[pl.ds(start, GROUP), :] * factor
                        carry = carry + (jnp.round(tile).astype(jnp.int32),)
                    at = pl.multiple_of(index * PART + pair * PAIR, PAIR)
                    out[pl.ds(at, PAIR), :] = jnp.concatenate(carry, axis=0).astype(jnp.int16)
                    return ()

                lax.fori_loop(0, PIECE // 4, pair_step, (), unroll=2)
            pad = jnp.zeros((8, HALF), jnp.float32)
            last = jnp.concatenate(levels + [digits(rates[...]), pad], axis=0)
            out[2 * PART :, :] = narrow(last)
        for out, group, half in ((keep_up, 1, 0), (keep_down, 3, 1)):

            def keep_step(row, carry):
                start = (half * (PIECE // 2) + row) * HOURS + group * GROUP
                out[lines_at(row, GROUP), :] = images[pl.ds(pl.multiple_of(start, GROUP), GROUP), :]
                return carry

            lax.fori_loop(0, PIECE // 2, keep_step, 0, unroll=4)


def render(piece, core, order, sky, rates, own, other):
    whole = lambda i, core: (0, 0)
    steps = PIECE // BLOCK
    sent = jax.ShapeDtypeStruct((SENT, HALF), jnp.int16)
    kept = jax.ShapeDtypeStruct((PART, HALF), jnp.float32)
    outs = [sent, sent, kept, kept, jax.ShapeDtypeStruct((2 * PART, HALF), jnp.float32)]
    return pl.pallas_call(
        render_kernel,
        grid_spec=pltpu.PrefetchScalarGridSpec(
            num_scalar_prefetch=1,
            grid=(steps,),
            in_specs=[
                pl.BlockSpec((HOURS, 1), whole),
                pl.BlockSpec((HOURS, PATCHES), whole),
                pl.BlockSpec((CHIP_ROWS, HALF), whole),
                pl.BlockSpec(
                    (None, PATCHES // 2, BLOCK, HALF),
                    lambda i, core: (0, 0, piece * steps + i, core[0]),
                ),
                pl.BlockSpec((PATCHES // 2, BLOCK, HALF), lambda i, core: (0, i, 0)),
            ],
            out_specs=[pl.BlockSpec(out.shape, whole) for out in outs],
            scratch_shapes=[
                pltpu.VMEM((HOURS * PIECE, HALF), jnp.float32),
                pltpu.VMEM((2, HOURS, HALF), jnp.float32),
                pltpu.VMEM((HOURS, PATCHES), jnp.bfloat16),
            ],
        ),
        out_shape=outs,
        compiler_params=pltpu.CompilerParams(vmem_limit_bytes=16 * 2**20),
        cost_estimate=pl.CostEstimate(
            flops=2 * PATCHES * HOURS * PIECE * HALF, bytes_accessed=18 * 2**20, transcendentals=0
        ),
        name="render",
    )(core, order, sky, rates, own, other)


def in_vmem(kernel, outs, scratch, name, cost, operands, scalars=0):
    spaces = [pltpu.SMEM] * scalars + [pltpu.VMEM] * (len(operands) - scalars)
    return pl.pallas_call(
        kernel,
        out_shape=outs,
        in_specs=[pl.BlockSpec(memory_space=space) for space in spaces],
        out_specs=jax.tree.map(lambda out: pl.BlockSpec(memory_space=pltpu.VMEM), outs),
        scratch_shapes=scratch,
        compiler_params=pltpu.CompilerParams(vmem_limit_bytes=9 * 2**20),
        cost_estimate=pl.CostEstimate(flops=0, bytes_accessed=cost * 2**20, transcendentals=0),
        name=name,
    )(*operands)


def merge_kernel(keep_up, keep_down, got_up, got_down, up, down, total):
    nothing = jnp.zeros((PAIR, HALF), jnp.float32)
    for keep, got, out in ((keep_up, got_up, up), (keep_down, got_down, down)):
        last = wide(got[2 * PART :, :])
        unit = twice(unit_of(last[:GROUP]))

        def add_step(pair, peak):
            at = lines_at(pair, PAIR)
            tile = keep[at, :] + wide(got[at, :]) * unit
            total[at, :] = tile
            return jnp.maximum(peak, jnp.abs(tile))

        peak = lax.fori_loop(0, PART // PAIR, add_step, nothing, unroll=2)
        level = level_of(jnp.maximum(peak[:GROUP], peak[GROUP:]))
        factor = twice(factor_of(level))

        def code_step(pair, carry):
            at = lines_at(pair, PAIR)
            out[at, :] = coded(total[at, :], factor)
            return carry

        lax.fori_loop(0, PART // PAIR, code_step, 0, unroll=2)
        out[PART:, :] = narrow(jnp.concatenate([level, last[PAIR : PAIR + RATES]], axis=0))


def merge(keep_up, keep_down, got_up, got_down):
    sent = jax.ShapeDtypeStruct((PART + GROUP + RATES, HALF), jnp.int16)
    scratch = [pltpu.VMEM((PART, HALF), jnp.float32)]
    return in_vmem(
        merge_kernel, [sent, sent], scratch, "merge", 5, (keep_up, keep_down, got_up, got_down)
    )


def join_kernel(piece, *refs):
    if piece:
        mine, got_up, got_down, up, down, near, far, back, own, total = refs
    else:
        rates, mine, got_up, got_down, up, down, near, far, back, own, own_rates, total = refs
    peak = jnp.zeros((PAIR, HALF), jnp.float32)
    for half, (direct, relayed) in enumerate(((got_down, up), (got_up, down))):
        direct_unit = twice(unit_of(wide(direct[2 * PART :, :])[GROUP:PAIR]))
        relayed_unit = twice(unit_of(wide(relayed[PART:, :])[:GROUP]))

        def add_step(pair, peak):
            at = lines_at(pair, PAIR)
            direct_at = pl.ds(pl.multiple_of(PART + pair * PAIR, PAIR), PAIR)
            out_at = pl.ds(pl.multiple_of(half * PART + pair * PAIR, PAIR), PAIR)
            tile = mine[out_at, :] + wide(direct[direct_at, :]) * direct_unit
            tile = tile + wide(relayed[at, :]) * relayed_unit
            total[out_at, :] = tile
            return jnp.maximum(peak, jnp.abs(tile))

        peak = lax.fori_loop(0, PART // PAIR, add_step, peak, unroll=2)
    level = level_of(jnp.maximum(peak[:GROUP], peak[GROUP:]))
    factor = factor_of(level)
    outs = (own, near, far, back)
    factors = [
        jnp.concatenate([factor[part * FINAL : (part + 1) * FINAL]] * 8, axis=0)
        for part in range(SIDE)
    ]


    def split_step(eight, carry):
        tile = total[lines_at(eight, 8 * GROUP), :]
        for part, out in enumerate(outs):
            starts = [k * GROUP + part * FINAL for k in range(8)]
            block = jnp.concatenate([tile[at : at + FINAL] for at in starts], axis=0)
            if part:
                out[lines_at(eight, 8 * FINAL), :] = coded(block, factors[part])
            else:
                out[lines_at(eight, 8 * FINAL), :] = block
        return carry

    lax.fori_loop(0, PIECE // 8, split_step, 0)
    for part, out in enumerate(outs):
        if part:
            first = PIECE * FINAL
            mark = level[part * FINAL : (part + 1) * FINAL]
            rest = jnp.zeros((16 - FINAL, HALF), jnp.float32)
            out[first : first + 16, :] = narrow(jnp.concatenate([mark, rest], axis=0))
    if not piece:
        places = ((got_up, 2 * PART, PAIR), (up, PART, GROUP), (got_down, 2 * PART, PAIR))
        ahead = [wide(got[start:, :])[at : at + RATES] for got, start, at in places]
        all_rates = narrow(jnp.concatenate([digits(rates[...])] + ahead, axis=0))
        for out in (near, far, back):
            out[PIECE * FINAL + 16 :, :] = all_rates
        own_rates[...] = all_rates


def join(piece, rates, *operands):
    sent = jax.ShapeDtypeStruct((SECOND if piece else FIRST, HALF), jnp.int16)
    outs = [sent] * 3 + [jax.ShapeDtypeStruct((PIECE * FINAL, HALF), jnp.float32)]
    if not piece:
        operands = (rates,) + operands
        outs.append(jax.ShapeDtypeStruct((SIDE * RATES, HALF), jnp.int16))
    scratch = [pltpu.VMEM((2 * PART, HALF), jnp.float32)]
    return in_vmem(functools.partial(join_kernel, piece), outs, scratch, "join", 6, operands)


def spots(eight, k):
    return pl.ds(pl.multiple_of(64 * eight, 64) + 8 * k, FINAL)


def run_down(piece, chips, rates, own, gots, lines, front, state):
    size = PIECE * FINAL
    units = [unit_of(wide(got[size:SECOND, :])[:FINAL]) for got in gots]
    units = [jnp.concatenate([unit] * 8, axis=0) for unit in units]

    def down(index, state):
        at = lines_at(index, 8 * FINAL)
        tile = own[at, :]
        for got, unit in zip(gots, units):
            tile = tile + wide(got[at, :]) * unit
        share = rates[lines_at(chips[piece * (PIECE // 8) + index], 8), :]
        for k in range(8):
            light = tile[k * FINAL : (k + 1) * FINAL]
            state = share[k : k + 1] * state + light
            lines[spots(index, k), :] = light
            front[spots(index, k), :] = state
        return state

    return lax.fori_loop(0, PIECE // 8, down, state)


def upper_kernel(chips, own_rates, near, far, back, mine, rates, lines, front, last):
    blocks = [own_rates] + [got.at[SECOND:FIRST] for got in (near, far, back)]
    for behind, block in enumerate(blocks):
        coded_rates = wide(block[...])
        for chip in range(SIDE):
            start = (behind * SIDE + chip) * CHIP_ROWS
            rates[start : start + CHIP_ROWS, :] = undigits(
                coded_rates[chip * RATES : (chip + 1) * RATES]
            )
    state = jnp.zeros((FINAL, HALF), jnp.float32)
    gots = (near, far, back)
    last[0:FINAL, :] = run_down(0, chips, rates, mine, gots, lines, front, state)


def upper(chips, *operands):
    rows = jax.ShapeDtypeStruct((8 * PIECE, HALF), jnp.float32)
    outs = [
        jax.ShapeDtypeStruct((ROWS, HALF), jnp.float32),
        rows,
        rows,
        jax.ShapeDtypeStruct((8, HALF), jnp.float32),
    ]
    return in_vmem(upper_kernel, outs, [], "upper", 4, (chips, *operands), scalars=1)


def glare_kernel(
    chips, rates, first_lines, first_front, last, near, far, back, mine, out, lines, front
):
    lines[0:16, :] = jnp.zeros((16, HALF), jnp.float32)
    lines[8 * (ROWS + 2) :, :] = jnp.zeros((16, HALF), jnp.float32)
    lines[16 : 16 + 8 * PIECE, :] = first_lines[...]
    front[: 8 * PIECE, :] = first_front[...]
    rest = slice(16 + 8 * PIECE, 16 + 8 * ROWS)
    run_down(
        1,
        chips,
        rates,
        mine,
        (near, far, back),
        lines.at[rest],
        front.at[8 * PIECE :],
        last[0:FINAL, :],
    )
    nothing = jnp.zeros((FINAL, HALF), jnp.float32)

    def up(step, state):
        eight = ROWS // 8 - 1 - step
        share = rates[lines_at(chips[eight], 8), :]
        light = [lines[spots(eight, k), :] for k in range(12)]
        for owner in (1, 0):
            veils, blurs = [None] * 4, [None] * 4
            for k in (3, 2, 1, 0):
                row = owner * 4 + k
                state = share[row : row + 1] * state + light[row + 2]
                veils[k] = 0.125 * (front[spots(eight, row), :] + state)
                near, wider = light[row + 1] + light[row + 3], light[row] + light[row + 4]
                blurs[k] = taps[2] * light[row + 2] + taps[1] * near + taps[0] * wider
            blocks, levels = [], []
            for values in (blurs, veils):
                block = jnp.concatenate(values, axis=0)
                level = level_of(jnp.max(jnp.abs(block), axis=0, keepdims=True))
                blocks.append(jnp.round(block * factor_of(level)))
                levels.append(level)
            rest = jnp.zeros((CHUNK - 8 * FINAL - 2, HALF), jnp.float32)
            out[2 * eight + owner] = narrow(jnp.concatenate(blocks + levels + [rest], axis=0))
        return state

    lax.fori_loop(0, ROWS // 8, up, nothing)


def glare(chips, *operands):
    out = jax.ShapeDtypeStruct((32, CHUNK, HALF), jnp.int16)
    scratch = [
        pltpu.VMEM((8 * (ROWS + 4), HALF), jnp.float32),
        pltpu.VMEM((8 * ROWS, HALF), jnp.float32),
    ]
    return in_vmem(glare_kernel, out, scratch, "glare", 8, (chips, *operands), scalars=1)


def finish_kernel(parts, acuity, veil, blurred):
    for source in range(32):
        x, y, core = source // 8, source // 2 % 4, source % 2
        first, second = (x, y) if core == 0 else (y, x)
        hour = first * GROUP + second * FINAL
        columns = slice(core * HALF, (core + 1) * HALF)
        block = wide(parts[source])
        units = unit_of(block[8 * FINAL : 8 * FINAL + 2])
        for row in range(4):
            at = row * FINAL
            blurred[row, hour : hour + FINAL, columns] = block[at : at + FINAL] * units[0:1]
            at = (row + 4) * FINAL
            veil[row, 0, hour : hour + FINAL, columns] = block[at : at + FINAL] * units[1:2]
    column = lax.broadcasted_iota(jnp.int32, (HOURS, 2 * HALF), 1)
    for row in range(4):
        image = blurred[row]
        total = taps[2] * image
        for offset in (-2, -1, 1, 2):
            moved = pltpu.roll(image, (-offset) % (2 * HALF), 1)
            inside = (column + offset >= 0) & (column + offset < 2 * HALF)
            total = total + taps[2 + offset] * jnp.where(inside, moved, 0.0)
        acuity[row, 0] = total


def finish(parts):
    shape = jax.ShapeDtypeStruct((4, 1, HOURS, 2 * HALF), jnp.float32)
    scratch = [pltpu.VMEM((4, HOURS, 2 * HALF), jnp.float32)]
    return in_vmem(finish_kernel, [shape, shape], scratch, "finish", 4, (parts,))


def hour_order(first, second):
    steps = jnp.arange(HOURS, dtype=jnp.int32)
    group, part, inner = steps // GROUP, steps // FINAL % SIDE, steps % FINAL
    return (first + group) % SIDE * GROUP + (second + part) % SIDE * FINAL + inner


def shards(coefficients, sky_year, hour_list, retention):
    me = lax.axis_index("patch")
    x, y, core = me // (2 * SIDE), me // 2 % SIDE, me % 2
    first, second = jnp.where(core == 0, x, y), jnp.where(core == 0, y, x)
    move = lambda value, pairs: lax.ppermute(value, "patch", pairs)
    first_up, first_down = ring(1, False), ring(-1, False)

    chip = jnp.arange(SIDE * SIDE, dtype=jnp.int32)
    one, two = chip // SIDE, chip % SIDE
    chips = jnp.where(
        core == 0,
        (x - one) % SIDE + SIDE * ((y - two) % SIDE),
        (y - two) % SIDE + SIDE * ((x - one) % SIDE),
    )

    spot = core.reshape(1)
    coefficients = pltpu.with_memory_space_constraint(coefficients, pltpu.HBM)
    others = [move(split(piece, spot, coefficients), siblings) for piece in range(PIECES)]
    own_rates = lax.dynamic_slice(retention, (0, core * HALF), (4, HALF))
    their_rates = lax.dynamic_slice(retention, (0, (1 - core) * HALF), (4, HALF))
    chosen = select(hour_list[:, None], sky_year, their_rates)
    got = move(chosen, siblings)
    sky = [message[:HOURS, : PATCHES // 2] for message in (chosen, got)]
    sky = jnp.concatenate(sky, axis=1).astype(jnp.bfloat16)
    sibling_rates = got[HOURS : HOURS + 4]
    rates = jnp.where(
        core == 0,
        jnp.concatenate([own_rates, sibling_rates]),
        jnp.concatenate([sibling_rates, own_rates]),
    )
    order = hour_order(first, second)[:, None]

    rendered = []
    for piece in range(PIECES):
        up, down, *kept = render(piece, spot, order, sky, rates, coefficients, others[piece])
        rendered.append((move(up, first_up), move(down, first_down), *kept))
    merged = []
    for up, down, keep_up, keep_down, mine in rendered:
        relay_up, relay_down = merge(keep_up, keep_down, up, down)
        merged.append((mine, up, down, move(relay_up, first_up), move(relay_down, first_down)))
    *sent, mine, coded_rates = join(0, rates, *merged[0])
    got = [move(part, ring(hop, True)) for hop, part in zip((1, 2, 3), sent)]
    above = upper(chips, coded_rates, *got, mine)
    *sent, mine = join(1, rates, *merged[1])
    got = [move(part, ring(hop, True)) for hop, part in zip((1, 2, 3), sent)]
    parts = glare(chips, *above, *got, mine)
    parts = lax.all_to_all(parts, "patch", 0, 0, tiled=True)
    return tuple(finish(parts))


def solution(mesh):
    placed = (P("view", "patch", None, None), P("patch", None), P(), P("patch", None))
    return jax.shard_map(
        shards,
        mesh=mesh,
        in_specs=placed,
        out_specs=(P("patch", "view", None, None), P("patch", "view", None, None)),
        check_vma=False,
    )
```

```python
import functools

import jax
import jax.numpy as jnp
from jax import lax
from jax.experimental import pallas as pl
from jax.experimental.pallas import tpu as pltpu
from jax.sharding import PartitionSpec as P

taps = (0.0625, 0.25, 0.375, 0.25, 0.0625)

SIDE = 4
ROWS = 128
HALF = 256
HOURS = 96
GROUP = HOURS // SIDE
FINAL = GROUP // SIDE
PATCHES = 144
BLOCK = 16
PIECES = 2
PIECE = ROWS // PIECES
PART = PIECE // 2 * GROUP
PAIR = 2 * GROUP
STEPS = 64.0
TOP = 32752.0
FLOOR = 2.0**-100
CHUNK = 56
CHIP_ROWS = 8
RATES = 3 * CHIP_ROWS
SENT = 2 * PART + PAIR + RATES + 8
SECOND = PIECE * FINAL + 16
FIRST = SECOND + SIDE * RATES


def place(x, y, core):
    return ((x % SIDE) * SIDE + y % SIDE) * 2 + core


def ring(hop, second):
    pairs = []
    for x in range(SIDE):
        for y in range(SIDE):
            for core in range(2):
                along_x = (core == 0) != second
                target = place(x + hop, y, core) if along_x else place(x, y + hop, core)
                pairs.append((place(x, y, core), target))
    return pairs


siblings = [(i, i ^ 1) for i in range(2 * SIDE * SIDE)]


def level_of(biggest):
    return jnp.ceil(STEPS * jnp.log2(jnp.maximum(biggest, FLOOR)))


def factor_of(level):
    return TOP * jnp.exp2(level * (-1.0 / STEPS))


def unit_of(level):
    return jnp.exp2(level * (1.0 / STEPS)) * (1.0 / TOP)


def coded(values, factor):
    return jnp.round(values * factor).astype(jnp.int32).astype(jnp.int16)


def wide(block):
    return block.astype(jnp.int32).astype(jnp.float32)


def narrow(block):
    return block.astype(jnp.int32).astype(jnp.int16)


def digits(rates):
    rest, parts = rates, []
    for _ in range(3):
        rest = rest * 32768.0
        part = jnp.minimum(jnp.floor(rest), 32767.0)
        rest = rest - part
        parts.append(part)
    return jnp.concatenate(parts, axis=0)


def undigits(lines):
    first, second, third = [lines[k * CHIP_ROWS : (k + 1) * CHIP_ROWS] for k in range(3)]
    return (first + (second + third * 2.0**-15) * 2.0**-15) * 2.0**-15


def twice(block):
    return jnp.concatenate([block, block], axis=0)


def lines_at(index, count):
    return pl.ds(pl.multiple_of(index * count, count), count)


def cut_copies(piece, core, source, out, sems):
    columns = pl.ds(pl.multiple_of((1 - core[0]) * HALF, HALF), HALF)
    copies = []
    for index in range(8):
        patches = pl.ds(index * (PATCHES // 16), PATCHES // 16)
        part = source.at[0, patches, pl.ds(piece * PIECE, PIECE), columns]
        copies.append(pltpu.make_async_copy(part, out.at[patches], sems.at[index]))
    for copy in copies:
        copy.start()
    return copies


def split_kernel(core, source, out, sems):
    for copy in cut_copies(1, core, source, out, sems):
        copy.wait()


def prepare_kernel(core, hours, rates, source, sky_year, out, own_sky, table, sems, sem):
    fetch = pltpu.make_async_copy(sky_year, table, sem)
    fetch.start()
    copies = cut_copies(0, core, source, out, sems)
    hour = lax.broadcasted_iota(jnp.int32, (table.shape[1], HALF), 0)
    chosen = jnp.where(hour == hours[...], 1.0, 0.0).astype(jnp.bfloat16)
    fetch.wait()
    sky = jnp.dot(table[...], chosen, preferred_element_type=jnp.float32)
    own_sky[...] = sky.astype(jnp.bfloat16)
    rest, parts = rates[...], []
    for _ in range(3):
        part = rest.astype(jnp.bfloat16).astype(jnp.float32)
        rest = rest - part
        parts.append(part)
    gap = jnp.zeros((8, HALF), jnp.float32)
    tail_lines = jnp.concatenate([sky[PIECE:], gap] + parts + [gap[:4]] + [gap] * 4, axis=0)
    out[PATCHES // 2] = sky[:PIECE].astype(jnp.bfloat16)
    out[PATCHES // 2 + 1] = tail_lines.astype(jnp.bfloat16)
    for copy in copies:
        copy.wait()


def split(core, coefficients):
    return pl.pallas_call(
        split_kernel,
        out_shape=jax.ShapeDtypeStruct((PATCHES // 2, PIECE, HALF), jnp.bfloat16),
        in_specs=[pl.BlockSpec(memory_space=pltpu.SMEM), pl.BlockSpec(memory_space=pl.ANY)],
        out_specs=pl.BlockSpec(memory_space=pltpu.VMEM),
        scratch_shapes=[pltpu.SemaphoreType.DMA((8,))],
        compiler_params=pltpu.CompilerParams(vmem_limit_bytes=4 * 2**20),
        cost_estimate=pl.CostEstimate(flops=0, bytes_accessed=5 * 2**20, transcendentals=0),
        name="split",
    )(core, coefficients)


def prepare(core, hours, rates, coefficients, sky_year):
    half = PATCHES // 2
    return pl.pallas_call(
        prepare_kernel,
        out_shape=[
            jax.ShapeDtypeStruct((half + 2, PIECE, HALF), jnp.bfloat16),
            jax.ShapeDtypeStruct((half, HALF), jnp.bfloat16),
        ],
        in_specs=[pl.BlockSpec(memory_space=pltpu.SMEM)]
        + [pl.BlockSpec(memory_space=pltpu.VMEM)] * 2
        + [pl.BlockSpec(memory_space=pl.ANY)] * 2,
        out_specs=[pl.BlockSpec(memory_space=pltpu.VMEM)] * 2,
        scratch_shapes=[
            pltpu.VMEM(sky_year.shape, jnp.bfloat16),
            pltpu.SemaphoreType.DMA((8,)),
            pltpu.SemaphoreType.DMA,
        ],
        compiler_params=pltpu.CompilerParams(vmem_limit_bytes=24 * 2**20),
        cost_estimate=pl.CostEstimate(flops=0, bytes_accessed=6 * 2**20, transcendentals=0),
        name="prepare",
    )(core, hours, rates, coefficients, sky_year)


def render_kernel(
    core, order, sky, rates, own, other, up, down, keep_up, keep_down, mine, images, peaks, ordered
):
    step = pl.program_id(0)

    @pl.when(step == 0)
    def _():
        hour = lax.broadcasted_iota(jnp.int32, (HOURS, HOURS), 1)
        chosen = jnp.where(order[...] == hour, 1.0, 0.0).astype(jnp.bfloat16)
        sorted_sky = jnp.dot(chosen, sky[...], preferred_element_type=jnp.float32)
        ordered[...] = sorted_sky.astype(jnp.bfloat16)
        peaks[...] = jnp.zeros_like(peaks)

    patches = jnp.concatenate([own[...], other[...]], axis=0)
    by_row = jnp.swapaxes(patches, 0, 1)
    rows_seen = ordered[...]
    peak = jnp.zeros((HOURS, HALF), jnp.float32)
    for row in range(BLOCK):
        image = jnp.dot(rows_seen, by_row[row], preferred_element_type=jnp.float32)
        peak = jnp.maximum(peak, jnp.abs(image))
        images[lines_at(step * BLOCK + row, HOURS), :] = image
        mine[lines_at(step * BLOCK + row, GROUP), :] = image[:GROUP]
    half = step // (PIECE // BLOCK // 2)
    peaks[half] = jnp.maximum(peaks[half], peak)

    @pl.when(step == pl.num_programs(0) - 1)
    def _():
        for out, parts in ((up, ((2, 0), (1, 1))), (down, ((2, 1), (3, 0)))):
            levels = []
            for index, (group, half) in enumerate(parts):
                hours = slice(group * GROUP, (group + 1) * GROUP)
                level = level_of(peaks[half, hours, :])
                factor = factor_of(level)
                levels.append(level)
                first = half * (PIECE // 2)

                def pair_step(pair, carry):
                    for k in range(2):
                        start = (first + 2 * pair + k) * HOURS + group * GROUP
                        start = pl.multiple_of(start, GROUP)
                        tile = images[pl.ds(start, GROUP), :] * factor
                        carry = carry + (jnp.round(tile).astype(jnp.int32),)
                    at = pl.multiple_of(index * PART + pair * PAIR, PAIR)
                    out[pl.ds(at, PAIR), :] = jnp.concatenate(carry, axis=0).astype(jnp.int16)
                    return ()

                lax.fori_loop(0, PIECE // 4, pair_step, (), unroll=2)
            pad = jnp.zeros((8, HALF), jnp.float32)
            last = jnp.concatenate(levels + [digits(rates[...]), pad], axis=0)
            out[2 * PART :, :] = narrow(last)
        for out, group, half in ((keep_up, 1, 0), (keep_down, 3, 1)):

            def keep_step(row, carry):
                start = (half * (PIECE // 2) + row) * HOURS + group * GROUP
                out[lines_at(row, GROUP), :] = images[pl.ds(pl.multiple_of(start, GROUP), GROUP), :]
                return carry

            lax.fori_loop(0, PIECE // 2, keep_step, 0, unroll=4)


def render(piece, core, order, sky, rates, own, other):
    whole = lambda i, core: (0, 0)
    steps = PIECE // BLOCK
    sent = jax.ShapeDtypeStruct((SENT, HALF), jnp.int16)
    kept = jax.ShapeDtypeStruct((PART, HALF), jnp.float32)
    outs = [sent, sent, kept, kept, jax.ShapeDtypeStruct((2 * PART, HALF), jnp.float32)]
    return pl.pallas_call(
        render_kernel,
        grid_spec=pltpu.PrefetchScalarGridSpec(
            num_scalar_prefetch=1,
            grid=(steps,),
            in_specs=[
                pl.BlockSpec((HOURS, 1), whole),
                pl.BlockSpec((HOURS, PATCHES), whole),
                pl.BlockSpec((CHIP_ROWS, HALF), whole),
                pl.BlockSpec(
                    (None, PATCHES // 2, BLOCK, HALF),
                    lambda i, core: (0, 0, piece * steps + i, core[0]),
                ),
                pl.BlockSpec((PATCHES // 2, BLOCK, HALF), lambda i, core: (0, i, 0)),
            ],
            out_specs=[pl.BlockSpec(out.shape, whole) for out in outs],
            scratch_shapes=[
                pltpu.VMEM((HOURS * PIECE, HALF), jnp.float32),
                pltpu.VMEM((2, HOURS, HALF), jnp.float32),
                pltpu.VMEM((HOURS, PATCHES), jnp.bfloat16),
            ],
        ),
        out_shape=outs,
        compiler_params=pltpu.CompilerParams(vmem_limit_bytes=16 * 2**20),
        cost_estimate=pl.CostEstimate(
            flops=2 * PATCHES * HOURS * PIECE * HALF, bytes_accessed=18 * 2**20, transcendentals=0
        ),
        name="render",
    )(core, order, sky, rates, own, other)


def in_vmem(kernel, outs, scratch, name, cost, operands, scalars=0):
    spaces = [pltpu.SMEM] * scalars + [pltpu.VMEM] * (len(operands) - scalars)
    return pl.pallas_call(
        kernel,
        out_shape=outs,
        in_specs=[pl.BlockSpec(memory_space=space) for space in spaces],
        out_specs=jax.tree.map(lambda out: pl.BlockSpec(memory_space=pltpu.VMEM), outs),
        scratch_shapes=scratch,
        compiler_params=pltpu.CompilerParams(vmem_limit_bytes=9 * 2**20),
        cost_estimate=pl.CostEstimate(flops=0, bytes_accessed=cost * 2**20, transcendentals=0),
        name=name,
    )(*operands)


def merge_kernel(keep_up, keep_down, got_up, got_down, up, down, total):
    nothing = jnp.zeros((PAIR, HALF), jnp.float32)
    for keep, got, out in ((keep_up, got_up, up), (keep_down, got_down, down)):
        last = wide(got[2 * PART :, :])
        unit = twice(unit_of(last[:GROUP]))

        def add_step(pair, peak):
            at = lines_at(pair, PAIR)
            tile = keep[at, :] + wide(got[at, :]) * unit
            total[at, :] = tile
            return jnp.maximum(peak, jnp.abs(tile))

        peak = lax.fori_loop(0, PART // PAIR, add_step, nothing, unroll=2)
        level = level_of(jnp.maximum(peak[:GROUP], peak[GROUP:]))
        factor = twice(factor_of(level))

        def code_step(pair, carry):
            at = lines_at(pair, PAIR)
            out[at, :] = coded(total[at, :], factor)
            return carry

        lax.fori_loop(0, PART // PAIR, code_step, 0, unroll=2)
        out[PART:, :] = narrow(jnp.concatenate([level, last[PAIR : PAIR + RATES]], axis=0))


def merge(keep_up, keep_down, got_up, got_down):
    sent = jax.ShapeDtypeStruct((PART + GROUP + RATES, HALF), jnp.int16)
    scratch = [pltpu.VMEM((PART, HALF), jnp.float32)]
    return in_vmem(
        merge_kernel, [sent, sent], scratch, "merge", 5, (keep_up, keep_down, got_up, got_down)
    )


def join_kernel(piece, *refs):
    if piece:
        mine, got_up, got_down, up, down, near, far, back, own, total = refs
    else:
        rates, mine, got_up, got_down, up, down, near, far, back, own, own_rates, total = refs
    peak = jnp.zeros((PAIR, HALF), jnp.float32)
    for half, (direct, relayed) in enumerate(((got_down, up), (got_up, down))):
        direct_unit = twice(unit_of(wide(direct[2 * PART :, :])[GROUP:PAIR]))
        relayed_unit = twice(unit_of(wide(relayed[PART:, :])[:GROUP]))

        def add_step(pair, peak):
            at = lines_at(pair, PAIR)
            direct_at = pl.ds(pl.multiple_of(PART + pair * PAIR, PAIR), PAIR)
            out_at = pl.ds(pl.multiple_of(half * PART + pair * PAIR, PAIR), PAIR)
            tile = mine[out_at, :] + wide(direct[direct_at, :]) * direct_unit
            tile = tile + wide(relayed[at, :]) * relayed_unit
            total[out_at, :] = tile
            return jnp.maximum(peak, jnp.abs(tile))

        peak = lax.fori_loop(0, PART // PAIR, add_step, peak, unroll=2)
    level = level_of(jnp.maximum(peak[:GROUP], peak[GROUP:]))
    factor = factor_of(level)
    outs = (own, near, far, back)
    factors = [
        jnp.concatenate([factor[part * FINAL : (part + 1) * FINAL]] * 8, axis=0)
        for part in range(SIDE)
    ]


    def split_step(eight, carry):
        tile = total[lines_at(eight, 8 * GROUP), :]
        for part, out in enumerate(outs):
            starts = [k * GROUP + part * FINAL for k in range(8)]
            block = jnp.concatenate([tile[at : at + FINAL] for at in starts], axis=0)
            if part:
                out[lines_at(eight, 8 * FINAL), :] = coded(block, factors[part])
            else:
                out[lines_at(eight, 8 * FINAL), :] = block
        return carry

    lax.fori_loop(0, PIECE // 8, split_step, 0)
    for part, out in enumerate(outs):
        if part:
            first = PIECE * FINAL
            mark = level[part * FINAL : (part + 1) * FINAL]
            rest = jnp.zeros((16 - FINAL, HALF), jnp.float32)
            out[first : first + 16, :] = narrow(jnp.concatenate([mark, rest], axis=0))
    if not piece:
        places = ((got_up, 2 * PART, PAIR), (up, PART, GROUP), (got_down, 2 * PART, PAIR))
        ahead = [wide(got[start:, :])[at : at + RATES] for got, start, at in places]
        all_rates = narrow(jnp.concatenate([digits(rates[...])] + ahead, axis=0))
        for out in (near, far, back):
            out[PIECE * FINAL + 16 :, :] = all_rates
        own_rates[...] = all_rates


def join(piece, rates, *operands):
    sent = jax.ShapeDtypeStruct((SECOND if piece else FIRST, HALF), jnp.int16)
    outs = [sent] * 3 + [jax.ShapeDtypeStruct((PIECE * FINAL, HALF), jnp.float32)]
    if not piece:
        operands = (rates,) + operands
        outs.append(jax.ShapeDtypeStruct((SIDE * RATES, HALF), jnp.int16))
    scratch = [pltpu.VMEM((2 * PART, HALF), jnp.float32)]
    return in_vmem(functools.partial(join_kernel, piece), outs, scratch, "join", 6, operands)


def spots(eight, k):
    return pl.ds(pl.multiple_of(64 * eight, 64) + 8 * k, FINAL)


def run_down(piece, chips, rates, own, gots, lines, front, state):
    size = PIECE * FINAL
    units = [unit_of(wide(got[size:SECOND, :])[:FINAL]) for got in gots]
    units = [jnp.concatenate([unit] * 8, axis=0) for unit in units]

    def down(index, state):
        at = lines_at(index, 8 * FINAL)
        tile = own[at, :]
        for got, unit in zip(gots, units):
            tile = tile + wide(got[at, :]) * unit
        share = rates[lines_at(chips[piece * (PIECE // 8) + index], 8), :]
        for k in range(8):
            light = tile[k * FINAL : (k + 1) * FINAL]
            state = share[k : k + 1] * state + light
            lines[spots(index, k), :] = light
            front[spots(index, k), :] = state
        return state

    return lax.fori_loop(0, PIECE // 8, down, state)


def upper_kernel(chips, own_rates, near, far, back, mine, rates, lines, front, last):
    blocks = [own_rates] + [got.at[SECOND:FIRST] for got in (near, far, back)]
    for behind, block in enumerate(blocks):
        coded_rates = wide(block[...])
        for chip in range(SIDE):
            start = (behind * SIDE + chip) * CHIP_ROWS
            rates[start : start + CHIP_ROWS, :] = undigits(
                coded_rates[chip * RATES : (chip + 1) * RATES]
            )
    state = jnp.zeros((FINAL, HALF), jnp.float32)
    gots = (near, far, back)
    last[0:FINAL, :] = run_down(0, chips, rates, mine, gots, lines, front, state)


def upper(chips, *operands):
    rows = jax.ShapeDtypeStruct((8 * PIECE, HALF), jnp.float32)
    outs = [
        jax.ShapeDtypeStruct((ROWS, HALF), jnp.float32),
        rows,
        rows,
        jax.ShapeDtypeStruct((8, HALF), jnp.float32),
    ]
    return in_vmem(upper_kernel, outs, [], "upper", 4, (chips, *operands), scalars=1)


def glare_kernel(
    chips, rates, first_lines, first_front, last, near, far, back, mine, out, lines, front
):
    lines[0:16, :] = jnp.zeros((16, HALF), jnp.float32)
    lines[8 * (ROWS + 2) :, :] = jnp.zeros((16, HALF), jnp.float32)
    lines[16 : 16 + 8 * PIECE, :] = first_lines[...]
    front[: 8 * PIECE, :] = first_front[...]
    rest = slice(16 + 8 * PIECE, 16 + 8 * ROWS)
    run_down(
        1,
        chips,
        rates,
        mine,
        (near, far, back),
        lines.at[rest],
        front.at[8 * PIECE :],
        last[0:FINAL, :],
    )
    nothing = jnp.zeros((FINAL, HALF), jnp.float32)

    def up(step, state):
        eight = ROWS // 8 - 1 - step
        share = rates[lines_at(chips[eight], 8), :]
        light = [lines[spots(eight, k), :] for k in range(12)]
        for owner in (1, 0):
            veils, blurs = [None] * 4, [None] * 4
            for k in (3, 2, 1, 0):
                row = owner * 4 + k
                state = share[row : row + 1] * state + light[row + 2]
                veils[k] = 0.125 * (front[spots(eight, row), :] + state)
                near, wider = light[row + 1] + light[row + 3], light[row] + light[row + 4]
                blurs[k] = taps[2] * light[row + 2] + taps[1] * near + taps[0] * wider
            blocks, levels = [], []
            for values in (blurs, veils):
                block = jnp.concatenate(values, axis=0)
                level = level_of(jnp.max(jnp.abs(block), axis=0, keepdims=True))
                blocks.append(jnp.round(block * factor_of(level)))
                levels.append(level)
            rest = jnp.zeros((CHUNK - 8 * FINAL - 2, HALF), jnp.float32)
            out[2 * eight + owner] = narrow(jnp.concatenate(blocks + levels + [rest], axis=0))
        return state

    lax.fori_loop(0, ROWS // 8, up, nothing)


def glare(chips, *operands):
    out = jax.ShapeDtypeStruct((32, CHUNK, HALF), jnp.int16)
    scratch = [
        pltpu.VMEM((8 * (ROWS + 4), HALF), jnp.float32),
        pltpu.VMEM((8 * ROWS, HALF), jnp.float32),
    ]
    return in_vmem(glare_kernel, out, scratch, "glare", 8, (chips, *operands), scalars=1)


def finish_kernel(parts, acuity, veil, blurred):
    for source in range(32):
        x, y, core = source // 8, source // 2 % 4, source % 2
        first, second = (x, y) if core == 0 else (y, x)
        hour = first * GROUP + second * FINAL
        columns = slice(core * HALF, (core + 1) * HALF)
        block = wide(parts[source])
        units = unit_of(block[8 * FINAL : 8 * FINAL + 2])
        for row in range(4):
            at = row * FINAL
            blurred[row, hour : hour + FINAL, columns] = block[at : at + FINAL] * units[0:1]
            at = (row + 4) * FINAL
            veil[row, 0, hour : hour + FINAL, columns] = block[at : at + FINAL] * units[1:2]
    column = lax.broadcasted_iota(jnp.int32, (HOURS, 2 * HALF), 1)
    for row in range(4):
        image = blurred[row]
        total = taps[2] * image
        for offset in (-2, -1, 1, 2):
            moved = pltpu.roll(image, (-offset) % (2 * HALF), 1)
            inside = (column + offset >= 0) & (column + offset < 2 * HALF)
            total = total + taps[2 + offset] * jnp.where(inside, moved, 0.0)
        acuity[row, 0] = total


def finish(parts):
    shape = jax.ShapeDtypeStruct((4, 1, HOURS, 2 * HALF), jnp.float32)
    scratch = [pltpu.VMEM((4, HOURS, 2 * HALF), jnp.float32)]
    return in_vmem(finish_kernel, [shape, shape], scratch, "finish", 4, (parts,))


def hour_order(first, second):
    steps = jnp.arange(HOURS, dtype=jnp.int32)
    group, part, inner = steps // GROUP, steps // FINAL % SIDE, steps % FINAL
    return (first + group) % SIDE * GROUP + (second + part) % SIDE * FINAL + inner


def shards(coefficients, sky_year, hour_list, retention):
    me = lax.axis_index("patch")
    x, y, core = me // (2 * SIDE), me // 2 % SIDE, me % 2
    first, second = jnp.where(core == 0, x, y), jnp.where(core == 0, y, x)
    move = lambda value, pairs: lax.ppermute(value, "patch", pairs)
    first_up, first_down = ring(1, False), ring(-1, False)

    chip = jnp.arange(SIDE * SIDE, dtype=jnp.int32)
    one, two = chip // SIDE, chip % SIDE
    chips = jnp.where(
        core == 0,
        (x - one) % SIDE + SIDE * ((y - two) % SIDE),
        (y - two) % SIDE + SIDE * ((x - one) % SIDE),
    )

    spot = core.reshape(1)
    coefficients = pltpu.with_memory_space_constraint(coefficients, pltpu.HBM)
    sky_year = pltpu.with_memory_space_constraint(sky_year, pltpu.HBM)
    own_rates = lax.dynamic_slice(retention, (0, core * HALF), (4, HALF))
    their_rates = lax.dynamic_slice(retention, (0, (1 - core) * HALF), (4, HALF))
    hours = jnp.pad(hour_list[None, :], ((0, 0), (0, HALF - HOURS)), constant_values=-1)
    message, own_sky = prepare(spot, hours, their_rates, coefficients, sky_year)
    others = [move(message, siblings), move(split(spot, coefficients), siblings)]
    half = PATCHES // 2
    extra = others[0][half:].reshape(2 * PIECE, HALF)
    sky = jnp.concatenate([own_sky[:, :HOURS], extra[:half, :HOURS]], axis=0).T
    digits_of = extra[half + 8 : half + 20].astype(jnp.float32)
    sibling_rates = digits_of[0:4] + (digits_of[4:8] + digits_of[8:12])
    rates = jnp.where(
        core == 0,
        jnp.concatenate([own_rates, sibling_rates]),
        jnp.concatenate([sibling_rates, own_rates]),
    )
    order = hour_order(first, second)[:, None]

    rendered = []
    for piece in range(PIECES):
        up, down, *kept = render(piece, spot, order, sky, rates, coefficients, others[piece])
        rendered.append((move(up, first_up), move(down, first_down), *kept))
    merged = []
    for up, down, keep_up, keep_down, mine in rendered:
        relay_up, relay_down = merge(keep_up, keep_down, up, down)
        merged.append((mine, up, down, move(relay_up, first_up), move(relay_down, first_down)))
    *sent, mine, coded_rates = join(0, rates, *merged[0])
    got = [move(part, ring(hop, True)) for hop, part in zip((1, 2, 3), sent)]
    above = upper(chips, coded_rates, *got, mine)
    *sent, mine = join(1, rates, *merged[1])
    got = [move(part, ring(hop, True)) for hop, part in zip((1, 2, 3), sent)]
    parts = glare(chips, *above, *got, mine)
    parts = lax.all_to_all(parts, "patch", 0, 0, tiled=True)
    return tuple(finish(parts))


def solution(mesh):
    placed = (P("view", "patch", None, None), P("patch", None), P(), P("patch", None))
    return jax.shard_map(
        shards,
        mesh=mesh,
        in_specs=placed,
        out_specs=(P("patch", "view", None, None), P("patch", "view", None, None)),
        check_vma=False,
    )
```

```python
import functools

import jax
import jax.numpy as jnp
from jax import lax
from jax.experimental import pallas as pl
from jax.experimental.pallas import tpu as pltpu
from jax.sharding import PartitionSpec as P

taps = (0.0625, 0.25, 0.375, 0.25, 0.0625)

SIDE = 4
ROWS = 128
HALF = 256
HOURS = 96
GROUP = HOURS // SIDE
FINAL = GROUP // SIDE
PATCHES = 144
BLOCK = 16
PIECES = 2
PIECE = ROWS // PIECES
PART = PIECE // 2 * GROUP
PAIR = 2 * GROUP
STEPS = 64.0
TOP = 32752.0
FLOOR = 2.0**-100
CHUNK = 56
CHIP_ROWS = 8
RATES = 3 * CHIP_ROWS
SENT = 2 * PART + PAIR + RATES + 8
SECOND = PIECE * FINAL + 16
FIRST = SECOND + SIDE * RATES


def place(x, y, core):
    return ((x % SIDE) * SIDE + y % SIDE) * 2 + core


def ring(hop, second):
    pairs = []
    for x in range(SIDE):
        for y in range(SIDE):
            for core in range(2):
                along_x = (core == 0) != second
                target = place(x + hop, y, core) if along_x else place(x, y + hop, core)
                pairs.append((place(x, y, core), target))
    return pairs


siblings = [(i, i ^ 1) for i in range(2 * SIDE * SIDE)]


def level_of(biggest):
    return jnp.ceil(STEPS * jnp.log2(jnp.maximum(biggest, FLOOR)))


def factor_of(level):
    return TOP * jnp.exp2(level * (-1.0 / STEPS))


def unit_of(level):
    return jnp.exp2(level * (1.0 / STEPS)) * (1.0 / TOP)


def coded(values, factor):
    return jnp.round(values * factor).astype(jnp.int32).astype(jnp.int16)


def wide(block):
    return block.astype(jnp.int32).astype(jnp.float32)


def narrow(block):
    return block.astype(jnp.int32).astype(jnp.int16)


def digits(rates):
    rest, parts = rates, []
    for _ in range(3):
        rest = rest * 32768.0
        part = jnp.minimum(jnp.floor(rest), 32767.0)
        rest = rest - part
        parts.append(part)
    return jnp.concatenate(parts, axis=0)


def undigits(lines):
    first, second, third = [lines[k * CHIP_ROWS : (k + 1) * CHIP_ROWS] for k in range(3)]
    return (first + (second + third * 2.0**-15) * 2.0**-15) * 2.0**-15


def twice(block):
    return jnp.concatenate([block, block], axis=0)


def lines_at(index, count):
    return pl.ds(pl.multiple_of(index * count, count), count)


def cut_copies(piece, core, source, out, sems):
    columns = pl.ds(pl.multiple_of((1 - core[0]) * HALF, HALF), HALF)
    copies = []
    for index in range(8):
        patches = pl.ds(index * (PATCHES // 16), PATCHES // 16)
        part = source.at[0, patches, pl.ds(piece * PIECE, PIECE), columns]
        copies.append(pltpu.make_async_copy(part, out.at[patches], sems.at[index]))
    for copy in copies:
        copy.start()
    return copies


def split_kernel(core, source, out, sems):
    for copy in cut_copies(1, core, source, out, sems):
        copy.wait()


def prepare_kernel(core, hours, rates, source, sky_year, out, own_sky, table, padded, sems, sem):
    fetch = pltpu.make_async_copy(sky_year, table, sem)
    fetch.start()
    copies = cut_copies(0, core, source, out, sems)
    hour = lax.broadcasted_iota(jnp.int32, (table.shape[1], HOURS), 0)
    chosen = jnp.where(hour == hours[...], 1.0, 0.0).astype(jnp.bfloat16)
    fetch.wait()
    padded[...] = jnp.zeros_like(padded)
    padded[:, :HOURS] = jnp.dot(table[...], chosen, preferred_element_type=jnp.float32)
    sky = padded[...]
    own_sky[...] = sky.astype(jnp.bfloat16)
    rest, parts = jnp.where(core[0] == 0, rates[:, HALF:], rates[:, :HALF]), []
    for _ in range(3):
        part = rest.astype(jnp.bfloat16).astype(jnp.float32)
        rest = rest - part
        parts.append(part)
    gap = jnp.zeros((8, HALF), jnp.float32)
    tail_lines = jnp.concatenate([sky[PIECE:], gap] + parts + [gap[:4]] + [gap] * 4, axis=0)
    out[PATCHES // 2] = sky[:PIECE].astype(jnp.bfloat16)
    out[PATCHES // 2 + 1] = tail_lines.astype(jnp.bfloat16)
    for copy in copies:
        copy.wait()


def split(core, coefficients):
    return pl.pallas_call(
        split_kernel,
        out_shape=jax.ShapeDtypeStruct((PATCHES // 2, PIECE, HALF), jnp.bfloat16),
        in_specs=[pl.BlockSpec(memory_space=pltpu.SMEM), pl.BlockSpec(memory_space=pl.ANY)],
        out_specs=pl.BlockSpec(memory_space=pltpu.VMEM),
        scratch_shapes=[pltpu.SemaphoreType.DMA((8,))],
        compiler_params=pltpu.CompilerParams(vmem_limit_bytes=4 * 2**20),
        cost_estimate=pl.CostEstimate(flops=0, bytes_accessed=5 * 2**20, transcendentals=0),
        name="split",
    )(core, coefficients)


def prepare(core, hours, rates, coefficients, sky_year):
    half = PATCHES // 2
    return pl.pallas_call(
        prepare_kernel,
        out_shape=[
            jax.ShapeDtypeStruct((half + 2, PIECE, HALF), jnp.bfloat16),
            jax.ShapeDtypeStruct((half, HALF), jnp.bfloat16),
        ],
        in_specs=[pl.BlockSpec(memory_space=pltpu.SMEM)]
        + [pl.BlockSpec(memory_space=pltpu.VMEM)] * 2
        + [pl.BlockSpec(memory_space=pl.ANY)] * 2,
        out_specs=[pl.BlockSpec(memory_space=pltpu.VMEM)] * 2,
        scratch_shapes=[
            pltpu.VMEM(sky_year.shape, jnp.bfloat16),
            pltpu.VMEM((half, HALF), jnp.float32),
            pltpu.SemaphoreType.DMA((8,)),
            pltpu.SemaphoreType.DMA,
        ],
        compiler_params=pltpu.CompilerParams(vmem_limit_bytes=14 * 2**20),
        cost_estimate=pl.CostEstimate(flops=0, bytes_accessed=6 * 2**20, transcendentals=0),
        name="prepare",
    )(core, hours, rates, coefficients, sky_year)


def render_kernel(
    core, order, sky, rates, own, other, up, down, keep_up, keep_down, mine, images, peaks, ordered
):
    step = pl.program_id(0)

    @pl.when(step == 0)
    def _():
        hour = lax.broadcasted_iota(jnp.int32, (HOURS, HOURS), 1)
        chosen = jnp.where(order[...] == hour, 1.0, 0.0).astype(jnp.bfloat16)
        sorted_sky = jnp.dot(chosen, sky[...], preferred_element_type=jnp.float32)
        ordered[...] = sorted_sky.astype(jnp.bfloat16)
        peaks[...] = jnp.zeros_like(peaks)

    patches = jnp.concatenate([own[...], other[...]], axis=0)
    by_row = jnp.swapaxes(patches, 0, 1)
    rows_seen = ordered[...]
    peak = jnp.zeros((HOURS, HALF), jnp.float32)
    for row in range(BLOCK):
        image = jnp.dot(rows_seen, by_row[row], preferred_element_type=jnp.float32)
        peak = jnp.maximum(peak, jnp.abs(image))
        images[lines_at(step * BLOCK + row, HOURS), :] = image
        mine[lines_at(step * BLOCK + row, GROUP), :] = image[:GROUP]
    half = step // (PIECE // BLOCK // 2)
    peaks[half] = jnp.maximum(peaks[half], peak)

    @pl.when(step == pl.num_programs(0) - 1)
    def _():
        for out, parts in ((up, ((2, 0), (1, 1))), (down, ((2, 1), (3, 0)))):
            levels = []
            for index, (group, half) in enumerate(parts):
                hours = slice(group * GROUP, (group + 1) * GROUP)
                level = level_of(peaks[half, hours, :])
                factor = factor_of(level)
                levels.append(level)
                first = half * (PIECE // 2)

                def pair_step(pair, carry):
                    for k in range(2):
                        start = (first + 2 * pair + k) * HOURS + group * GROUP
                        start = pl.multiple_of(start, GROUP)
                        tile = images[pl.ds(start, GROUP), :] * factor
                        carry = carry + (jnp.round(tile).astype(jnp.int32),)
                    at = pl.multiple_of(index * PART + pair * PAIR, PAIR)
                    out[pl.ds(at, PAIR), :] = jnp.concatenate(carry, axis=0).astype(jnp.int16)
                    return ()

                lax.fori_loop(0, PIECE // 4, pair_step, (), unroll=2)
            pad = jnp.zeros((8, HALF), jnp.float32)
            last = jnp.concatenate(levels + [digits(rates[...]), pad], axis=0)
            out[2 * PART :, :] = narrow(last)
        for out, group, half in ((keep_up, 1, 0), (keep_down, 3, 1)):

            def keep_step(row, carry):
                start = (half * (PIECE // 2) + row) * HOURS + group * GROUP
                out[lines_at(row, GROUP), :] = images[pl.ds(pl.multiple_of(start, GROUP), GROUP), :]
                return carry

            lax.fori_loop(0, PIECE // 2, keep_step, 0, unroll=4)


def render(piece, core, order, sky, rates, own, other):
    whole = lambda i, core: (0, 0)
    steps = PIECE // BLOCK
    sent = jax.ShapeDtypeStruct((SENT, HALF), jnp.int16)
    kept = jax.ShapeDtypeStruct((PART, HALF), jnp.float32)
    outs = [sent, sent, kept, kept, jax.ShapeDtypeStruct((2 * PART, HALF), jnp.float32)]
    return pl.pallas_call(
        render_kernel,
        grid_spec=pltpu.PrefetchScalarGridSpec(
            num_scalar_prefetch=1,
            grid=(steps,),
            in_specs=[
                pl.BlockSpec((HOURS, 1), whole),
                pl.BlockSpec((HOURS, PATCHES), whole),
                pl.BlockSpec((CHIP_ROWS, HALF), whole),
                pl.BlockSpec(
                    (None, PATCHES // 2, BLOCK, HALF),
                    lambda i, core: (0, 0, piece * steps + i, core[0]),
                ),
                pl.BlockSpec((PATCHES // 2, BLOCK, HALF), lambda i, core: (0, i, 0)),
            ],
            out_specs=[pl.BlockSpec(out.shape, whole) for out in outs],
            scratch_shapes=[
                pltpu.VMEM((HOURS * PIECE, HALF), jnp.float32),
                pltpu.VMEM((2, HOURS, HALF), jnp.float32),
                pltpu.VMEM((HOURS, PATCHES), jnp.bfloat16),
            ],
        ),
        out_shape=outs,
        compiler_params=pltpu.CompilerParams(vmem_limit_bytes=16 * 2**20),
        cost_estimate=pl.CostEstimate(
            flops=2 * PATCHES * HOURS * PIECE * HALF, bytes_accessed=18 * 2**20, transcendentals=0
        ),
        name="render",
    )(core, order, sky, rates, own, other)


def in_vmem(kernel, outs, scratch, name, cost, operands, scalars=0):
    spaces = [pltpu.SMEM] * scalars + [pltpu.VMEM] * (len(operands) - scalars)
    return pl.pallas_call(
        kernel,
        out_shape=outs,
        in_specs=[pl.BlockSpec(memory_space=space) for space in spaces],
        out_specs=jax.tree.map(lambda out: pl.BlockSpec(memory_space=pltpu.VMEM), outs),
        scratch_shapes=scratch,
        compiler_params=pltpu.CompilerParams(vmem_limit_bytes=9 * 2**20),
        cost_estimate=pl.CostEstimate(flops=0, bytes_accessed=cost * 2**20, transcendentals=0),
        name=name,
    )(*operands)


def merge_kernel(keep_up, keep_down, got_up, got_down, up, down, total):
    nothing = jnp.zeros((PAIR, HALF), jnp.float32)
    for keep, got, out in ((keep_up, got_up, up), (keep_down, got_down, down)):
        last = wide(got[2 * PART :, :])
        unit = twice(unit_of(last[:GROUP]))

        def add_step(pair, peak):
            at = lines_at(pair, PAIR)
            tile = keep[at, :] + wide(got[at, :]) * unit
            total[at, :] = tile
            return jnp.maximum(peak, jnp.abs(tile))

        peak = lax.fori_loop(0, PART // PAIR, add_step, nothing, unroll=2)
        level = level_of(jnp.maximum(peak[:GROUP], peak[GROUP:]))
        factor = twice(factor_of(level))

        def code_step(pair, carry):
            at = lines_at(pair, PAIR)
            out[at, :] = coded(total[at, :], factor)
            return carry

        lax.fori_loop(0, PART // PAIR, code_step, 0, unroll=2)
        out[PART:, :] = narrow(jnp.concatenate([level, last[PAIR : PAIR + RATES]], axis=0))


def merge(keep_up, keep_down, got_up, got_down):
    sent = jax.ShapeDtypeStruct((PART + GROUP + RATES, HALF), jnp.int16)
    scratch = [pltpu.VMEM((PART, HALF), jnp.float32)]
    return in_vmem(
        merge_kernel, [sent, sent], scratch, "merge", 5, (keep_up, keep_down, got_up, got_down)
    )


def join_kernel(piece, *refs):
    if piece:
        mine, got_up, got_down, up, down, near, far, back, own, total = refs
    else:
        rates, mine, got_up, got_down, up, down, near, far, back, own, own_rates, total = refs
    peak = jnp.zeros((PAIR, HALF), jnp.float32)
    for half, (direct, relayed) in enumerate(((got_down, up), (got_up, down))):
        direct_unit = twice(unit_of(wide(direct[2 * PART :, :])[GROUP:PAIR]))
        relayed_unit = twice(unit_of(wide(relayed[PART:, :])[:GROUP]))

        def add_step(pair, peak):
            at = lines_at(pair, PAIR)
            direct_at = pl.ds(pl.multiple_of(PART + pair * PAIR, PAIR), PAIR)
            out_at = pl.ds(pl.multiple_of(half * PART + pair * PAIR, PAIR), PAIR)
            tile = mine[out_at, :] + wide(direct[direct_at, :]) * direct_unit
            tile = tile + wide(relayed[at, :]) * relayed_unit
            total[out_at, :] = tile
            return jnp.maximum(peak, jnp.abs(tile))

        peak = lax.fori_loop(0, PART // PAIR, add_step, peak, unroll=2)
    level = level_of(jnp.maximum(peak[:GROUP], peak[GROUP:]))
    factor = factor_of(level)
    outs = (own, near, far, back)
    factors = [
        jnp.concatenate([factor[part * FINAL : (part + 1) * FINAL]] * 8, axis=0)
        for part in range(SIDE)
    ]


    def split_step(eight, carry):
        tile = total[lines_at(eight, 8 * GROUP), :]
        for part, out in enumerate(outs):
            starts = [k * GROUP + part * FINAL for k in range(8)]
            block = jnp.concatenate([tile[at : at + FINAL] for at in starts], axis=0)
            if part:
                out[lines_at(eight, 8 * FINAL), :] = coded(block, factors[part])
            else:
                out[lines_at(eight, 8 * FINAL), :] = block
        return carry

    lax.fori_loop(0, PIECE // 8, split_step, 0)
    for part, out in enumerate(outs):
        if part:
            first = PIECE * FINAL
            mark = level[part * FINAL : (part + 1) * FINAL]
            rest = jnp.zeros((16 - FINAL, HALF), jnp.float32)
            out[first : first + 16, :] = narrow(jnp.concatenate([mark, rest], axis=0))
    if not piece:
        places = ((got_up, 2 * PART, PAIR), (up, PART, GROUP), (got_down, 2 * PART, PAIR))
        ahead = [wide(got[start:, :])[at : at + RATES] for got, start, at in places]
        all_rates = narrow(jnp.concatenate([digits(rates[...])] + ahead, axis=0))
        for out in (near, far, back):
            out[PIECE * FINAL + 16 :, :] = all_rates
        own_rates[...] = all_rates


def join(piece, rates, *operands):
    sent = jax.ShapeDtypeStruct((SECOND if piece else FIRST, HALF), jnp.int16)
    outs = [sent] * 3 + [jax.ShapeDtypeStruct((PIECE * FINAL, HALF), jnp.float32)]
    if not piece:
        operands = (rates,) + operands
        outs.append(jax.ShapeDtypeStruct((SIDE * RATES, HALF), jnp.int16))
    scratch = [pltpu.VMEM((2 * PART, HALF), jnp.float32)]
    return in_vmem(functools.partial(join_kernel, piece), outs, scratch, "join", 6, operands)


def spots(eight, k):
    return pl.ds(pl.multiple_of(64 * eight, 64) + 8 * k, FINAL)


def run_down(piece, chips, rates, own, gots, lines, front, state):
    size = PIECE * FINAL
    units = [unit_of(wide(got[size:SECOND, :])[:FINAL]) for got in gots]
    units = [jnp.concatenate([unit] * 8, axis=0) for unit in units]

    def down(index, state):
        at = lines_at(index, 8 * FINAL)
        tile = own[at, :]
        for got, unit in zip(gots, units):
            tile = tile + wide(got[at, :]) * unit
        share = rates[lines_at(chips[piece * (PIECE // 8) + index], 8), :]
        for k in range(8):
            light = tile[k * FINAL : (k + 1) * FINAL]
            state = share[k : k + 1] * state + light
            lines[spots(index, k), :] = light
            front[spots(index, k), :] = state
        return state

    return lax.fori_loop(0, PIECE // 8, down, state)


def upper_kernel(chips, own_rates, near, far, back, mine, rates, lines, front, last):
    blocks = [own_rates] + [got.at[SECOND:FIRST] for got in (near, far, back)]
    for behind, block in enumerate(blocks):
        coded_rates = wide(block[...])
        for chip in range(SIDE):
            start = (behind * SIDE + chip) * CHIP_ROWS
            rates[start : start + CHIP_ROWS, :] = undigits(
                coded_rates[chip * RATES : (chip + 1) * RATES]
            )
    state = jnp.zeros((FINAL, HALF), jnp.float32)
    gots = (near, far, back)
    last[0:FINAL, :] = run_down(0, chips, rates, mine, gots, lines, front, state)


def upper(chips, *operands):
    rows = jax.ShapeDtypeStruct((8 * PIECE, HALF), jnp.float32)
    outs = [
        jax.ShapeDtypeStruct((ROWS, HALF), jnp.float32),
        rows,
        rows,
        jax.ShapeDtypeStruct((8, HALF), jnp.float32),
    ]
    return in_vmem(upper_kernel, outs, [], "upper", 4, (chips, *operands), scalars=1)


def glare_kernel(
    chips, rates, first_lines, first_front, last, near, far, back, mine, out, lines, front
):
    lines[0:16, :] = jnp.zeros((16, HALF), jnp.float32)
    lines[8 * (ROWS + 2) :, :] = jnp.zeros((16, HALF), jnp.float32)
    lines[16 : 16 + 8 * PIECE, :] = first_lines[...]
    front[: 8 * PIECE, :] = first_front[...]
    rest = slice(16 + 8 * PIECE, 16 + 8 * ROWS)
    run_down(
        1,
        chips,
        rates,
        mine,
        (near, far, back),
        lines.at[rest],
        front.at[8 * PIECE :],
        last[0:FINAL, :],
    )
    nothing = jnp.zeros((FINAL, HALF), jnp.float32)

    def up(step, state):
        eight = ROWS // 8 - 1 - step
        share = rates[lines_at(chips[eight], 8), :]
        light = [lines[spots(eight, k), :] for k in range(12)]
        for owner in (1, 0):
            veils, blurs = [None] * 4, [None] * 4
            for k in (3, 2, 1, 0):
                row = owner * 4 + k
                state = share[row : row + 1] * state + light[row + 2]
                veils[k] = 0.125 * (front[spots(eight, row), :] + state)
                near, wider = light[row + 1] + light[row + 3], light[row] + light[row + 4]
                blurs[k] = taps[2] * light[row + 2] + taps[1] * near + taps[0] * wider
            blocks, levels = [], []
            for values in (blurs, veils):
                block = jnp.concatenate(values, axis=0)
                level = level_of(jnp.max(jnp.abs(block), axis=0, keepdims=True))
                blocks.append(jnp.round(block * factor_of(level)))
                levels.append(level)
            rest = jnp.zeros((CHUNK - 8 * FINAL - 2, HALF), jnp.float32)
            out[2 * eight + owner] = narrow(jnp.concatenate(blocks + levels + [rest], axis=0))
        return state

    lax.fori_loop(0, ROWS // 8, up, nothing)


def glare(chips, *operands):
    out = jax.ShapeDtypeStruct((32, CHUNK, HALF), jnp.int16)
    scratch = [
        pltpu.VMEM((8 * (ROWS + 4), HALF), jnp.float32),
        pltpu.VMEM((8 * ROWS, HALF), jnp.float32),
    ]
    return in_vmem(glare_kernel, out, scratch, "glare", 8, (chips, *operands), scalars=1)


def finish_kernel(parts, acuity, veil, blurred, glares, finished, sems):
    for source in range(32):
        x, y, core = source // 8, source // 2 % 4, source % 2
        first, second = (x, y) if core == 0 else (y, x)
        hour = first * GROUP + second * FINAL
        columns = slice(core * HALF, (core + 1) * HALF)
        block = wide(parts[source])
        units = unit_of(block[8 * FINAL : 8 * FINAL + 2])
        for row in range(4):
            at = row * FINAL
            blurred[row, hour : hour + FINAL, columns] = block[at : at + FINAL] * units[0:1]
            at = (row + 4) * FINAL
            glares[row, 0, hour : hour + FINAL, columns] = block[at : at + FINAL] * units[1:2]
    copies = [pltpu.make_async_copy(glares, veil, sems.at[4])]
    copies[0].start()
    column = lax.broadcasted_iota(jnp.int32, (HOURS, 2 * HALF), 1)
    for row in range(4):
        image = blurred[row]
        total = taps[2] * image
        for offset in (-2, -1, 1, 2):
            moved = pltpu.roll(image, (-offset) % (2 * HALF), 1)
            inside = (column + offset >= 0) & (column + offset < 2 * HALF)
            total = total + taps[2 + offset] * jnp.where(inside, moved, 0.0)
        finished[row, 0] = total
        copies.append(pltpu.make_async_copy(finished.at[row], acuity.at[row], sems.at[row]))
        copies[-1].start()
    for copy in copies:
        copy.wait()


def finish(parts):
    shape = (4, 1, HOURS, 2 * HALF)
    return pl.pallas_call(
        finish_kernel,
        out_shape=[pltpu.HBM(shape, jnp.float32)] * 2,
        in_specs=[pl.BlockSpec(memory_space=pltpu.VMEM)],
        out_specs=[pl.BlockSpec(memory_space=pl.ANY)] * 2,
        scratch_shapes=[
            pltpu.VMEM((4, HOURS, 2 * HALF), jnp.float32),
            pltpu.VMEM(shape, jnp.float32),
            pltpu.VMEM(shape, jnp.float32),
            pltpu.SemaphoreType.DMA((5,)),
        ],
        compiler_params=pltpu.CompilerParams(vmem_limit_bytes=9 * 2**20),
        cost_estimate=pl.CostEstimate(flops=0, bytes_accessed=4 * 2**20, transcendentals=0),
        name="finish",
    )(parts)


def hour_order(first, second):
    steps = jnp.arange(HOURS, dtype=jnp.int32)
    group, part, inner = steps // GROUP, steps // FINAL % SIDE, steps % FINAL
    return (first + group) % SIDE * GROUP + (second + part) % SIDE * FINAL + inner


def shards(coefficients, sky_year, hour_list, retention):
    me = lax.axis_index("patch")
    x, y, core = me // (2 * SIDE), me // 2 % SIDE, me % 2
    first, second = jnp.where(core == 0, x, y), jnp.where(core == 0, y, x)
    move = lambda value, pairs: lax.ppermute(value, "patch", pairs)
    first_up, first_down = ring(1, False), ring(-1, False)

    chip = jnp.arange(SIDE * SIDE, dtype=jnp.int32)
    one, two = chip // SIDE, chip % SIDE
    chips = jnp.where(
        core == 0,
        (x - one) % SIDE + SIDE * ((y - two) % SIDE),
        (y - two) % SIDE + SIDE * ((x - one) % SIDE),
    )

    spot = core.reshape(1)
    coefficients = pltpu.with_memory_space_constraint(coefficients, pltpu.HBM)
    sky_year = pltpu.with_memory_space_constraint(sky_year, pltpu.HBM)
    own_rates = lax.dynamic_slice(retention, (0, core * HALF), (4, HALF))
    message, own_sky = prepare(spot, hour_list[None, :], retention, coefficients, sky_year)
    others = [move(message, siblings), move(split(spot, coefficients), siblings)]
    half = PATCHES // 2
    extra = others[0][half:].reshape(2 * PIECE, HALF)
    sky = jnp.concatenate([own_sky[:, :HOURS], extra[:half, :HOURS]], axis=0).T
    digits_of = extra[half + 8 : half + 20].astype(jnp.float32)
    sibling_rates = digits_of[0:4] + (digits_of[4:8] + digits_of[8:12])
    rates = jnp.where(
        core == 0,
        jnp.concatenate([own_rates, sibling_rates]),
        jnp.concatenate([sibling_rates, own_rates]),
    )
    order = hour_order(first, second)[:, None]

    rendered = []
    for piece in range(PIECES):
        up, down, *kept = render(piece, spot, order, sky, rates, coefficients, others[piece])
        rendered.append((move(up, first_up), move(down, first_down), *kept))
    merged = []
    for up, down, keep_up, keep_down, mine in rendered:
        relay_up, relay_down = merge(keep_up, keep_down, up, down)
        merged.append((mine, up, down, move(relay_up, first_up), move(relay_down, first_down)))
    *sent, mine, coded_rates = join(0, rates, *merged[0])
    got = [move(part, ring(hop, True)) for hop, part in zip((1, 2, 3), sent)]
    above = upper(chips, coded_rates, *got, mine)
    *sent, mine = join(1, rates, *merged[1])
    got = [move(part, ring(hop, True)) for hop, part in zip((1, 2, 3), sent)]
    parts = glare(chips, *above, *got, mine)
    parts = lax.all_to_all(parts, "patch", 0, 0, tiled=True)
    return tuple(finish(parts))


def solution(mesh):
    placed = (P("view", "patch", None, None), P("patch", None), P(), P("patch", None))
    return jax.shard_map(
        shards,
        mesh=mesh,
        in_specs=placed,
        out_specs=(P("patch", "view", None, None), P("patch", "view", None, None)),
        check_vma=False,
    )
```

```python
import functools

import jax
import jax.numpy as jnp
from jax import lax
from jax.experimental import pallas as pl
from jax.experimental.pallas import tpu as pltpu
from jax.sharding import PartitionSpec as P

taps = (0.0625, 0.25, 0.375, 0.25, 0.0625)

SIDE = 4
ROWS = 128
HALF = 256
HOURS = 96
GROUP = HOURS // SIDE
FINAL = GROUP // SIDE
PATCHES = 144
BLOCK = 16
PIECES = 2
PIECE = ROWS // PIECES
PART = PIECE // 2 * GROUP
PAIR = 2 * GROUP
STEPS = 64.0
TOP = 32752.0
FLOOR = 2.0**-100
CHUNK = 56
CHIP_ROWS = 8
RATES = 3 * CHIP_ROWS
SENT = 2 * PART + PAIR + RATES + 8
SECOND = PIECE * FINAL + 16
FIRST = SECOND + SIDE * RATES


def place(x, y, core):
    return ((x % SIDE) * SIDE + y % SIDE) * 2 + core


def ring(hop, second):
    pairs = []
    for x in range(SIDE):
        for y in range(SIDE):
            for core in range(2):
                along_x = (core == 0) != second
                target = place(x + hop, y, core) if along_x else place(x, y + hop, core)
                pairs.append((place(x, y, core), target))
    return pairs


siblings = [(i, i ^ 1) for i in range(2 * SIDE * SIDE)]


def level_of(biggest):
    return jnp.ceil(STEPS * jnp.log2(jnp.maximum(biggest, FLOOR)))


def factor_of(level):
    return TOP * jnp.exp2(level * (-1.0 / STEPS))


def unit_of(level):
    return jnp.exp2(level * (1.0 / STEPS)) * (1.0 / TOP)


def coded(values, factor):
    return jnp.round(values * factor).astype(jnp.int32).astype(jnp.int16)


def wide(block):
    return block.astype(jnp.int32).astype(jnp.float32)


def narrow(block):
    return block.astype(jnp.int32).astype(jnp.int16)


def digits(rates):
    rest, parts = rates, []
    for _ in range(3):
        rest = rest * 32768.0
        part = jnp.minimum(jnp.floor(rest), 32767.0)
        rest = rest - part
        parts.append(part)
    return jnp.concatenate(parts, axis=0)


def undigits(lines):
    first, second, third = [lines[k * CHIP_ROWS : (k + 1) * CHIP_ROWS] for k in range(3)]
    return (first + (second + third * 2.0**-15) * 2.0**-15) * 2.0**-15


def twice(block):
    return jnp.concatenate([block, block], axis=0)


def lines_at(index, count):
    return pl.ds(pl.multiple_of(index * count, count), count)


def cut_copies(piece, core, source, held, out, sems):
    columns = pl.ds(pl.multiple_of((1 - core[0]) * HALF, HALF), HALF)
    copies = []
    for index in range(8):
        patches = pl.ds(index * (PATCHES // 16), PATCHES // 16)
        part = source.at[0, patches, pl.ds(piece * PIECE, PIECE), columns]
        copies.append(
            (
                pltpu.make_async_copy(part, held.at[patches], sems.at[0, index]),
                pltpu.make_async_copy(held.at[patches], out.at[patches], sems.at[1, index]),
            )
        )
    for copy, _ in copies:
        copy.start()
    return copies


def split_kernel(core, source, out, held, sems):
    copies = cut_copies(1, core, source, held, out, sems)
    for copy, onward in copies:
        copy.wait()
        onward.start()
    for _, onward in copies:
        onward.wait()


def prepare_kernel(
    core,
    hour_list,
    retention,
    source,
    sky_year,
    out,
    own_sky,
    held,
    hours,
    rates,
    table,
    padded,
    sems,
    more,
):
    fetches = [
        pltpu.make_async_copy(arg, copy, more.at[index])
        for index, (arg, copy) in enumerate(
            ((hour_list, hours), (retention, rates), (sky_year, table))
        )
    ]
    for fetch in fetches:
        fetch.start()
    copies = cut_copies(0, core, source, held, out, sems)
    fetches[0].wait()
    hour = lax.broadcasted_iota(jnp.int32, (table.shape[1], HOURS), 0)
    chosen = jnp.where(hour == hours[...], 1.0, 0.0).astype(jnp.bfloat16)
    padded[...] = jnp.zeros_like(padded)
    for copy, onward in copies:
        copy.wait()
        onward.start()
    for fetch in fetches[1:]:
        fetch.wait()
    padded[:, :HOURS] = jnp.dot(table[...], chosen, preferred_element_type=jnp.float32)
    sky = padded[...]
    own_sky[...] = sky.astype(jnp.bfloat16)
    rest, parts = jnp.where(core[0] == 0, rates[:, HALF:], rates[:, :HALF]), []
    for _ in range(3):
        part = rest.astype(jnp.bfloat16).astype(jnp.float32)
        rest = rest - part
        parts.append(part)
    gap = jnp.zeros((8, HALF), jnp.float32)
    tail_lines = jnp.concatenate([sky[PIECE:], gap] + parts + [gap[:4]] + [gap] * 4, axis=0)
    half = PATCHES // 2
    held[half] = sky[:PIECE].astype(jnp.bfloat16)
    held[half + 1] = tail_lines.astype(jnp.bfloat16)
    extra = pltpu.make_async_copy(held.at[half : half + 2], out.at[half : half + 2], more.at[3])
    extra.start()
    for _, onward in copies:
        onward.wait()
    extra.wait()


def split(core, coefficients):
    shape = (PATCHES // 2, PIECE, HALF)
    return pl.pallas_call(
        split_kernel,
        out_shape=jax.ShapeDtypeStruct(shape, jnp.bfloat16),
        in_specs=[pl.BlockSpec(memory_space=pltpu.SMEM), pl.BlockSpec(memory_space=pl.ANY)],
        out_specs=pl.BlockSpec(memory_space=pl.ANY),
        scratch_shapes=[pltpu.VMEM(shape, jnp.bfloat16), pltpu.SemaphoreType.DMA((2, 8))],
        compiler_params=pltpu.CompilerParams(vmem_limit_bytes=4 * 2**20),
        cost_estimate=pl.CostEstimate(flops=0, bytes_accessed=5 * 2**20, transcendentals=0),
        name="split",
    )(core, coefficients)


def prepare(core, *operands):
    half = PATCHES // 2
    hours, rates, _, table = operands
    shape = (half + 2, PIECE, HALF)
    return pl.pallas_call(
        prepare_kernel,
        out_shape=[
            jax.ShapeDtypeStruct(shape, jnp.bfloat16),
            jax.ShapeDtypeStruct((half, HALF), jnp.bfloat16),
        ],
        in_specs=[pl.BlockSpec(memory_space=pltpu.SMEM)] + [pl.BlockSpec(memory_space=pl.ANY)] * 4,
        out_specs=[pl.BlockSpec(memory_space=pl.ANY), pl.BlockSpec(memory_space=pltpu.VMEM)],
        scratch_shapes=[
            pltpu.VMEM(shape, jnp.bfloat16),
            pltpu.VMEM(hours.shape, hours.dtype),
            pltpu.VMEM(rates.shape, rates.dtype),
            pltpu.VMEM(table.shape, jnp.bfloat16),
            pltpu.VMEM((half, HALF), jnp.float32),
            pltpu.SemaphoreType.DMA((2, 8)),
            pltpu.SemaphoreType.DMA((4,)),
        ],
        compiler_params=pltpu.CompilerParams(vmem_limit_bytes=16 * 2**20),
        cost_estimate=pl.CostEstimate(flops=0, bytes_accessed=6 * 2**20, transcendentals=0),
        name="prepare",
    )(core, *operands)


def render_kernel(
    core, order, sky, rates, own, other, up, down, keep_up, keep_down, mine, images, peaks, ordered
):
    step = pl.program_id(0)

    @pl.when(step == 0)
    def _():
        hour = lax.broadcasted_iota(jnp.int32, (HOURS, HOURS), 1)
        chosen = jnp.where(order[...] == hour, 1.0, 0.0).astype(jnp.bfloat16)
        sorted_sky = jnp.dot(chosen, sky[...], preferred_element_type=jnp.float32)
        ordered[...] = sorted_sky.astype(jnp.bfloat16)
        peaks[...] = jnp.zeros_like(peaks)

    patches = jnp.concatenate([own[...], other[...]], axis=0)
    by_row = jnp.swapaxes(patches, 0, 1)
    rows_seen = ordered[...]
    peak = jnp.zeros((HOURS, HALF), jnp.float32)
    for row in range(BLOCK):
        image = jnp.dot(rows_seen, by_row[row], preferred_element_type=jnp.float32)
        peak = jnp.maximum(peak, jnp.abs(image))
        images[lines_at(step * BLOCK + row, HOURS), :] = image
        mine[lines_at(step * BLOCK + row, GROUP), :] = image[:GROUP]
    half = step // (PIECE // BLOCK // 2)
    peaks[half] = jnp.maximum(peaks[half], peak)

    @pl.when(step == pl.num_programs(0) - 1)
    def _():
        for out, parts in ((up, ((2, 0), (1, 1))), (down, ((2, 1), (3, 0)))):
            levels = []
            for index, (group, half) in enumerate(parts):
                hours = slice(group * GROUP, (group + 1) * GROUP)
                level = level_of(peaks[half, hours, :])
                factor = factor_of(level)
                levels.append(level)
                first = half * (PIECE // 2)

                def pair_step(pair, carry):
                    for k in range(2):
                        start = (first + 2 * pair + k) * HOURS + group * GROUP
                        start = pl.multiple_of(start, GROUP)
                        tile = images[pl.ds(start, GROUP), :] * factor
                        carry = carry + (jnp.round(tile).astype(jnp.int32),)
                    at = pl.multiple_of(index * PART + pair * PAIR, PAIR)
                    out[pl.ds(at, PAIR), :] = jnp.concatenate(carry, axis=0).astype(jnp.int16)
                    return ()

                lax.fori_loop(0, PIECE // 4, pair_step, (), unroll=2)
            pad = jnp.zeros((8, HALF), jnp.float32)
            last = jnp.concatenate(levels + [digits(rates[...]), pad], axis=0)
            out[2 * PART :, :] = narrow(last)
        for out, group, half in ((keep_up, 1, 0), (keep_down, 3, 1)):

            def keep_step(row, carry):
                start = (half * (PIECE // 2) + row) * HOURS + group * GROUP
                out[lines_at(row, GROUP), :] = images[pl.ds(pl.multiple_of(start, GROUP), GROUP), :]
                return carry

            lax.fori_loop(0, PIECE // 2, keep_step, 0, unroll=4)


def render(piece, core, order, sky, rates, own, other):
    whole = lambda i, core: (0, 0)
    steps = PIECE // BLOCK
    sent = jax.ShapeDtypeStruct((SENT, HALF), jnp.int16)
    kept = jax.ShapeDtypeStruct((PART, HALF), jnp.float32)
    outs = [sent, sent, kept, kept, jax.ShapeDtypeStruct((2 * PART, HALF), jnp.float32)]
    return pl.pallas_call(
        render_kernel,
        grid_spec=pltpu.PrefetchScalarGridSpec(
            num_scalar_prefetch=1,
            grid=(steps,),
            in_specs=[
                pl.BlockSpec((HOURS, 1), whole),
                pl.BlockSpec((HOURS, PATCHES), whole),
                pl.BlockSpec((CHIP_ROWS, HALF), whole),
                pl.BlockSpec(
                    (None, PATCHES // 2, BLOCK, HALF),
                    lambda i, core: (0, 0, piece * steps + i, core[0]),
                ),
                pl.BlockSpec((PATCHES // 2, BLOCK, HALF), lambda i, core: (0, i, 0)),
            ],
            out_specs=[pl.BlockSpec(out.shape, whole) for out in outs],
            scratch_shapes=[
                pltpu.VMEM((HOURS * PIECE, HALF), jnp.float32),
                pltpu.VMEM((2, HOURS, HALF), jnp.float32),
                pltpu.VMEM((HOURS, PATCHES), jnp.bfloat16),
            ],
        ),
        out_shape=outs,
        compiler_params=pltpu.CompilerParams(vmem_limit_bytes=16 * 2**20),
        cost_estimate=pl.CostEstimate(
            flops=2 * PATCHES * HOURS * PIECE * HALF, bytes_accessed=18 * 2**20, transcendentals=0
        ),
        name="render",
    )(core, order, sky, rates, own, other)


def in_vmem(kernel, outs, scratch, name, cost, operands, scalars=0):
    spaces = [pltpu.SMEM] * scalars + [pltpu.VMEM] * (len(operands) - scalars)
    return pl.pallas_call(
        kernel,
        out_shape=outs,
        in_specs=[pl.BlockSpec(memory_space=space) for space in spaces],
        out_specs=jax.tree.map(lambda out: pl.BlockSpec(memory_space=pltpu.VMEM), outs),
        scratch_shapes=scratch,
        compiler_params=pltpu.CompilerParams(vmem_limit_bytes=9 * 2**20),
        cost_estimate=pl.CostEstimate(flops=0, bytes_accessed=cost * 2**20, transcendentals=0),
        name=name,
    )(*operands)


def merge_kernel(keep_up, keep_down, got_up, got_down, up, down, total):
    nothing = jnp.zeros((PAIR, HALF), jnp.float32)
    for keep, got, out in ((keep_up, got_up, up), (keep_down, got_down, down)):
        last = wide(got[2 * PART :, :])
        unit = twice(unit_of(last[:GROUP]))

        def add_step(pair, peak):
            at = lines_at(pair, PAIR)
            tile = keep[at, :] + wide(got[at, :]) * unit
            total[at, :] = tile
            return jnp.maximum(peak, jnp.abs(tile))

        peak = lax.fori_loop(0, PART // PAIR, add_step, nothing, unroll=2)
        level = level_of(jnp.maximum(peak[:GROUP], peak[GROUP:]))
        factor = twice(factor_of(level))

        def code_step(pair, carry):
            at = lines_at(pair, PAIR)
            out[at, :] = coded(total[at, :], factor)
            return carry

        lax.fori_loop(0, PART // PAIR, code_step, 0, unroll=2)
        out[PART:, :] = narrow(jnp.concatenate([level, last[PAIR : PAIR + RATES]], axis=0))


def merge(keep_up, keep_down, got_up, got_down):
    sent = jax.ShapeDtypeStruct((PART + GROUP + RATES, HALF), jnp.int16)
    scratch = [pltpu.VMEM((PART, HALF), jnp.float32)]
    return in_vmem(
        merge_kernel, [sent, sent], scratch, "merge", 5, (keep_up, keep_down, got_up, got_down)
    )


def join_kernel(piece, *refs):
    if piece:
        mine, got_up, got_down, up, down, near, far, back, own, total = refs
    else:
        rates, mine, got_up, got_down, up, down, near, far, back, own, own_rates, total = refs
    peak = jnp.zeros((PAIR, HALF), jnp.float32)
    for half, (direct, relayed) in enumerate(((got_down, up), (got_up, down))):
        direct_unit = twice(unit_of(wide(direct[2 * PART :, :])[GROUP:PAIR]))
        relayed_unit = twice(unit_of(wide(relayed[PART:, :])[:GROUP]))

        def add_step(pair, peak):
            at = lines_at(pair, PAIR)
            direct_at = pl.ds(pl.multiple_of(PART + pair * PAIR, PAIR), PAIR)
            out_at = pl.ds(pl.multiple_of(half * PART + pair * PAIR, PAIR), PAIR)
            tile = mine[out_at, :] + wide(direct[direct_at, :]) * direct_unit
            tile = tile + wide(relayed[at, :]) * relayed_unit
            total[out_at, :] = tile
            return jnp.maximum(peak, jnp.abs(tile))

        peak = lax.fori_loop(0, PART // PAIR, add_step, peak, unroll=2)
    level = level_of(jnp.maximum(peak[:GROUP], peak[GROUP:]))
    factor = factor_of(level)
    outs = (own, near, far, back)
    factors = [
        jnp.concatenate([factor[part * FINAL : (part + 1) * FINAL]] * 8, axis=0)
        for part in range(SIDE)
    ]


    def split_step(eight, carry):
        tile = total[lines_at(eight, 8 * GROUP), :]
        for part, out in enumerate(outs):
            starts = [k * GROUP + part * FINAL for k in range(8)]
            block = jnp.concatenate([tile[at : at + FINAL] for at in starts], axis=0)
            if part:
                out[lines_at(eight, 8 * FINAL), :] = coded(block, factors[part])
            else:
                out[lines_at(eight, 8 * FINAL), :] = block
        return carry

    lax.fori_loop(0, PIECE // 8, split_step, 0)
    for part, out in enumerate(outs):
        if part:
            first = PIECE * FINAL
            mark = level[part * FINAL : (part + 1) * FINAL]
            rest = jnp.zeros((16 - FINAL, HALF), jnp.float32)
            out[first : first + 16, :] = narrow(jnp.concatenate([mark, rest], axis=0))
    if not piece:
        places = ((got_up, 2 * PART, PAIR), (up, PART, GROUP), (got_down, 2 * PART, PAIR))
        ahead = [wide(got[start:, :])[at : at + RATES] for got, start, at in places]
        all_rates = narrow(jnp.concatenate([digits(rates[...])] + ahead, axis=0))
        for out in (near, far, back):
            out[PIECE * FINAL + 16 :, :] = all_rates
        own_rates[...] = all_rates


def join(piece, rates, *operands):
    sent = jax.ShapeDtypeStruct((SECOND if piece else FIRST, HALF), jnp.int16)
    outs = [sent] * 3 + [jax.ShapeDtypeStruct((PIECE * FINAL, HALF), jnp.float32)]
    if not piece:
        operands = (rates,) + operands
        outs.append(jax.ShapeDtypeStruct((SIDE * RATES, HALF), jnp.int16))
    scratch = [pltpu.VMEM((2 * PART, HALF), jnp.float32)]
    return in_vmem(functools.partial(join_kernel, piece), outs, scratch, "join", 6, operands)


def spots(eight, k):
    return pl.ds(pl.multiple_of(64 * eight, 64) + 8 * k, FINAL)


def run_down(piece, chips, rates, own, gots, lines, front, state):
    size = PIECE * FINAL
    units = [unit_of(wide(got[size:SECOND, :])[:FINAL]) for got in gots]
    units = [jnp.concatenate([unit] * 8, axis=0) for unit in units]

    def down(index, state):
        at = lines_at(index, 8 * FINAL)
        tile = own[at, :]
        for got, unit in zip(gots, units):
            tile = tile + wide(got[at, :]) * unit
        share = rates[lines_at(chips[piece * (PIECE // 8) + index], 8), :]
        for k in range(8):
            light = tile[k * FINAL : (k + 1) * FINAL]
            state = share[k : k + 1] * state + light
            lines[spots(index, k), :] = light
            front[spots(index, k), :] = state
        return state

    return lax.fori_loop(0, PIECE // 8, down, state)


def upper_kernel(chips, own_rates, near, far, back, mine, rates, lines, front, last):
    blocks = [own_rates] + [got.at[SECOND:FIRST] for got in (near, far, back)]
    for behind, block in enumerate(blocks):
        coded_rates = wide(block[...])
        for chip in range(SIDE):
            start = (behind * SIDE + chip) * CHIP_ROWS
            rates[start : start + CHIP_ROWS, :] = undigits(
                coded_rates[chip * RATES : (chip + 1) * RATES]
            )
    state = jnp.zeros((FINAL, HALF), jnp.float32)
    gots = (near, far, back)
    last[0:FINAL, :] = run_down(0, chips, rates, mine, gots, lines, front, state)


def upper(chips, *operands):
    rows = jax.ShapeDtypeStruct((8 * PIECE, HALF), jnp.float32)
    outs = [
        jax.ShapeDtypeStruct((ROWS, HALF), jnp.float32),
        rows,
        rows,
        jax.ShapeDtypeStruct((8, HALF), jnp.float32),
    ]
    return in_vmem(upper_kernel, outs, [], "upper", 4, (chips, *operands), scalars=1)


def glare_kernel(
    chips, rates, first_lines, first_front, last, near, far, back, mine, out, lines, front
):
    lines[0:16, :] = jnp.zeros((16, HALF), jnp.float32)
    lines[8 * (ROWS + 2) :, :] = jnp.zeros((16, HALF), jnp.float32)
    lines[16 : 16 + 8 * PIECE, :] = first_lines[...]
    front[: 8 * PIECE, :] = first_front[...]
    rest = slice(16 + 8 * PIECE, 16 + 8 * ROWS)
    run_down(
        1,
        chips,
        rates,
        mine,
        (near, far, back),
        lines.at[rest],
        front.at[8 * PIECE :],
        last[0:FINAL, :],
    )
    nothing = jnp.zeros((FINAL, HALF), jnp.float32)

    def up(step, state):
        eight = ROWS // 8 - 1 - step
        share = rates[lines_at(chips[eight], 8), :]
        light = [lines[spots(eight, k), :] for k in range(12)]
        for owner in (1, 0):
            veils, blurs = [None] * 4, [None] * 4
            for k in (3, 2, 1, 0):
                row = owner * 4 + k
                state = share[row : row + 1] * state + light[row + 2]
                veils[k] = 0.125 * (front[spots(eight, row), :] + state)
                near, wider = light[row + 1] + light[row + 3], light[row] + light[row + 4]
                blurs[k] = taps[2] * light[row + 2] + taps[1] * near + taps[0] * wider
            blocks, levels = [], []
            for values in (blurs, veils):
                block = jnp.concatenate(values, axis=0)
                level = level_of(jnp.max(jnp.abs(block), axis=0, keepdims=True))
                blocks.append(jnp.round(block * factor_of(level)))
                levels.append(level)
            rest = jnp.zeros((CHUNK - 8 * FINAL - 2, HALF), jnp.float32)
            out[2 * eight + owner] = narrow(jnp.concatenate(blocks + levels + [rest], axis=0))
        return state

    lax.fori_loop(0, ROWS // 8, up, nothing)


def glare(chips, *operands):
    out = jax.ShapeDtypeStruct((32, CHUNK, HALF), jnp.int16)
    scratch = [
        pltpu.VMEM((8 * (ROWS + 4), HALF), jnp.float32),
        pltpu.VMEM((8 * ROWS, HALF), jnp.float32),
    ]
    return in_vmem(glare_kernel, out, scratch, "glare", 8, (chips, *operands), scalars=1)


def finish_kernel(parts, acuity, veil, blurred, glares, finished, sems):
    for source in range(32):
        x, y, core = source // 8, source // 2 % 4, source % 2
        first, second = (x, y) if core == 0 else (y, x)
        hour = first * GROUP + second * FINAL
        columns = slice(core * HALF, (core + 1) * HALF)
        block = wide(parts[source])
        units = unit_of(block[8 * FINAL : 8 * FINAL + 2])
        for row in range(4):
            at = row * FINAL
            blurred[row, hour : hour + FINAL, columns] = block[at : at + FINAL] * units[0:1]
            at = (row + 4) * FINAL
            glares[row, 0, hour : hour + FINAL, columns] = block[at : at + FINAL] * units[1:2]
    copies = [pltpu.make_async_copy(glares, veil, sems.at[4])]
    copies[0].start()
    column = lax.broadcasted_iota(jnp.int32, (HOURS, 2 * HALF), 1)
    for row in range(4):
        image = blurred[row]
        total = taps[2] * image
        for offset in (-2, -1, 1, 2):
            moved = pltpu.roll(image, (-offset) % (2 * HALF), 1)
            inside = (column + offset >= 0) & (column + offset < 2 * HALF)
            total = total + taps[2 + offset] * jnp.where(inside, moved, 0.0)
        finished[row, 0] = total
        copies.append(pltpu.make_async_copy(finished.at[row], acuity.at[row], sems.at[row]))
        copies[-1].start()
    for copy in copies:
        copy.wait()


def finish(parts):
    shape = (4, 1, HOURS, 2 * HALF)
    return pl.pallas_call(
        finish_kernel,
        out_shape=[pltpu.HBM(shape, jnp.float32)] * 2,
        in_specs=[pl.BlockSpec(memory_space=pltpu.VMEM)],
        out_specs=[pl.BlockSpec(memory_space=pl.ANY)] * 2,
        scratch_shapes=[
            pltpu.VMEM((4, HOURS, 2 * HALF), jnp.float32),
            pltpu.VMEM(shape, jnp.float32),
            pltpu.VMEM(shape, jnp.float32),
            pltpu.SemaphoreType.DMA((5,)),
        ],
        compiler_params=pltpu.CompilerParams(vmem_limit_bytes=9 * 2**20),
        cost_estimate=pl.CostEstimate(flops=0, bytes_accessed=4 * 2**20, transcendentals=0),
        name="finish",
    )(parts)


def hour_order(first, second):
    steps = jnp.arange(HOURS, dtype=jnp.int32)
    group, part, inner = steps // GROUP, steps // FINAL % SIDE, steps % FINAL
    return (first + group) % SIDE * GROUP + (second + part) % SIDE * FINAL + inner


def shards(coefficients, sky_year, hour_list, retention):
    me = lax.axis_index("patch")
    x, y, core = me // (2 * SIDE), me // 2 % SIDE, me % 2
    first, second = jnp.where(core == 0, x, y), jnp.where(core == 0, y, x)
    move = lambda value, pairs: lax.ppermute(value, "patch", pairs)
    first_up, first_down = ring(1, False), ring(-1, False)

    chip = jnp.arange(SIDE * SIDE, dtype=jnp.int32)
    one, two = chip // SIDE, chip % SIDE
    chips = jnp.where(
        core == 0,
        (x - one) % SIDE + SIDE * ((y - two) % SIDE),
        (y - two) % SIDE + SIDE * ((x - one) % SIDE),
    )

    spot = core.reshape(1)
    coefficients = pltpu.with_memory_space_constraint(coefficients, pltpu.HBM)
    sky_year = pltpu.with_memory_space_constraint(sky_year, pltpu.HBM)
    own_rates = lax.dynamic_slice(retention, (0, core * HALF), (4, HALF))
    hours, given = [
        pltpu.with_memory_space_constraint(arg, pltpu.HBM) for arg in (hour_list[None, :], retention)
    ]
    message, own_sky = prepare(spot, hours, given, coefficients, sky_year)
    others = [move(message, siblings), move(split(spot, coefficients), siblings)]
    half = PATCHES // 2
    extra = others[0][half:].reshape(2 * PIECE, HALF)
    sky = jnp.concatenate([own_sky[:, :HOURS], extra[:half, :HOURS]], axis=0).T
    digits_of = extra[half + 8 : half + 20].astype(jnp.float32)
    sibling_rates = digits_of[0:4] + (digits_of[4:8] + digits_of[8:12])
    rates = jnp.where(
        core == 0,
        jnp.concatenate([own_rates, sibling_rates]),
        jnp.concatenate([sibling_rates, own_rates]),
    )
    order = hour_order(first, second)[:, None]

    rendered = []
    for piece in range(PIECES):
        up, down, *kept = render(piece, spot, order, sky, rates, coefficients, others[piece])
        rendered.append((move(up, first_up), move(down, first_down), *kept))
    merged = []
    for up, down, keep_up, keep_down, mine in rendered:
        relay_up, relay_down = merge(keep_up, keep_down, up, down)
        merged.append((mine, up, down, move(relay_up, first_up), move(relay_down, first_down)))
    *sent, mine, coded_rates = join(0, rates, *merged[0])
    got = [move(part, ring(hop, True)) for hop, part in zip((1, 2, 3), sent)]
    above = upper(chips, coded_rates, *got, mine)
    *sent, mine = join(1, rates, *merged[1])
    got = [move(part, ring(hop, True)) for hop, part in zip((1, 2, 3), sent)]
    parts = glare(chips, *above, *got, mine)
    parts = lax.all_to_all(parts, "patch", 0, 0, tiled=True)
    return tuple(finish(parts))


def solution(mesh):
    placed = (P("view", "patch", None, None), P("patch", None), P(), P("patch", None))
    return jax.shard_map(
        shards,
        mesh=mesh,
        in_specs=placed,
        out_specs=(P("patch", "view", None, None), P("patch", "view", None, None)),
        check_vma=False,
    )
```

```python
import functools

import jax
import jax.numpy as jnp
from jax import lax
from jax.experimental import pallas as pl
from jax.experimental.pallas import tpu as pltpu
from jax.sharding import PartitionSpec as P

taps = (0.0625, 0.25, 0.375, 0.25, 0.0625)

SIDE = 4
ROWS = 128
HALF = 256
HOURS = 96
GROUP = HOURS // SIDE
FINAL = GROUP // SIDE
PATCHES = 144
BLOCK = 16
PIECES = 2
PIECE = ROWS // PIECES
PART = PIECE // 2 * GROUP
PAIR = 2 * GROUP
STEPS = 64.0
TOP = 32752.0
FLOOR = 2.0**-100
CHUNK = 56
CHIP_ROWS = 8
RATES = 3 * CHIP_ROWS
SENT = 2 * PART + PAIR + RATES + 8
SECOND = PIECE * FINAL + 16
FIRST = SECOND + SIDE * RATES


def place(x, y, core):
    return ((x % SIDE) * SIDE + y % SIDE) * 2 + core


def ring(hop, second):
    pairs = []
    for x in range(SIDE):
        for y in range(SIDE):
            for core in range(2):
                along_x = (core == 0) != second
                target = place(x + hop, y, core) if along_x else place(x, y + hop, core)
                pairs.append((place(x, y, core), target))
    return pairs


siblings = [(i, i ^ 1) for i in range(2 * SIDE * SIDE)]


def level_of(biggest):
    return jnp.ceil(STEPS * jnp.log2(jnp.maximum(biggest, FLOOR)))


def factor_of(level):
    return TOP * jnp.exp2(level * (-1.0 / STEPS))


def unit_of(level):
    return jnp.exp2(level * (1.0 / STEPS)) * (1.0 / TOP)


def coded(values, factor):
    return jnp.round(values * factor).astype(jnp.int32).astype(jnp.int16)


def wide(block):
    return block.astype(jnp.int32).astype(jnp.float32)


def narrow(block):
    return block.astype(jnp.int32).astype(jnp.int16)


def digits(rates):
    rest, parts = rates, []
    for _ in range(3):
        rest = rest * 32768.0
        part = jnp.minimum(jnp.floor(rest), 32767.0)
        rest = rest - part
        parts.append(part)
    return jnp.concatenate(parts, axis=0)


def undigits(lines):
    first, second, third = [lines[k * CHIP_ROWS : (k + 1) * CHIP_ROWS] for k in range(3)]
    return (first + (second + third * 2.0**-15) * 2.0**-15) * 2.0**-15


def twice(block):
    return jnp.concatenate([block, block], axis=0)


def lines_at(index, count):
    return pl.ds(pl.multiple_of(index * count, count), count)


def cut_copies(piece, core, source, held, out, sems):
    columns = pl.ds(pl.multiple_of((1 - core[0]) * HALF, HALF), HALF)
    copies = []
    for index in range(8):
        patches = pl.ds(index * (PATCHES // 16), PATCHES // 16)
        part = source.at[0, patches, pl.ds(piece * PIECE, PIECE), columns]
        copies.append(
            (
                pltpu.make_async_copy(part, held.at[patches], sems.at[0, index]),
                pltpu.make_async_copy(held.at[patches], out.at[patches], sems.at[1, index]),
            )
        )
    for copy, _ in copies:
        copy.start()
    return copies


def split_kernel(core, source, out, held, sems):
    copies = cut_copies(1, core, source, held, out, sems)
    for copy, onward in copies:
        copy.wait()
        onward.start()
    for _, onward in copies:
        onward.wait()


def prepare_kernel(
    core,
    hour_list,
    retention,
    source,
    sky_year,
    out,
    own_sky,
    held,
    hours,
    rates,
    table,
    padded,
    sems,
    more,
):
    fetches = [
        pltpu.make_async_copy(arg, copy, more.at[index])
        for index, (arg, copy) in enumerate(
            ((hour_list, hours), (retention, rates), (sky_year, table))
        )
    ]
    for fetch in fetches:
        fetch.start()
    copies = cut_copies(0, core, source, held, out, sems)
    fetches[0].wait()
    hour = lax.broadcasted_iota(jnp.int32, (table.shape[1], HOURS), 0)
    chosen = jnp.where(hour == hours[...], 1.0, 0.0).astype(jnp.bfloat16)
    padded[...] = jnp.zeros_like(padded)
    for copy, onward in copies:
        copy.wait()
        onward.start()
    for fetch in fetches[1:]:
        fetch.wait()
    padded[:, :HOURS] = jnp.dot(table[...], chosen, preferred_element_type=jnp.float32)
    sky = padded[...]
    own_sky[...] = sky.astype(jnp.bfloat16)
    rest, parts = jnp.where(core[0] == 0, rates[:, HALF:], rates[:, :HALF]), []
    for _ in range(3):
        part = rest.astype(jnp.bfloat16).astype(jnp.float32)
        rest = rest - part
        parts.append(part)
    gap = jnp.zeros((8, HALF), jnp.float32)
    tail_lines = jnp.concatenate([sky[PIECE:], gap] + parts + [gap[:4]] + [gap] * 4, axis=0)
    half = PATCHES // 2
    held[half] = sky[:PIECE].astype(jnp.bfloat16)
    held[half + 1] = tail_lines.astype(jnp.bfloat16)
    extra = pltpu.make_async_copy(held.at[half : half + 2], out.at[half : half + 2], more.at[3])
    extra.start()
    for _, onward in copies:
        onward.wait()
    extra.wait()


def split(core, coefficients):
    shape = (PATCHES // 2, PIECE, HALF)
    return pl.pallas_call(
        split_kernel,
        out_shape=jax.ShapeDtypeStruct(shape, jnp.bfloat16),
        in_specs=[pl.BlockSpec(memory_space=pltpu.SMEM), pl.BlockSpec(memory_space=pl.ANY)],
        out_specs=pl.BlockSpec(memory_space=pl.ANY),
        scratch_shapes=[pltpu.VMEM(shape, jnp.bfloat16), pltpu.SemaphoreType.DMA((2, 8))],
        compiler_params=pltpu.CompilerParams(vmem_limit_bytes=4 * 2**20),
        cost_estimate=pl.CostEstimate(flops=0, bytes_accessed=5 * 2**20, transcendentals=0),
        name="split",
    )(core, coefficients)


def prepare(core, *operands):
    half = PATCHES // 2
    hours, rates, _, table = operands
    shape = (half + 2, PIECE, HALF)
    return pl.pallas_call(
        prepare_kernel,
        out_shape=[
            jax.ShapeDtypeStruct(shape, jnp.bfloat16),
            jax.ShapeDtypeStruct((half, HALF), jnp.bfloat16),
        ],
        in_specs=[pl.BlockSpec(memory_space=pltpu.SMEM)] + [pl.BlockSpec(memory_space=pl.ANY)] * 4,
        out_specs=[pl.BlockSpec(memory_space=pl.ANY), pl.BlockSpec(memory_space=pltpu.VMEM)],
        scratch_shapes=[
            pltpu.VMEM(shape, jnp.bfloat16),
            pltpu.VMEM(hours.shape, hours.dtype),
            pltpu.VMEM(rates.shape, rates.dtype),
            pltpu.VMEM(table.shape, jnp.bfloat16),
            pltpu.VMEM((half, HALF), jnp.float32),
            pltpu.SemaphoreType.DMA((2, 8)),
            pltpu.SemaphoreType.DMA((4,)),
        ],
        compiler_params=pltpu.CompilerParams(vmem_limit_bytes=16 * 2**20),
        cost_estimate=pl.CostEstimate(flops=0, bytes_accessed=6 * 2**20, transcendentals=0),
        name="prepare",
    )(core, *operands)


def render_kernel(
    core, order, sky, rates, own, other, up, down, keep_up, keep_down, mine, images, peaks, ordered
):
    step = pl.program_id(0)

    @pl.when(step == 0)
    def _():
        hour = lax.broadcasted_iota(jnp.int32, (HOURS, HOURS), 1)
        chosen = jnp.where(order[...] == hour, 1.0, 0.0).astype(jnp.bfloat16)
        sorted_sky = jnp.dot(chosen, sky[...], preferred_element_type=jnp.float32)
        ordered[...] = sorted_sky.astype(jnp.bfloat16)
        peaks[...] = jnp.zeros_like(peaks)

    patches = jnp.concatenate([own[...], other[...]], axis=0)
    by_row = jnp.swapaxes(patches, 0, 1)
    rows_seen = ordered[...]
    peak = jnp.zeros((HOURS, HALF), jnp.float32)
    for row in range(BLOCK):
        image = jnp.dot(rows_seen, by_row[row], preferred_element_type=jnp.float32)
        peak = jnp.maximum(peak, jnp.abs(image))
        images[lines_at(step * BLOCK + row, HOURS), :] = image
        mine[lines_at(step * BLOCK + row, GROUP), :] = image[:GROUP]
    half = step // (PIECE // BLOCK // 2)
    peaks[half] = jnp.maximum(peaks[half], peak)

    @pl.when(step == pl.num_programs(0) - 1)
    def _():
        for out, parts in ((up, ((2, 0), (1, 1))), (down, ((2, 1), (3, 0)))):
            levels = []
            for index, (group, half) in enumerate(parts):
                hours = slice(group * GROUP, (group + 1) * GROUP)
                level = level_of(peaks[half, hours, :])
                factor = factor_of(level)
                levels.append(level)
                first = half * (PIECE // 2)

                def pair_step(pair, carry):
                    for k in range(2):
                        start = (first + 2 * pair + k) * HOURS + group * GROUP
                        start = pl.multiple_of(start, GROUP)
                        tile = images[pl.ds(start, GROUP), :] * factor
                        carry = carry + (jnp.round(tile).astype(jnp.int32),)
                    at = pl.multiple_of(index * PART + pair * PAIR, PAIR)
                    out[pl.ds(at, PAIR), :] = jnp.concatenate(carry, axis=0).astype(jnp.int16)
                    return ()

                lax.fori_loop(0, PIECE // 4, pair_step, (), unroll=2)
            pad = jnp.zeros((8, HALF), jnp.float32)
            last = jnp.concatenate(levels + [digits(rates[...]), pad], axis=0)
            out[2 * PART :, :] = narrow(last)
        for out, group, half in ((keep_up, 1, 0), (keep_down, 3, 1)):

            def keep_step(row, carry):
                start = (half * (PIECE // 2) + row) * HOURS + group * GROUP
                out[lines_at(row, GROUP), :] = images[pl.ds(pl.multiple_of(start, GROUP), GROUP), :]
                return carry

            lax.fori_loop(0, PIECE // 2, keep_step, 0, unroll=4)


def render(piece, core, order, sky, rates, own, other):
    whole = lambda i, core: (0, 0)
    steps = PIECE // BLOCK
    sent = jax.ShapeDtypeStruct((SENT, HALF), jnp.int16)
    kept = jax.ShapeDtypeStruct((PART, HALF), jnp.float32)
    outs = [sent, sent, kept, kept, jax.ShapeDtypeStruct((2 * PART, HALF), jnp.float32)]
    return pl.pallas_call(
        render_kernel,
        grid_spec=pltpu.PrefetchScalarGridSpec(
            num_scalar_prefetch=1,
            grid=(steps,),
            in_specs=[
                pl.BlockSpec((HOURS, 1), whole),
                pl.BlockSpec((HOURS, PATCHES), whole),
                pl.BlockSpec((CHIP_ROWS, HALF), whole),
                pl.BlockSpec(
                    (None, PATCHES // 2, BLOCK, HALF),
                    lambda i, core: (0, 0, piece * steps + i, core[0]),
                ),
                pl.BlockSpec((PATCHES // 2, BLOCK, HALF), lambda i, core: (0, i, 0)),
            ],
            out_specs=[pl.BlockSpec(out.shape, whole) for out in outs],
            scratch_shapes=[
                pltpu.VMEM((HOURS * PIECE, HALF), jnp.float32),
                pltpu.VMEM((2, HOURS, HALF), jnp.float32),
                pltpu.VMEM((HOURS, PATCHES), jnp.bfloat16),
            ],
        ),
        out_shape=outs,
        compiler_params=pltpu.CompilerParams(vmem_limit_bytes=16 * 2**20),
        cost_estimate=pl.CostEstimate(
            flops=2 * PATCHES * HOURS * PIECE * HALF, bytes_accessed=18 * 2**20, transcendentals=0
        ),
        name="render",
    )(core, order, sky, rates, own, other)


def in_vmem(kernel, outs, scratch, name, cost, operands, scalars=0):
    spaces = [pltpu.SMEM] * scalars + [pltpu.VMEM] * (len(operands) - scalars)
    return pl.pallas_call(
        kernel,
        out_shape=outs,
        in_specs=[pl.BlockSpec(memory_space=space) for space in spaces],
        out_specs=jax.tree.map(lambda out: pl.BlockSpec(memory_space=pltpu.VMEM), outs),
        scratch_shapes=scratch,
        compiler_params=pltpu.CompilerParams(vmem_limit_bytes=9 * 2**20),
        cost_estimate=pl.CostEstimate(flops=0, bytes_accessed=cost * 2**20, transcendentals=0),
        name=name,
    )(*operands)


def merge_kernel(keep_up, keep_down, got_up, got_down, up, down, total):
    nothing = jnp.zeros((PAIR, HALF), jnp.float32)
    for keep, got, out in ((keep_up, got_up, up), (keep_down, got_down, down)):
        last = wide(got[2 * PART :, :])
        unit = twice(unit_of(last[:GROUP]))

        def add_step(pair, peak):
            at = lines_at(pair, PAIR)
            tile = keep[at, :] + wide(got[at, :]) * unit
            total[at, :] = tile
            return jnp.maximum(peak, jnp.abs(tile))

        peak = lax.fori_loop(0, PART // PAIR, add_step, nothing, unroll=2)
        level = level_of(jnp.maximum(peak[:GROUP], peak[GROUP:]))
        factor = twice(factor_of(level))

        def code_step(pair, carry):
            at = lines_at(pair, PAIR)
            out[at, :] = coded(total[at, :], factor)
            return carry

        lax.fori_loop(0, PART // PAIR, code_step, 0, unroll=2)
        out[PART:, :] = narrow(jnp.concatenate([level, last[PAIR : PAIR + RATES]], axis=0))


def merge(keep_up, keep_down, got_up, got_down):
    sent = jax.ShapeDtypeStruct((PART + GROUP + RATES, HALF), jnp.int16)
    scratch = [pltpu.VMEM((PART, HALF), jnp.float32)]
    return in_vmem(
        merge_kernel, [sent, sent], scratch, "merge", 5, (keep_up, keep_down, got_up, got_down)
    )


def join_kernel(piece, *refs):
    if piece:
        mine, got_up, got_down, up, down, near, far, back, own, total = refs
    else:
        rates, mine, got_up, got_down, up, down, near, far, back, own, own_rates, total = refs
    peak = jnp.zeros((PAIR, HALF), jnp.float32)
    for half, (direct, relayed) in enumerate(((got_down, up), (got_up, down))):
        direct_unit = twice(unit_of(wide(direct[2 * PART :, :])[GROUP:PAIR]))
        relayed_unit = twice(unit_of(wide(relayed[PART:, :])[:GROUP]))

        def add_step(pair, peak):
            at = lines_at(pair, PAIR)
            direct_at = pl.ds(pl.multiple_of(PART + pair * PAIR, PAIR), PAIR)
            out_at = pl.ds(pl.multiple_of(half * PART + pair * PAIR, PAIR), PAIR)
            tile = mine[out_at, :] + wide(direct[direct_at, :]) * direct_unit
            tile = tile + wide(relayed[at, :]) * relayed_unit
            total[out_at, :] = tile
            return jnp.maximum(peak, jnp.abs(tile))

        peak = lax.fori_loop(0, PART // PAIR, add_step, peak, unroll=2)
    level = level_of(jnp.maximum(peak[:GROUP], peak[GROUP:]))
    factor = factor_of(level)
    outs = (own, near, far, back)
    factors = [
        jnp.concatenate([factor[part * FINAL : (part + 1) * FINAL]] * 8, axis=0)
        for part in range(SIDE)
    ]


    def split_step(eight, carry):
        tile = total[lines_at(eight, 8 * GROUP), :]
        for part, out in enumerate(outs):
            starts = [k * GROUP + part * FINAL for k in range(8)]
            block = jnp.concatenate([tile[at : at + FINAL] for at in starts], axis=0)
            if part:
                out[lines_at(eight, 8 * FINAL), :] = coded(block, factors[part])
            else:
                out[lines_at(eight, 8 * FINAL), :] = block
        return carry

    lax.fori_loop(0, PIECE // 8, split_step, 0)
    for part, out in enumerate(outs):
        if part:
            first = PIECE * FINAL
            mark = level[part * FINAL : (part + 1) * FINAL]
            rest = jnp.zeros((16 - FINAL, HALF), jnp.float32)
            out[first : first + 16, :] = narrow(jnp.concatenate([mark, rest], axis=0))
    if not piece:
        places = ((got_up, 2 * PART, PAIR), (up, PART, GROUP), (got_down, 2 * PART, PAIR))
        ahead = [wide(got[start:, :])[at : at + RATES] for got, start, at in places]
        all_rates = narrow(jnp.concatenate([digits(rates[...])] + ahead, axis=0))
        for out in (near, far, back):
            out[PIECE * FINAL + 16 :, :] = all_rates
        own_rates[...] = all_rates


def join(piece, rates, *operands):
    sent = jax.ShapeDtypeStruct((SECOND if piece else FIRST, HALF), jnp.int16)
    outs = [sent] * 3 + [jax.ShapeDtypeStruct((PIECE * FINAL, HALF), jnp.float32)]
    if not piece:
        operands = (rates,) + operands
        outs.append(jax.ShapeDtypeStruct((SIDE * RATES, HALF), jnp.int16))
    scratch = [pltpu.VMEM((2 * PART, HALF), jnp.float32)]
    return in_vmem(functools.partial(join_kernel, piece), outs, scratch, "join", 6, operands)


def spots(eight, k):
    return pl.ds(pl.multiple_of(64 * eight, 64) + 8 * k, FINAL)


def run_down(piece, chips, rates, own, gots, lines, front, state):
    size = PIECE * FINAL
    units = [unit_of(wide(got[size:SECOND, :])[:FINAL]) for got in gots]
    units = [jnp.concatenate([unit] * 8, axis=0) for unit in units]

    def down(index, state):
        at = lines_at(index, 8 * FINAL)
        tile = own[at, :]
        for got, unit in zip(gots, units):
            tile = tile + wide(got[at, :]) * unit
        share = rates[lines_at(chips[piece * (PIECE // 8) + index], 8), :]
        for k in range(8):
            light = tile[k * FINAL : (k + 1) * FINAL]
            state = share[k : k + 1] * state + light
            lines[spots(index, k), :] = light
            front[spots(index, k), :] = state
        return state

    return lax.fori_loop(0, PIECE // 8, down, state)


def upper_kernel(chips, own_rates, near, far, back, mine, rates, lines, front, last):
    blocks = [own_rates] + [got.at[SECOND:FIRST] for got in (near, far, back)]
    for behind, block in enumerate(blocks):
        coded_rates = wide(block[...])
        for chip in range(SIDE):
            start = (behind * SIDE + chip) * CHIP_ROWS
            rates[start : start + CHIP_ROWS, :] = undigits(
                coded_rates[chip * RATES : (chip + 1) * RATES]
            )
    state = jnp.zeros((FINAL, HALF), jnp.float32)
    gots = (near, far, back)
    last[0:FINAL, :] = run_down(0, chips, rates, mine, gots, lines, front, state)


def upper(chips, *operands):
    rows = jax.ShapeDtypeStruct((8 * PIECE, HALF), jnp.float32)
    outs = [
        jax.ShapeDtypeStruct((ROWS, HALF), jnp.float32),
        rows,
        rows,
        jax.ShapeDtypeStruct((8, HALF), jnp.float32),
    ]
    return in_vmem(upper_kernel, outs, [], "upper", 4, (chips, *operands), scalars=1)


def glare_kernel(
    chips, rates, first_lines, first_front, last, near, far, back, mine, out, lines, front
):
    lines[0:16, :] = jnp.zeros((16, HALF), jnp.float32)
    lines[8 * (ROWS + 2) :, :] = jnp.zeros((16, HALF), jnp.float32)
    lines[16 : 16 + 8 * PIECE, :] = first_lines[...]
    front[: 8 * PIECE, :] = first_front[...]
    rest = slice(16 + 8 * PIECE, 16 + 8 * ROWS)
    run_down(
        1,
        chips,
        rates,
        mine,
        (near, far, back),
        lines.at[rest],
        front.at[8 * PIECE :],
        last[0:FINAL, :],
    )
    nothing = jnp.zeros((FINAL, HALF), jnp.float32)

    def up(step, state):
        eight = ROWS // 8 - 1 - step
        share = rates[lines_at(chips[eight], 8), :]
        light = [lines[spots(eight, k), :] for k in range(12)]
        for owner in (1, 0):
            veils, blurs = [None] * 4, [None] * 4
            for k in (3, 2, 1, 0):
                row = owner * 4 + k
                state = share[row : row + 1] * state + light[row + 2]
                veils[k] = 0.125 * (front[spots(eight, row), :] + state)
                near, wider = light[row + 1] + light[row + 3], light[row] + light[row + 4]
                blurs[k] = taps[2] * light[row + 2] + taps[1] * near + taps[0] * wider
            blocks, levels = [], []
            for values in (blurs, veils):
                block = jnp.concatenate(values, axis=0)
                level = level_of(jnp.max(jnp.abs(block), axis=0, keepdims=True))
                blocks.append(jnp.round(block * factor_of(level)))
                levels.append(level)
            rest = jnp.zeros((CHUNK - 8 * FINAL - 2, HALF), jnp.float32)
            out[2 * eight + owner] = narrow(jnp.concatenate(blocks + levels + [rest], axis=0))
        return state

    lax.fori_loop(0, ROWS // 8, up, nothing)


def glare(chips, *operands):
    out = jax.ShapeDtypeStruct((32, CHUNK, HALF), jnp.int16)
    scratch = [
        pltpu.VMEM((8 * (ROWS + 4), HALF), jnp.float32),
        pltpu.VMEM((8 * ROWS, HALF), jnp.float32),
    ]
    return in_vmem(glare_kernel, out, scratch, "glare", 8, (chips, *operands), scalars=1)


def finish_kernel(parts, acuity, veil, blurred, glares, finished, sems):
    for source in range(32):
        x, y, core = source // 8, source // 2 % 4, source % 2
        first, second = (x, y) if core == 0 else (y, x)
        hour = first * GROUP + second * FINAL
        columns = slice(core * HALF, (core + 1) * HALF)
        block = wide(parts[source])
        units = unit_of(block[8 * FINAL : 8 * FINAL + 2])
        for row in range(4):
            at = row * FINAL
            blurred[row, hour : hour + FINAL, columns] = block[at : at + FINAL] * units[0:1]
            at = (row + 4) * FINAL
            glares[row, 0, hour : hour + FINAL, columns] = block[at : at + FINAL] * units[1:2]
    copies = [pltpu.make_async_copy(glares, veil, sems.at[4])]
    copies[0].start()
    column = lax.broadcasted_iota(jnp.int32, (HOURS, 2 * HALF), 1)
    for row in range(4):
        image = blurred[row]
        total = taps[2] * image
        for offset in (-2, -1, 1, 2):
            moved = pltpu.roll(image, (-offset) % (2 * HALF), 1)
            inside = (column + offset >= 0) & (column + offset < 2 * HALF)
            total = total + taps[2 + offset] * jnp.where(inside, moved, 0.0)
        finished[row, 0] = total
        copies.append(pltpu.make_async_copy(finished.at[row], acuity.at[row], sems.at[row]))
        copies[-1].start()
    for copy in copies:
        copy.wait()


def finish(parts):
    shape = (4, 1, HOURS, 2 * HALF)
    return pl.pallas_call(
        finish_kernel,
        out_shape=[pltpu.HBM(shape, jnp.float32)] * 2,
        in_specs=[pl.BlockSpec(memory_space=pltpu.VMEM)],
        out_specs=[pl.BlockSpec(memory_space=pl.ANY)] * 2,
        scratch_shapes=[
            pltpu.VMEM((4, HOURS, 2 * HALF), jnp.float32),
            pltpu.VMEM(shape, jnp.float32),
            pltpu.VMEM(shape, jnp.float32),
            pltpu.SemaphoreType.DMA((5,)),
        ],
        compiler_params=pltpu.CompilerParams(vmem_limit_bytes=9 * 2**20),
        cost_estimate=pl.CostEstimate(flops=0, bytes_accessed=4 * 2**20, transcendentals=0),
        name="finish",
    )(parts)


def hour_order(first, second):
    steps = jnp.arange(HOURS, dtype=jnp.int32)
    group, part, inner = steps // GROUP, steps // FINAL % SIDE, steps % FINAL
    return (first + group) % SIDE * GROUP + (second + part) % SIDE * FINAL + inner


def shards(coefficients, sky_year, hour_list, retention):
    me = lax.axis_index("patch")
    x, y, core = me // (2 * SIDE), me // 2 % SIDE, me % 2
    first, second = jnp.where(core == 0, x, y), jnp.where(core == 0, y, x)
    move = lambda value, pairs: lax.ppermute(value, "patch", pairs)
    first_up, first_down = ring(1, False), ring(-1, False)

    chip = jnp.arange(SIDE * SIDE, dtype=jnp.int32)
    one, two = chip // SIDE, chip % SIDE
    chips = jnp.where(
        core == 0,
        (x - one) % SIDE + SIDE * ((y - two) % SIDE),
        (y - two) % SIDE + SIDE * ((x - one) % SIDE),
    )

    spot = core.reshape(1)
    coefficients = pltpu.with_memory_space_constraint(coefficients, pltpu.HBM)
    sky_year = pltpu.with_memory_space_constraint(sky_year, pltpu.HBM)
    own_rates = lax.dynamic_slice(retention, (0, core * HALF), (4, HALF))
    hours, given = [
        pltpu.with_memory_space_constraint(arg, pltpu.HBM) for arg in (hour_list[None, :], retention)
    ]
    message, own_sky = prepare(spot, hours, given, coefficients, sky_year)
    others = [move(message, siblings), move(split(spot, coefficients), siblings)]
    half = PATCHES // 2
    extra = others[0][half:].reshape(2 * PIECE, HALF)
    sky = jnp.concatenate([own_sky[:, :HOURS], extra[:half, :HOURS]], axis=0).T
    digits_of = extra[half + 8 : half + 20].astype(jnp.float32)
    sibling_rates = digits_of[0:4] + (digits_of[4:8] + digits_of[8:12])
    rates = jnp.where(
        core == 0,
        jnp.concatenate([own_rates, sibling_rates]),
        jnp.concatenate([sibling_rates, own_rates]),
    )
    order = hour_order(first, second)[:, None]

    rendered = []
    for piece in range(PIECES):
        up, down, *kept = render(piece, spot, order, sky, rates, coefficients, others[piece])
        rendered.append((move(up, first_up), move(down, first_down), *kept))
    merged = []
    for up, down, keep_up, keep_down, mine in rendered:
        relay_up, relay_down = merge(keep_up, keep_down, up, down)
        merged.append((mine, up, down, move(relay_up, first_up), move(relay_down, first_down)))
    *sent, mine, coded_rates = join(0, rates, *merged[0])
    *relays, sent = lax.optimization_barrier((*merged[1][3:], sent))
    merged[1] = (*merged[1][:3], *relays)
    got = [move(part, ring(hop, True)) for hop, part in zip((1, 2, 3), sent)]
    above = upper(chips, coded_rates, *got, mine)
    *sent, mine = join(1, rates, *merged[1])
    got = [move(part, ring(hop, True)) for hop, part in zip((1, 2, 3), sent)]
    parts = glare(chips, *above, *got, mine)
    parts = lax.all_to_all(parts, "patch", 0, 0, tiled=True)
    return tuple(finish(parts))


def solution(mesh):
    placed = (P("view", "patch", None, None), P("patch", None), P(), P("patch", None))
    return jax.shard_map(
        shards,
        mesh=mesh,
        in_specs=placed,
        out_specs=(P("patch", "view", None, None), P("patch", "view", None, None)),
        check_vma=False,
    )
```
